32 devices in a mesh: runs: 2 (over y), gz: 4 (over x, core), gx: 4 (over z).
Axes of the slice: x: 2, y: 2, z: 4, core: 2. Of those that a mesh axis runs over, the one named last changes fastest.
Arguments:
- magnetic: float32 [3, 64, 64, 1024], P(None, 'gx', 'gz', 'runs'), parts along dimension 3, may hold values from -12 to 12
- friction: float32 [64], P('gz'), may hold values from 0.3 to 3
Outputs:
- relaxed: float32 [3, 64, 64, 1024], P(None, 'gx', 'gz', 'runs'), parts along dimension 3
- potential: float32 [3, 64, 64, 1024], P(None, 'gx', 'gz', 'runs'), parts along dimension 3
The draws below stay inside these ranges and needn't reach their ends.
There are 2 independent parts, one for each index of `runs`. The reference program is written for one: setup_inputs(seed, part) draws one part's arguments, and reference() takes and returns one part's arrays. A program takes and returns all parts, laid end to end along the dimension named above; an argument that names none is the same for every part. Nothing has to cross between parts.
All inputs are finite; a program needn't handle non-finite values.
Results may differ from the reference program's by a relative error of at most 0.00017.
Values sent between devices are 32-bit elements; how exact they have to be, the bound alone decides.
No kernel may reach another device: no remote copies, remote signals or barrier semaphores. Data moves between devices by JAX's collectives and lax.ppermute only.
A program may use at most 64 MiB of HBM per device.

```python
import math
import jax
import jax.numpy as jnp

NY = 512
DESCENTS = 2
RELAX = 2
NX = 64
NZ = 64


def draw_magnetic(key, part):
    x_frac = jnp.arange(NX, dtype=jnp.float32) / (NX - 1)
    z_frac = jnp.arange(NZ, dtype=jnp.float32) / (NZ - 1)
    amplitude = 1.7 * jnp.exp(jnp.log(3.0) * (0.5 * x_frac[:, None, None] - z_frac[None, :, None]))
    base = jax.random.truncated_normal(key, -4.0, 4.0, (3, NX, NZ, NY), jnp.float32)
    return (base * amplitude[None]).astype(jnp.float32)


def steps_of(key, extent, pieces, low, high):
    def one(position, shards_of):
        draws = jax.random.uniform(jax.random.fold_in(jax.random.fold_in(key, 6), position), (shards_of,), jnp.float32, low / len(pieces), high / len(pieces))
        return jnp.repeat(jnp.exp(draws), extent[position] // shards_of).reshape((-1,) + (1,) * (len(extent) - position - 1))

    level = one(*pieces[0])
    for cut in pieces[1:]:
        level = level * one(*cut)
    return level


def setup_inputs(seed: int = 0, part: int = 0) -> dict:
    arg_keys = jax.random.split(jax.random.key(seed), 3)
    own_keys = jax.random.split(jax.random.fold_in(arg_keys[2], part), 3)
    magnetic = draw_magnetic(jax.random.fold_in(jax.random.fold_in(arg_keys[2], part), 71), part)
    friction = jnp.clip(jnp.exp(math.log(3.0) - 2.3025851 * jax.random.uniform(arg_keys[1], (NZ,), jnp.float32) ** steps_of(arg_keys[1], (NZ,), ((0, 4),), -0.2, 0.2)), 0.3, 3.0)
    return dict(magnetic=magnetic, friction=friction)


step_scale = 0.5
time_step = 0.2


def diff_x(padded):
    return 0.5 * (padded[..., 2:, 1:-1, :] - padded[..., :-2, 1:-1, :])


def diff_z(padded):
    return 0.5 * (padded[..., 1:-1, 2:, :] - padded[..., 1:-1, :-2, :])


def diff_y(padded):
    middle = padded[..., 1:-1, 1:-1, :]
    return 0.5 * (jnp.roll(middle, -1, axis=-1) - jnp.roll(middle, 1, axis=-1))


def interior(padded):
    return padded[..., 1:-1, 1:-1, :]


def curl_of(padded):
    return jnp.stack([diff_y(padded[2]) - diff_z(padded[1]), diff_z(padded[0]) - diff_x(padded[2]), diff_x(padded[1]) - diff_y(padded[0])])


def divergence(padded):
    return diff_x(padded[0]) + diff_y(padded[1]) + diff_z(padded[2])


def gradient(scalar):
    return jnp.stack([diff_x(scalar), diff_y(scalar), diff_z(scalar)])


def cross_product(left, right):
    return jnp.stack([left[1] * right[2] - left[2] * right[1], left[2] * right[0] - left[0] * right[2], left[0] * right[1] - left[1] * right[0]])


def dot_product(left, right):
    return left[0] * right[0] + left[1] * right[1] + left[2] * right[2]


def pad_rim(values, width):
    return jnp.pad(values, ((0, 0), (width, width), (width, width), (0, 0)))


def omega_parts(widened):
    current = curl_of(widened)
    spread = divergence(widened)
    middle = interior(widened)
    square = jnp.maximum(dot_product(middle, middle), 1.0)
    lorentz = cross_product(current, middle)
    omega_field = (lorentz - spread[None] * middle) / square[None]
    return omega_field, current, spread, lorentz, square


def descent_force(omega_rim, field_rim, omega_core, current, spread, field_core):
    twisted = curl_of(cross_product(omega_rim, field_rim))
    twisted = twisted - cross_product(omega_core, current)
    twisted = twisted - gradient(dot_product(omega_rim, field_rim))
    twisted = twisted + omega_core * spread[None]
    return twisted + dot_product(omega_core, omega_core)[None] * field_core


def reference(magnetic, friction):
    field_now = magnetic
    cell_count = NX * NZ * NY
    for sweep_step in range(DESCENTS):
        widened = pad_rim(field_now, 2)
        omega_rim, current_rim, spread_rim, lorentz_rim, square_rim = omega_parts(widened)
        field_rim = interior(widened)
        omega_core = interior(omega_rim)
        current = interior(current_rim)
        spread = interior(spread_rim)
        lorentz = interior(lorentz_rim)
        square = interior(square_rim)
        descent = descent_force(omega_rim, field_rim, omega_core, current, spread, field_now)
        density = dot_product(lorentz, lorentz) / square + spread * spread
        step_rate = step_scale * (jnp.sum(density) / cell_count) / (jnp.sum(dot_product(descent, descent)) / cell_count + 1e-6)
        field_now = field_now + step_rate * descent
    relaxed = field_now
    columns = jnp.stack([-relaxed[1], relaxed[0]])
    suffix = jnp.flip(jnp.cumsum(jnp.flip(columns, 2), axis=2), 2)
    potential = jnp.concatenate([suffix, jnp.zeros_like(suffix[:1])], 0)
    for sweep_step in range(RELAX):
        induced = curl_of(pad_rim(potential, 1))
        current = curl_of(pad_rim(induced, 1))
        square = jnp.maximum(dot_product(induced, induced), 1.0)
        velocity = cross_product(current, induced) / (friction[None, :, None] * square)[None]
        potential = potential + time_step * cross_product(velocity, induced)
    return relaxed, potential
```

```python
import jax
import jax.numpy as jnp
from jax import lax
from jax.sharding import PartitionSpec as P

DESCENTS = 2
RELAX = 2


step_scale = 0.5
time_step = 0.2


def padded_2(cells, sides, width):
    for axis, dim in sides:
        count = lax.axis_size(axis)
        ends = count - 1
        head = lax.slice_in_dim(cells, 0, width, axis=dim)
        tail = lax.slice_in_dim(cells, cells.shape[dim] - width, cells.shape[dim], axis=dim)
        cells = jnp.concatenate(
            [
                lax.ppermute(tail, axis, [(i, (i + 1) % count) for i in range(ends)]),
                cells,
                lax.ppermute(head, axis, [((i + 1) % count, i) for i in range(ends)]),
            ],
            axis=dim,
        )
    return cells


def passed_along(value, axis, steps):
    count = lax.axis_size(axis)
    first, last = (max(0, -steps), min(count, count - steps))
    return lax.ppermute(value, axis, [(source, source + steps) for source in range(first, last)])


def summed_over(value, axis):
    count = lax.axis_size(axis)
    if count & (count - 1):
        return lax.psum(value, axis)
    stride = 1
    while stride < count:
        width = min(4, count // stride)
        others = [lax.ppermute(value, axis, [(i, i ^ (stride * step)) for i in range(count)]) for step in range(1, width)]
        value = value + others[0]
        if width == 4:
            value = value + (others[1] + others[2])
        stride *= width
    return value


def diff_x(padded):
    return 0.5 * (padded[..., 2:, 1:-1, :] - padded[..., :-2, 1:-1, :])


def diff_z(padded):
    return 0.5 * (padded[..., 1:-1, 2:, :] - padded[..., 1:-1, :-2, :])


def diff_y(padded):
    middle = padded[..., 1:-1, 1:-1, :]
    return 0.5 * (jnp.roll(middle, -1, axis=-1) - jnp.roll(middle, 1, axis=-1))


def interior(padded):
    return padded[..., 1:-1, 1:-1, :]


def curl_of(padded):
    return jnp.stack(
        [
            diff_y(padded[2]) - diff_z(padded[1]),
            diff_z(padded[0]) - diff_x(padded[2]),
            diff_x(padded[1]) - diff_y(padded[0]),
        ]
    )


def divergence(padded):
    return diff_x(padded[0]) + diff_y(padded[1]) + diff_z(padded[2])


def gradient(scalar):
    return jnp.stack([diff_x(scalar), diff_y(scalar), diff_z(scalar)])


def cross_product(left, right):
    return jnp.stack(
        [
            left[1] * right[2] - left[2] * right[1],
            left[2] * right[0] - left[0] * right[2],
            left[0] * right[1] - left[1] * right[0],
        ]
    )


def dot_product(left, right):
    return left[0] * right[0] + left[1] * right[1] + left[2] * right[2]


def omega_parts(widened):
    current = curl_of(widened)
    spread = divergence(widened)
    middle = interior(widened)
    square = jnp.maximum(dot_product(middle, middle), 1.0)
    lorentz = cross_product(current, middle)
    omega_field = (lorentz - spread[None] * middle) / square[None]
    return (omega_field, current, spread, lorentz, square)


def descent_force(omega_rim, field_rim, omega_core, current, spread, field_core):
    twisted = curl_of(cross_product(omega_rim, field_rim))
    twisted = twisted - cross_product(omega_core, current)
    twisted = twisted - gradient(dot_product(omega_rim, field_rim))
    twisted = twisted + omega_core * spread[None]
    return twisted + dot_product(omega_core, omega_core)[None] * field_core


def inside_rim(length, index, count):
    places = index * length + jnp.arange(length + 2, dtype=jnp.int32) - 1
    return ((places >= 0) & (places < length * count)).astype(jnp.float32)


def body(magnetic, friction):
    cx = magnetic.shape[1]
    cz = magnetic.shape[2]
    ny = magnetic.shape[3]
    cell_count = cx * cz * ny * lax.axis_size("gz") * lax.axis_size("gx")
    field_now = magnetic
    for sweep_step in range(DESCENTS):
        widened = padded_2(field_now, (("gz", 2), ("gx", 1)), 2)
        omega_rim, current_rim, spread_rim, lorentz_rim, square_rim = omega_parts(widened)
        field_rim = interior(widened)
        omega_core = interior(omega_rim)
        current = interior(current_rim)
        spread = interior(spread_rim)
        lorentz = interior(lorentz_rim)
        square = interior(square_rim)
        descent = descent_force(omega_rim, field_rim, omega_core, current, spread, field_now)
        density = dot_product(lorentz, lorentz) / square + spread * spread
        partial = jnp.stack([jnp.sum(density, axis=(0, 1)), jnp.sum(dot_product(descent, descent), axis=(0, 1))])
        partial = jnp.sum(partial.reshape(2, -1, 128), axis=1)
        partial = summed_over(summed_over(partial, "gx"), "gz")
        totals = jnp.sum(partial, axis=1)
        step_rate = step_scale * (totals[0] / cell_count) / (totals[1] / cell_count + 1e-06)
        field_now = field_now + step_rate * descent
    columns = jnp.stack([-field_now[1], field_now[0]])
    heights = jnp.arange(cz, dtype=jnp.int32)
    upper = (heights[None, :] >= heights[:, None]).astype(jnp.float32)
    suffix = jnp.einsum("axwy,zw->axzy", columns, upper, precision=lax.Precision.HIGHEST)
    slab_totals = suffix[:, :, 0, :]
    above = jnp.zeros_like(slab_totals)
    for passage in range(lax.axis_size("gz") - 1):
        above = passed_along(above + slab_totals, "gz", -1)
    suffix = suffix + above[:, :, None, :]
    potential = jnp.concatenate([suffix, jnp.zeros_like(suffix[:1])], 0)
    inside = (
        inside_rim(cx, lax.axis_index("gx"), lax.axis_size("gx"))[:, None, None]
        * inside_rim(cz, lax.axis_index("gz"), lax.axis_size("gz"))[None, :, None]
    )
    for sweep_step in range(RELAX):
        widened = padded_2(potential, (("gz", 2), ("gx", 1)), 2)
        induced_rim = curl_of(widened) * inside[None]
        current = curl_of(induced_rim)
        induced = interior(induced_rim)
        square = jnp.maximum(dot_product(induced, induced), 1.0)
        velocity = cross_product(current, induced) / (friction[None, :, None] * square)[None]
        potential = potential + time_step * cross_product(velocity, induced)
    return (field_now, potential)


def solution(mesh):
    return jax.shard_map(
        body,
        mesh=mesh,
        in_specs=(P(None, "gx", "gz", "runs"), P("gz")),
        out_specs=(P(None, "gx", "gz", "runs"), P(None, "gx", "gz", "runs")),
        check_vma=False,
    )
```

```python
import functools

import jax
import jax.numpy as jnp
from jax import lax
from jax.experimental import pallas as pl
from jax.experimental.pallas import tpu as pltpu
from jax.sharding import PartitionSpec as P

DESCENTS = 2
RELAX = 2

step_scale = 0.5
time_step = 0.2

LANES = 128
ROWS = 8
HALO = 4
BASE = 8


def pairings(count):
    first = [(i, i ^ 1) for i in range(count) if i ^ 1 < count]
    second = [(i, i + 1 if i % 2 else i - 1) for i in range(count)]
    return first, [pair for pair in second if 0 <= pair[1] < count]


def is_even(axis):
    return lax.axis_index(axis) % 2 == 0


def edges(cells, axis, dim):
    far = cells.shape[dim] - HALO
    even = is_even(axis)
    first = lax.dynamic_slice_in_dim(cells, jnp.where(even, far, 0), HALO, dim)
    second = lax.dynamic_slice_in_dim(cells, jnp.where(even, 0, far), HALO, dim)
    return first, second


def swapped(pair, axis):
    first, second = pairings(lax.axis_size(axis))
    return lax.ppermute(pair[0], axis, first), lax.ppermute(pair[1], axis, second)


def shared(tile_copies):
    return lax.all_to_all(tile_copies, ("gz", "gx"), 0, 0)


def y_diff(blocks, lane):
    count = len(blocks)
    after = [pltpu.roll(b, LANES - 1, 1) for b in blocks]
    before = [pltpu.roll(b, 1, 1) for b in blocks]
    return [
        jnp.where(lane == LANES - 1, after[(j + 1) % count], after[j])
        - jnp.where(lane == 0, before[(j - 1) % count], before[j])
        for j in range(count)
    ]


def cross(a, b):
    return (a[1] * b[2] - a[2] * b[1], a[2] * b[0] - a[0] * b[2], a[0] * b[1] - a[1] * b[0])


def dot(a, b):
    return a[0] * b[0] + a[1] * b[1] + a[2] * b[2]


def iotas():
    return (
        lax.broadcasted_iota(jnp.int32, (ROWS, LANES), 0),
        lax.broadcasted_iota(jnp.int32, (ROWS, LANES), 1),
    )


def windows(low, high):
    return [low + ROWS * w for w in range(-(-(high - low) // ROWS))]


def own_place(cx, cz):
    return (
        lax.axis_index("gx") * cx,
        lax.axis_size("gx") * cx,
        lax.axis_index("gz") * cz,
        lax.axis_size("gz") * cz,
    )


def descent_stages(bp, bx0, halo, cx, cz, blocks, omega_ref, lane):
    planes = cx + 2 * halo + 2

    def plane(x, _):
        at = x + (bx0 - halo - 1)
        for r in windows(BASE - halo - 1, BASE + cz + halo + 1):
            def ld(c, j, dx=0, dz=0):
                return bp[c, at + dx, j, r + dz : r + dz + ROWS, :]

            dy = [y_diff([ld(c, j) for j in range(blocks)], lane) for c in range(3)]
            for j in range(blocks):
                field = [ld(c, j) for c in range(3)]
                dx = [ld(c, j, dx=1) - ld(c, j, dx=-1) for c in range(3)]
                dz = [ld(c, j, dz=1) - ld(c, j, dz=-1) for c in range(3)]
                current = (dy[2][j] - dz[1], dz[0] - dx[2], dx[1] - dy[0][j])
                spread = dx[0] + dy[1][j] + dz[2]
                square = jnp.maximum(dot(field, field), 1.0)
                inverse = 0.5 / square
                lorentz = cross(current, field)
                omega = [(lorentz[c] - spread * field[c]) * inverse for c in range(3)]
                twist = cross(omega, field)
                along = dot(omega, field)
                for k, value in enumerate([*twist, along, *omega, *current, spread]):
                    omega_ref[k, x, j, r : r + ROWS, :] = value
        return 0

    lax.fori_loop(0, planes, plane, 0)


def doubled_force(bp, bx0, omega_ref, at, x, r, blocks, lane):
    def ld(k, j, dx=0, dz=0):
        return omega_ref[k, at + dx, j, r + dz : r + dz + ROWS, :]

    dy = {k: y_diff([ld(k, j) for j in range(blocks)], lane) for k in (0, 2, 3)}
    for j in range(blocks):
        field = [bp[c, x + bx0, j, r : r + ROWS, :] for c in range(3)]
        omega = [ld(4 + c, j) for c in range(3)]
        current = [ld(7 + c, j) for c in range(3)]
        spread = ld(10, j)

        def dx(k):
            return ld(k, j, dx=1) - ld(k, j, dx=-1)

        def dz(k):
            return ld(k, j, dz=1) - ld(k, j, dz=-1)

        curled = (dy[2][j] - dz(1) - dx(3), dz(0) - dx(2) - dy[3][j], dx(1) - dy[0][j] - dz(3))
        bent = cross(omega, current)
        size = dot(omega, omega)
        twice = size + size
        force = [curled[c] - bent[c] + omega[c] * spread + twice * field[c] for c in range(3)]
        yield j, force, field, size, spread


def density_of(field, size, spread):
    square = dot(field, field)
    return size * jnp.maximum(square, 1.0) + 0.25 * (spread * spread) * jnp.maximum(1.0 - square, 0.0)


def store_sums(sums_ref, functional, slope, rows):
    functional = jnp.sum(functional, axis=0, keepdims=True)
    slope = jnp.sum(slope, axis=0, keepdims=True)
    tile = jnp.where(rows == 0, functional, jnp.where(rows == 1, slope, 0.0))
    for k in range(sums_ref.shape[0]):
        sums_ref[k] = tile


def half_rate(sums_ref, cells):
    total = sums_ref[0]
    for k in range(1, sums_ref.shape[0]):
        total = total + sums_ref[k]
    functional = jnp.sum(total[0:1], axis=1, keepdims=True) / cells
    slope = jnp.sum(total[1:2], axis=1, keepdims=True) * 0.25 / cells
    return (0.5 * step_scale) * functional / (slope + 1e-6)


def first_kernel(
    core, face_xa, face_xb, face_za, face_zb, corner_a, corner_b, bp, fp, sums_ref, omega_ref
):
    _, cx, cz, ny = core.shape
    blocks = ny // LANES
    rows, lane = iotas()
    even_x, even_z = is_even("gx"), is_even("gz")
    x_first, x_all, z_first, z_all = own_place(cx, cz)
    top = BASE + cz

    def z_halos(plane, c, j, a, b):
        bp[c, plane, j, BASE - HALO : BASE, :] = jnp.where(even_z, b, a)
        bp[c, plane, j, top : top + HALO, :] = jnp.where(even_z, a, b)

    def own(x, _):
        for c in range(3):
            for j in range(blocks):
                cut = slice(j * LANES, (j + 1) * LANES)
                for z in range(0, cz, ROWS):
                    bp[c, x + HALO, j, BASE + z : BASE + z + ROWS, :] = core[c, x, z : z + ROWS, cut]
                z_halos(x + HALO, c, j, face_za[c, x, :, cut], face_zb[c, x, :, cut])
        return 0

    def rim(x, _):
        for c in range(3):
            for j in range(blocks):
                cut = slice(j * LANES, (j + 1) * LANES)
                for low, plane in ((True, x), (False, x + HALO + cx)):
                    use_a = even_x != low
                    for z in range(0, cz, ROWS):
                        bp[c, plane, j, BASE + z : BASE + z + ROWS, :] = jnp.where(
                            use_a, face_xa[c, x, z : z + ROWS, cut], face_xb[c, x, z : z + ROWS, cut]
                        )
                    corner = jnp.where(use_a, corner_a[c, x, :, cut], corner_b[c, x, :, cut])
                    z_halos(plane, c, j, corner[:HALO], corner[HALO:])
        return 0

    lax.fori_loop(0, cx, own, 0)
    lax.fori_loop(0, HALO, rim, 0)

    halo = HALO - 2
    descent_stages(bp, HALO, halo, cx, cz, blocks, omega_ref, lane)

    def plane(x, sums):
        functional, slope = sums
        own_x = (x >= halo) & (x < halo + cx)
        there = x_first + x - halo
        inside_x = (there >= 0) & (there < x_all)
        for r in windows(BASE - halo, BASE + cz + halo):
            height = rows + (r - BASE)
            owned = (height >= 0) & (height < cz) & own_x
            inside = (height + z_first >= 0) & (height + z_first < z_all) & inside_x
            for j, force, field, size, spread in doubled_force(bp, HALO - halo, omega_ref, x + 1, x, r, blocks, lane):
                functional = functional + jnp.where(owned, density_of(field, size, spread), 0.0)
                slope = slope + jnp.where(owned, dot(force, force), 0.0)
                for c in range(3):
                    fp[c, x, j, r : r + ROWS, :] = jnp.where(inside, force[c], 0.0)
        return functional, slope

    zero = jnp.zeros((ROWS, LANES), jnp.float32)
    functional, slope = lax.fori_loop(0, cx + 2 * halo, plane, (zero, zero))
    store_sums(sums_ref, functional, slope, rows)


def second_kernel(
    cells, bp0, fp0, sums0, friction, core_b, core_f, face_xa, face_xb, face_za, face_zb, totals, sums_ref, bp, omega_ref
):
    _, cx, cz, ny = core_b.shape
    blocks = ny // LANES
    rows, lane = iotas()
    even_x, even_z = is_even("gx"), is_even("gz")
    rate = half_rate(sums0, cells)
    halo = HALO - 2

    def step(x, _):
        for c in range(3):
            for j in range(blocks):
                for r in range(0, cz + 2 * BASE, ROWS):
                    bp[c, x, j, r : r + ROWS, :] = (
                        bp0[c, x + HALO - halo, j, r : r + ROWS, :] + rate * fp0[c, x, j, r : r + ROWS, :]
                    )
        return 0

    lax.fori_loop(0, cx + 2 * halo, step, 0)
    descent_stages(bp, halo, 0, cx, cz, blocks, omega_ref, lane)

    def plane(x, sums):
        functional, slope = sums
        for z in range(0, cz, ROWS):
            r = BASE + z
            for j, force, field, size, spread in doubled_force(bp, halo, omega_ref, x + 1, x, r, blocks, lane):
                cut = slice(j * LANES, (j + 1) * LANES)
                functional = functional + density_of(field, size, spread)
                slope = slope + dot(force, force)
                for c in range(3):
                    core_b[c, x, z : z + ROWS, cut] = field[c]
                    core_f[c, x, z : z + ROWS, cut] = force[c]
        for j in range(blocks):
            cut = slice(j * LANES, (j + 1) * LANES)
            for k, (source, c) in enumerate(((core_f, 0), (core_f, 1), (core_b, 0), (core_b, 1))):
                low, high = source[c, x, 0:HALO, cut], source[c, x, cz - HALO : cz, cut]
                face_za[k * cx + x, :, cut] = jnp.where(even_z, high, low)
                face_zb[k * cx + x, :, cut] = jnp.where(even_z, low, high)
                column = source[c, x, 0:ROWS, cut]
                for z in range(ROWS, cz, ROWS):
                    column = column + source[c, x, z : z + ROWS, cut]
                totals[k * cx + x, :, cut] = jnp.sum(column, axis=0, keepdims=True)
        return functional, slope

    zero = jnp.zeros((ROWS, LANES), jnp.float32)
    functional, slope = lax.fori_loop(0, cx, plane, (zero, zero))
    store_sums(sums_ref, functional, slope, rows)

    def faces(x, _):
        for j in range(blocks):
            cut = slice(j * LANES, (j + 1) * LANES)
            for k, (source, c) in enumerate(((core_f, 0), (core_f, 1), (core_b, 0), (core_b, 1))):
                for z in range(0, cz, ROWS):
                    low = source[c, x, z : z + ROWS, cut]
                    high = source[c, x + cx - HALO, z : z + ROWS, cut]
                    face_xa[k, x, z : z + ROWS, cut] = jnp.where(even_x, high, low)
                    face_xb[k, x, z : z + ROWS, cut] = jnp.where(even_x, low, high)
        return 0

    lax.fori_loop(0, HALO, faces, 0)
    for j in range(blocks):
        cut = slice(j * LANES, (j + 1) * LANES)
        low, high = friction[0:HALO], friction[cz - HALO : cz]
        face_za[4 * cx, :, cut] = jnp.where(even_z, high, low)
        face_zb[4 * cx, :, cut] = jnp.where(even_z, low, high)


def third_kernel(
    cells,
    core_b,
    core_f,
    sums0,
    friction,
    face_xa,
    face_xb,
    face_za,
    face_zb,
    above,
    corner_a,
    corner_b,
    relaxed,
    potential,
    ap,
    bm,
    an,
    rub,
):
    _, cx, cz, ny = core_b.shape
    blocks = ny // LANES
    rows, lane = iotas()
    even_x, even_z = is_even("gx"), is_even("gz")
    x_first, x_all, z_first, z_all = own_place(cx, cz)
    rate = half_rate(sums0, cells)
    top = BASE + cz

    rub[BASE:top] = friction[...]
    rub[BASE - HALO : BASE] = jnp.where(even_z, face_zb[4 * cx, :, :LANES], face_za[4 * cx, :, :LANES])
    rub[top : top + HALO] = jnp.where(even_z, face_za[4 * cx, :, :LANES], face_zb[4 * cx, :, :LANES])
    for r in range(0, cz + 2 * BASE, ROWS):
        height = rows + (r - BASE) + z_first
        inside = (height >= 0) & (height < z_all)
        rub[r : r + ROWS] = jnp.where(inside, time_step / rub[r : r + ROWS], 0.0)

    def suffix(value):
        for reach in (1, 2, 4):
            value = value + jnp.where(rows < ROWS - reach, pltpu.roll(value, ROWS - reach, 0), 0.0)
        return value

    def prefix(value):
        for reach in (1, 2, 4):
            value = value + jnp.where(rows >= reach, pltpu.roll(value, reach, 0), 0.0)
        return value

    def column(c, plane, j, low, own, high, beyond):
        sign = 1.0 if c == 0 else -1.0
        out = 1 - c
        ap[out, plane, j, top : top + HALO, :] = high
        value = ap[out, plane, j, top : top + ROWS, :]
        ap[out, plane, j, top : top + ROWS, :] = sign * (beyond - (prefix(value) - value))
        carry = beyond
        for z in reversed(range(0, cz, ROWS)):
            value = suffix(own[z // ROWS]) + carry
            ap[out, plane, j, BASE + z : BASE + z + ROWS, :] = sign * value
            carry = value[0:1]
        ap[out, plane, j, BASE - HALO : BASE, :] = low
        value = suffix(ap[out, plane, j, 0:BASE, :]) + carry
        ap[out, plane, j, 0:BASE, :] = jnp.where(z_first > 0, sign * value, 0.0)

    def own_plane(x, _):
        for j in range(blocks):
            cut = slice(j * LANES, (j + 1) * LANES)
            for c in range(3):
                own = [
                    core_b[c, x, z : z + ROWS, cut] + rate * core_f[c, x, z : z + ROWS, cut]
                    for z in range(0, cz, ROWS)
                ]
                for z in range(0, cz, ROWS):
                    relaxed[c, x, z : z + ROWS, cut] = own[z // ROWS]
                if c == 2:
                    continue
                a, b = [
                    face[(2 + c) * cx + x, :, cut] + rate * face[c * cx + x, :, cut] for face in (face_za, face_zb)
                ]
                beyond = above[(2 + c) * cx + x, :, cut] + rate * above[c * cx + x, :, cut]
                column(c, x + HALO, j, jnp.where(even_z, b, a), own, jnp.where(even_z, a, b), beyond)
        return 0

    lax.fori_loop(0, cx, own_plane, 0)

    def rim_plane(x, _):
        for j in range(blocks):
            cut = slice(j * LANES, (j + 1) * LANES)
            for low, plane in ((True, x), (False, x + HALO + cx)):
                use_a = even_x != low

                def picked(k, span):
                    return jnp.where(use_a, face_xa[k, x, span, cut], face_xb[k, x, span, cut])

                for c in range(2):
                    own = [
                        picked(2 + c, slice(z, z + ROWS)) + rate * picked(c, slice(z, z + ROWS))
                        for z in range(0, cz, ROWS)
                    ]
                    corner = [jnp.where(use_a, corner_a[k, x, :, cut], corner_b[k, x, :, cut]) for k in (2 + c, c)]
                    corner = corner[0] + rate * corner[1]
                    column(c, plane, j, corner[4:8], own, jnp.concatenate([corner[1:4], corner[3:4]], 0), corner[0:1])
        return 0

    lax.fori_loop(0, HALO, rim_plane, 0)

    def induced(a_ref, ax0, halo, flat):
        def plane(x, _):
            at = x + (ax0 - halo - 1)
            there = x_first + x - halo - 1
            inside_x = (there >= 0) & (there < x_all)
            for r in windows(BASE - halo - 1, top + halo + 1):
                height = rows + (r - BASE) + z_first
                inside = (height >= 0) & (height < z_all) & inside_x

                def ld(c, j, dx=0, dz=0):
                    return a_ref[c, at + dx, j, r + dz : r + dz + ROWS, :]

                dy = {c: y_diff([ld(c, j) for j in range(blocks)], lane) for c in ((0,) if flat else (0, 2))}
                for j in range(blocks):
                    curl_x = ld(1, j, dz=-1) - ld(1, j, dz=1)
                    curl_y = ld(0, j, dz=1) - ld(0, j, dz=-1)
                    curl_z = ld(1, j, dx=1) - ld(1, j, dx=-1) - dy[0][j]
                    if not flat:
                        curl_x = curl_x + dy[2][j]
                        curl_y = curl_y - (ld(2, j, dx=1) - ld(2, j, dx=-1))
                    for c, value in enumerate((curl_x, curl_y, curl_z)):
                        bm[c, x, j, r : r + ROWS, :] = jnp.where(inside, value, 0.0)
            return 0

        lax.fori_loop(0, cx + 2 * halo + 2, plane, 0)

    def pushed(x, r):
        def ld(c, j, dx=0, dz=0):
            return bm[c, x + dx, j, r + dz : r + dz + ROWS, :]

        dy = [y_diff([ld(c, j) for j in range(blocks)], lane) if c != 1 else None for c in range(3)]
        weight = rub[r : r + ROWS]
        for j in range(blocks):
            field = [ld(c, j) for c in range(3)]
            current = (
                dy[2][j] - (ld(1, j, dz=1) - ld(1, j, dz=-1)),
                (ld(0, j, dz=1) - ld(0, j, dz=-1)) - (ld(2, j, dx=1) - ld(2, j, dx=-1)),
                (ld(1, j, dx=1) - ld(1, j, dx=-1)) - dy[0][j],
            )
            square = dot(field, field)
            scale = weight * (0.0625 / jnp.maximum(0.25 * square, 1.0))
            both = dot(current, field)
            yield j, [scale * (field[c] * both - current[c] * square) for c in range(3)]

    halo = HALO - 2
    induced(ap, HALO, halo, True)

    def first_step(x, _):
        for r in windows(BASE - halo, top + halo):
            for j, change in pushed(x + 1, r):
                for c in range(2):
                    an[c, x, j, r : r + ROWS, :] = ap[c, x + HALO - halo, j, r : r + ROWS, :] + change[c]
                an[2, x, j, r : r + ROWS, :] = change[2]
        return 0

    lax.fori_loop(0, cx + 2 * halo, first_step, 0)
    induced(an, halo, 0, False)

    def last_step(x, _):
        for z in range(0, cz, ROWS):
            for j, change in pushed(x + 1, BASE + z):
                cut = slice(j * LANES, (j + 1) * LANES)
                for c in range(3):
                    potential[c, x, z : z + ROWS, cut] = (
                        an[c, x + halo, j, BASE + z : BASE + z + ROWS, :] + change[c]
                    )
        return 0

    lax.fori_loop(0, cx, last_step, 0)


def pack_kernel(*refs):
    *parts, face_za, face_zb, above, corner_a, corner_b = refs
    cx = above.shape[0] // 4
    even_x, even_z = is_even("gx"), is_even("gz")
    total = parts[0][...]
    for part in parts[1:]:
        total = total + part[...]
    above[...] = total

    def plane(x, _):
        for k in range(4):
            packed = []
            for at in (x, x + cx - HALO):
                a, b = face_za[k * cx + at], face_zb[k * cx + at]
                low, high = jnp.where(even_z, b, a), jnp.where(even_z, a, b)
                packed.append(jnp.concatenate([above[k * cx + at], high[0 : HALO - 1], low], axis=0))
            corner_a[k, x] = jnp.where(even_x, packed[1], packed[0])
            corner_b[k, x] = jnp.where(even_x, packed[0], packed[1])
        return 0

    lax.fori_loop(0, HALO, plane, 0)


def call(kernel, outs, *args, scratch=(), cost=0):
    shapes = [jax.ShapeDtypeStruct(shape, jnp.float32) for shape in outs]
    return pl.pallas_call(
        kernel,
        out_shape=shapes,
        in_specs=[pl.BlockSpec(memory_space=pltpu.VMEM)] * len(args),
        out_specs=[pl.BlockSpec(memory_space=pltpu.VMEM)] * len(outs),
        scratch_shapes=[pltpu.VMEM(shape, jnp.float32) for shape in scratch],
        compiler_params=pltpu.CompilerParams(vmem_limit_bytes=56 * 1024 * 1024),
        cost_estimate=pl.CostEstimate(flops=cost, bytes_accessed=cost // 10, transcendentals=0),
    )(*args)


def body(magnetic, friction):
    _, cx, cz, ny = magnetic.shape
    blocks = ny // LANES
    height = cz + 2 * BASE
    count_z, count_x = lax.axis_size("gz"), lax.axis_size("gx")
    devices = count_z * count_x
    cells = cx * cz * ny * devices
    work = cx * cz * ny * 200

    def padded(components, layers):
        return (components, cx + 2 * layers, blocks, height, LANES)

    tiles = (devices, ROWS, LANES)
    core = (3, cx, cz, ny)
    rubbed = jnp.broadcast_to(friction[:, None], (cz, LANES))

    faces_x = swapped(edges(magnetic, "gx", 1), "gx")
    faces_z = swapped(edges(magnetic, "gz", 2), "gz")
    corners = swapped(edges(jnp.concatenate(faces_z, axis=2), "gx", 1), "gx")
    bp, fp, sums = call(
        first_kernel,
        [padded(3, HALO), padded(3, HALO - 2), tiles],
        magnetic,
        *faces_x,
        *faces_z,
        *corners,
        scratch=[padded(11, HALO - 1)],
        cost=2 * work,
    )
    core_b, core_f, *faces, totals, sums = call(
        functools.partial(second_kernel, cells),
        [core, core, (4, HALO, cz, ny), (4, HALO, cz, ny), (4 * cx + 1, HALO, ny), (4 * cx + 1, HALO, ny), (4 * cx, 1, ny), tiles],
        bp,
        fp,
        shared(sums),
        rubbed,
        scratch=[padded(3, HALO - 2), padded(11, 1)],
        cost=work,
    )
    below = [
        lax.ppermute(totals, "gz", [(i, i - steps) for i in range(steps, count_z)]) for steps in range(1, count_z)
    ]
    faces_z = swapped(faces[2:], "gz")
    faces_x = swapped(faces[:2], "gx")
    sums = shared(sums)
    above, *corners = call(
        pack_kernel,
        [(4 * cx, 1, ny), (4, HALO, 2 * HALO, ny), (4, HALO, 2 * HALO, ny)],
        *below,
        *faces_z,
        cost=work // 50,
    )
    corners = swapped(corners, "gx")
    return tuple(
        call(
            functools.partial(third_kernel, cells),
            [core, core],
            core_b,
            core_f,
            sums,
            rubbed,
            *faces_x,
            *faces_z,
            above,
            *corners,
            scratch=[padded(2, HALO), padded(3, HALO - 1), padded(3, HALO - 2), (height, LANES)],
            cost=work,
        )
    )


def solution(mesh):
    return jax.shard_map(
        body,
        mesh=mesh,
        in_specs=(P(None, "gx", "gz", "runs"), P("gz")),
        out_specs=(P(None, "gx", "gz", "runs"), P(None, "gx", "gz", "runs")),
        check_vma=False,
    )
```

```python
import functools

import jax
import jax.numpy as jnp
from jax import lax
from jax.experimental import pallas as pl
from jax.experimental.pallas import tpu as pltpu
from jax.sharding import PartitionSpec as P

DESCENTS = 2
RELAX = 2

step_scale = 0.5
time_step = 0.2

LANES = 128
ROWS = 8
HALO = 4
BASE = 8


AXES = ("runs", "gz", "gx")


def pairings(axis):
    sizes = [lax.axis_size(name) for name in AXES]
    along = AXES.index(axis)
    places = [(r, z, x) for r in range(sizes[0]) for z in range(sizes[1]) for x in range(sizes[2])]

    def flat(place):
        return (place[0] * sizes[1] + place[1]) * sizes[2] + place[2]

    def moved(place, name, to):
        return tuple(to if name == other else at for other, at in zip(AXES, place))

    first, second = [], []
    for place in places:
        at = place[along]
        if at ^ 1 < sizes[along]:
            first.append((flat(place), flat(moved(place, axis, at ^ 1))))
        to = at + 1 if at % 2 else at - 1
        if 0 <= to < sizes[along]:
            second.append((flat(place), flat(moved(place, axis, to))))
        elif sizes[0] % 2 == 0:
            second.append((flat(place), flat(moved(place, "runs", place[0] ^ 1))))
    return first, second


def is_even(axis):
    return lax.axis_index(axis) % 2 == 0


def edges(cells, axis, dim):
    far = cells.shape[dim] - HALO
    even = is_even(axis)
    first = lax.dynamic_slice_in_dim(cells, jnp.where(even, far, 0), HALO, dim)
    second = lax.dynamic_slice_in_dim(cells, jnp.where(even, 0, far), HALO, dim)
    return first, second


def swapped(pair, axis):
    first, second = pairings(axis)
    return lax.ppermute(pair[0], AXES, first), lax.ppermute(pair[1], AXES, second)


def sorted_out(axis, first, second):
    at = lax.axis_index(axis)
    even = at % 2 == 0
    low = jnp.where(at > 0, jnp.where(even, second, first), 0.0)
    high = jnp.where(at < lax.axis_size(axis) - 1, jnp.where(even, first, second), 0.0)
    return low, high


def shared(tile_copies):
    return lax.all_to_all(tile_copies, ("gz", "gx"), 0, 0)


def y_diff(blocks):
    wide = [pltpu.roll(blocks[-1], 1, 1), *blocks, pltpu.roll(blocks[0], LANES - 1, 1)]
    return [wide[j + 2] - wide[j] for j in range(len(blocks))]


def dealing(ny, back):
    blocks = ny // LANES
    source = lax.broadcasted_iota(jnp.int32, (ny, ny), 0)
    target = lax.broadcasted_iota(jnp.int32, (ny, ny), 1)
    if back:
        source, target = target, source
    return ((target % LANES) * blocks + target // LANES == source).astype(jnp.bfloat16)


def dealt(value, matrix):
    rows = value.shape[0]
    high = value.astype(jnp.bfloat16)
    rest = (value - high.astype(jnp.float32)).astype(jnp.bfloat16)
    both = jnp.dot(jnp.concatenate([high, rest], axis=0), matrix, preferred_element_type=jnp.float32)
    return both[:rows] + both[rows:]


def cross(a, b):
    return (a[1] * b[2] - a[2] * b[1], a[2] * b[0] - a[0] * b[2], a[0] * b[1] - a[1] * b[0])


def dot(a, b):
    return a[0] * b[0] + a[1] * b[1] + a[2] * b[2]


def row_index():
    return lax.broadcasted_iota(jnp.int32, (ROWS, LANES), 0)


def windows(low, high):
    return [low + ROWS * w for w in range(-(-(high - low) // ROWS))]


def own_place(cx, cz):
    return (
        lax.axis_index("gx") * cx,
        lax.axis_size("gx") * cx,
        lax.axis_index("gz") * cz,
        lax.axis_size("gz") * cz,
    )


def descent_stages(bp, bx0, halo, cx, cz, blocks, omega_ref):
    planes = cx + 2 * halo + 2

    def plane(x, _):
        at = x + (bx0 - halo - 1)
        for r in windows(BASE - halo - 1, BASE + cz + halo + 1):
            def ld(c, j, dx=0, dz=0):
                return bp[c, at + dx, j, r + dz : r + dz + ROWS, :]

            dy = [y_diff([ld(c, j) for j in range(blocks)]) for c in range(3)]
            for j in range(blocks):
                field = [ld(c, j) for c in range(3)]
                dx = [ld(c, j, dx=1) - ld(c, j, dx=-1) for c in range(3)]
                dz = [ld(c, j, dz=1) - ld(c, j, dz=-1) for c in range(3)]
                current = (dy[2][j] - dz[1], dz[0] - dx[2], dx[1] - dy[0][j])
                spread = dx[0] + dy[1][j] + dz[2]
                square = jnp.maximum(dot(field, field), 1.0)
                inverse = 0.5 / square
                lorentz = cross(current, field)
                omega = [(lorentz[c] - spread * field[c]) * inverse for c in range(3)]
                twist = cross(omega, field)
                along = dot(omega, field)
                for k, value in enumerate([*twist, along, *omega, *current, spread]):
                    omega_ref[k, x, j, r : r + ROWS, :] = value
        return 0

    lax.fori_loop(0, planes, plane, 0)


def doubled_force(bp, bx0, omega_ref, at, x, r, blocks):
    def ld(k, j, dx=0, dz=0):
        return omega_ref[k, at + dx, j, r + dz : r + dz + ROWS, :]

    dy = {k: y_diff([ld(k, j) for j in range(blocks)]) for k in (0, 2, 3)}
    for j in range(blocks):
        field = [bp[c, x + bx0, j, r : r + ROWS, :] for c in range(3)]
        omega = [ld(4 + c, j) for c in range(3)]
        current = [ld(7 + c, j) for c in range(3)]
        spread = ld(10, j)

        def dx(k):
            return ld(k, j, dx=1) - ld(k, j, dx=-1)

        def dz(k):
            return ld(k, j, dz=1) - ld(k, j, dz=-1)

        curled = (dy[2][j] - dz(1) - dx(3), dz(0) - dx(2) - dy[3][j], dx(1) - dy[0][j] - dz(3))
        bent = cross(omega, current)
        size = dot(omega, omega)
        twice = size + size
        force = [curled[c] - bent[c] + omega[c] * spread + twice * field[c] for c in range(3)]
        yield j, force, field, size, spread


def density_of(field, size, spread):
    square = dot(field, field)
    return size * jnp.maximum(square, 1.0) + 0.25 * (spread * spread) * jnp.maximum(1.0 - square, 0.0)


def store_sums(sums_ref, functional, slope, rows):
    functional = jnp.sum(functional, axis=0, keepdims=True)
    slope = jnp.sum(slope, axis=0, keepdims=True)
    tile = jnp.where(rows == 0, functional, jnp.where(rows == 1, slope, 0.0))
    for k in range(sums_ref.shape[0]):
        sums_ref[k] = tile


def half_rate(sums_ref, cells):
    total = sums_ref[0]
    for k in range(1, sums_ref.shape[0]):
        total = total + sums_ref[k]
    functional = jnp.sum(total[0:1], axis=1, keepdims=True) / cells
    slope = jnp.sum(total[1:2], axis=1, keepdims=True) * 0.25 / cells
    return (0.5 * step_scale) * functional / (slope + 1e-6)


def entry_kernel(magnetic, core, face_xa, face_xb, face_za, face_zb, held, arrived):
    _, cx, cz, ny = magnetic.shape
    even_x, even_z = is_even("gx"), is_even("gz")
    copies = [pltpu.make_async_copy(magnetic.at[c], held.at[c], arrived.at[c]) for c in range(3)]
    for copy in copies:
        copy.start()
    matrix = dealing(ny, False)
    for c in range(3):
        copies[c].wait()
        value = dealt(held[c].reshape(cx * cz, ny), matrix).reshape(cx, cz, ny)
        core[c] = value
        low, high = value[:HALO], value[cx - HALO :]
        face_xa[c] = jnp.where(even_x, high, low)
        face_xb[c] = jnp.where(even_x, low, high)
        low, high = value[:, :HALO], value[:, cz - HALO :]
        face_za[c] = jnp.where(even_z, high, low)
        face_zb[c] = jnp.where(even_z, low, high)


def first_kernel(
    core, face_xa, face_xb, face_za, face_zb, corner_a, corner_b, bp, fp, sums_ref, omega_ref
):
    _, cx, cz, ny = core.shape
    blocks = ny // LANES
    rows = row_index()
    x_first, x_all, z_first, z_all = own_place(cx, cz)
    top = BASE + cz

    def z_halos(plane, c, j, a, b):
        low, high = sorted_out("gz", a, b)
        bp[c, plane, j, BASE - HALO : BASE, :] = low
        bp[c, plane, j, top : top + HALO, :] = high

    def own(x, _):
        for c in range(3):
            for j in range(blocks):
                cut = slice(j * LANES, (j + 1) * LANES)
                for z in range(0, cz, ROWS):
                    bp[c, x + HALO, j, BASE + z : BASE + z + ROWS, :] = core[c, x, z : z + ROWS, cut]
                z_halos(x + HALO, c, j, face_za[c, x, :, cut], face_zb[c, x, :, cut])
        return 0

    def rim(x, _):
        for c in range(3):
            for j in range(blocks):
                cut = slice(j * LANES, (j + 1) * LANES)
                planes = (x, x + HALO + cx)
                for z in range(0, cz, ROWS):
                    span = slice(z, z + ROWS)
                    both = sorted_out("gx", face_xa[c, x, span, cut], face_xb[c, x, span, cut])
                    for plane, value in zip(planes, both):
                        bp[c, plane, j, BASE + z : BASE + z + ROWS, :] = value
                both = sorted_out("gx", corner_a[c, x, :, cut], corner_b[c, x, :, cut])
                for plane, value in zip(planes, both):
                    z_halos(plane, c, j, value[:HALO], value[HALO:])
        return 0

    lax.fori_loop(0, cx, own, 0)
    lax.fori_loop(0, HALO, rim, 0)

    halo = HALO - 2
    descent_stages(bp, HALO, halo, cx, cz, blocks, omega_ref)

    def plane(x, sums):
        functional, slope = sums
        own_x = (x >= halo) & (x < halo + cx)
        there = x_first + x - halo
        inside_x = (there >= 0) & (there < x_all)
        for r in windows(BASE - halo, BASE + cz + halo):
            height = rows + (r - BASE)
            owned = (height >= 0) & (height < cz) & own_x
            inside = (height + z_first >= 0) & (height + z_first < z_all) & inside_x
            for j, force, field, size, spread in doubled_force(bp, HALO - halo, omega_ref, x + 1, x, r, blocks):
                functional = functional + jnp.where(owned, density_of(field, size, spread), 0.0)
                slope = slope + jnp.where(owned, dot(force, force), 0.0)
                for c in range(3):
                    fp[c, x, j, r : r + ROWS, :] = jnp.where(inside, force[c], 0.0)
        return functional, slope

    zero = jnp.zeros((ROWS, LANES), jnp.float32)
    functional, slope = lax.fori_loop(0, cx + 2 * halo, plane, (zero, zero), unroll=4)
    store_sums(sums_ref, functional, slope, rows)


def second_kernel(
    cells, bp0, fp0, sums0, friction, core_b, core_f, face_xa, face_xb, face_za, face_zb, sums_ref, bp, omega_ref
):
    _, cx, cz, ny = core_b.shape
    blocks = ny // LANES
    rows = row_index()
    even_x, even_z = is_even("gx"), is_even("gz")
    rate = half_rate(sums0, cells)
    halo = HALO - 2

    def step(x, _):
        for c in range(3):
            for j in range(blocks):
                for r in range(0, cz + 2 * BASE, ROWS):
                    bp[c, x, j, r : r + ROWS, :] = (
                        bp0[c, x + HALO - halo, j, r : r + ROWS, :] + rate * fp0[c, x, j, r : r + ROWS, :]
                    )
        return 0

    lax.fori_loop(0, cx + 2 * halo, step, 0, unroll=2)
    descent_stages(bp, halo, 0, cx, cz, blocks, omega_ref)

    def plane(x, sums):
        functional, slope = sums
        for z in range(0, cz, ROWS):
            r = BASE + z
            for j, force, field, size, spread in doubled_force(bp, halo, omega_ref, x + 1, x, r, blocks):
                cut = slice(j * LANES, (j + 1) * LANES)
                functional = functional + density_of(field, size, spread)
                slope = slope + dot(force, force)
                for c in range(3):
                    core_b[c, x, z : z + ROWS, cut] = field[c]
                    core_f[c, x, z : z + ROWS, cut] = force[c]
        for j in range(blocks):
            cut = slice(j * LANES, (j + 1) * LANES)
            for k, (source, c) in enumerate(((core_f, 0), (core_f, 1), (core_b, 0), (core_b, 1))):
                low, high = source[c, x, 0:HALO, cut], source[c, x, cz - HALO : cz, cut]
                face_za[k * cx + x, :, cut] = jnp.where(even_z, high, low)
                face_zb[k * cx + x, :, cut] = jnp.where(even_z, low, high)
                column = source[c, x, 0:ROWS, cut]
                for z in range(ROWS, cz, ROWS):
                    column = column + source[c, x, z : z + ROWS, cut]
                face_za[4 * cx + 1 + x, k : k + 1, cut] = jnp.sum(column, axis=0, keepdims=True)
        return functional, slope

    zero = jnp.zeros((ROWS, LANES), jnp.float32)
    functional, slope = lax.fori_loop(0, cx, plane, (zero, zero), unroll=4)
    store_sums(sums_ref, functional, slope, rows)

    def faces(x, _):
        for j in range(blocks):
            cut = slice(j * LANES, (j + 1) * LANES)
            for k, (source, c) in enumerate(((core_f, 0), (core_f, 1), (core_b, 0), (core_b, 1))):
                for z in range(0, cz, ROWS):
                    low = source[c, x, z : z + ROWS, cut]
                    high = source[c, x + cx - HALO, z : z + ROWS, cut]
                    face_xa[k, x, z : z + ROWS, cut] = jnp.where(even_x, high, low)
                    face_xb[k, x, z : z + ROWS, cut] = jnp.where(even_x, low, high)
        return 0

    lax.fori_loop(0, HALO, faces, 0)
    for j in range(blocks):
        cut = slice(j * LANES, (j + 1) * LANES)
        low, high = friction[0:HALO], friction[cz - HALO : cz]
        face_za[4 * cx, :, cut] = jnp.where(even_z, high, low)
        face_zb[4 * cx, :, cut] = jnp.where(even_z, low, high)


def third_kernel(
    cells,
    core_b,
    core_f,
    sums0,
    friction,
    face_xa,
    face_xb,
    face_za,
    face_zb,
    above,
    corner_a,
    corner_b,
    relaxed,
    potential,
    ap,
    bm,
    an,
    rub,
):
    _, cx, cz, ny = core_b.shape
    blocks = ny // LANES
    rows = row_index()
    x_first, x_all, z_first, z_all = own_place(cx, cz)
    rate = half_rate(sums0, cells)
    top = BASE + cz

    rub[BASE:top] = friction[...]
    low, high = sorted_out("gz", face_za[4 * cx, :, :LANES], face_zb[4 * cx, :, :LANES])
    rub[BASE - HALO : BASE] = low
    rub[top : top + HALO] = high
    for r in range(0, cz + 2 * BASE, ROWS):
        height = rows + (r - BASE) + z_first
        inside = (height >= 0) & (height < z_all)
        rub[r : r + ROWS] = jnp.where(inside, time_step / rub[r : r + ROWS], 0.0)

    def suffix(value):
        for reach in (1, 2, 4):
            value = value + jnp.where(rows < ROWS - reach, pltpu.roll(value, ROWS - reach, 0), 0.0)
        return value

    def prefix(value):
        for reach in (1, 2, 4):
            value = value + jnp.where(rows >= reach, pltpu.roll(value, reach, 0), 0.0)
        return value

    def column(c, plane, j, low, own, high, beyond):
        sign = 1.0 if c == 0 else -1.0
        out = 1 - c
        ap[out, plane, j, top : top + HALO, :] = high
        value = ap[out, plane, j, top : top + ROWS, :]
        ap[out, plane, j, top : top + ROWS, :] = sign * (beyond - (prefix(value) - value))
        carry = beyond
        for z in reversed(range(0, cz, ROWS)):
            value = suffix(own[z // ROWS]) + carry
            ap[out, plane, j, BASE + z : BASE + z + ROWS, :] = sign * value
            carry = value[0:1]
        ap[out, plane, j, BASE - HALO : BASE, :] = low
        value = suffix(ap[out, plane, j, 0:BASE, :]) + carry
        ap[out, plane, j, 0:BASE, :] = jnp.where(z_first > 0, sign * value, 0.0)

    def own_plane(x, _):
        for j in range(blocks):
            cut = slice(j * LANES, (j + 1) * LANES)
            for c in range(3):
                own = [
                    core_b[c, x, z : z + ROWS, cut] + rate * core_f[c, x, z : z + ROWS, cut]
                    for z in range(0, cz, ROWS)
                ]
                for z in range(0, cz, ROWS):
                    relaxed[c, x, z : z + ROWS, cut] = own[z // ROWS]
                if c == 2:
                    continue
                a, b = [
                    face[(2 + c) * cx + x, :, cut] + rate * face[c * cx + x, :, cut] for face in (face_za, face_zb)
                ]
                low, high = sorted_out("gz", a, b)
                column(c, x + HALO, j, low, own, high, above[x, c : c + 1, cut])
        return 0

    lax.fori_loop(0, cx, own_plane, 0, unroll=2)

    def rim_plane(x, _):
        for j in range(blocks):
            cut = slice(j * LANES, (j + 1) * LANES)
            for c in range(2):
                own = []
                for z in range(0, cz, ROWS):
                    span = slice(z, z + ROWS)
                    a, b = [face[2 + c, x, span, cut] + rate * face[c, x, span, cut] for face in (face_xa, face_xb)]
                    own.append(sorted_out("gx", a, b))
                corners = sorted_out("gx", corner_a[c, x, :, cut], corner_b[c, x, :, cut])
                for side, plane in enumerate((x, x + HALO + cx)):
                    corner = corners[side]
                    high = jnp.concatenate([corner[1:4], corner[3:4]], 0)
                    column(c, plane, j, corner[4:8], [pair[side] for pair in own], high, corner[0:1])
        return 0

    lax.fori_loop(0, HALO, rim_plane, 0)

    def induced(a_ref, ax0, halo, flat):
        def plane(x, _):
            at = x + (ax0 - halo - 1)
            there = x_first + x - halo - 1
            inside_x = (there >= 0) & (there < x_all)
            for r in windows(BASE - halo - 1, top + halo + 1):
                height = rows + (r - BASE) + z_first
                inside = (height >= 0) & (height < z_all) & inside_x

                def ld(c, j, dx=0, dz=0):
                    return a_ref[c, at + dx, j, r + dz : r + dz + ROWS, :]

                dy = {c: y_diff([ld(c, j) for j in range(blocks)]) for c in ((0,) if flat else (0, 2))}
                for j in range(blocks):
                    curl_x = ld(1, j, dz=-1) - ld(1, j, dz=1)
                    curl_y = ld(0, j, dz=1) - ld(0, j, dz=-1)
                    curl_z = ld(1, j, dx=1) - ld(1, j, dx=-1) - dy[0][j]
                    if not flat:
                        curl_x = curl_x + dy[2][j]
                        curl_y = curl_y - (ld(2, j, dx=1) - ld(2, j, dx=-1))
                    for c, value in enumerate((curl_x, curl_y, curl_z)):
                        bm[c, x, j, r : r + ROWS, :] = jnp.where(inside, value, 0.0)
            return 0

        lax.fori_loop(0, cx + 2 * halo + 2, plane, 0, unroll=6)

    def pushed(x, r):
        def ld(c, j, dx=0, dz=0):
            return bm[c, x + dx, j, r + dz : r + dz + ROWS, :]

        dy = [y_diff([ld(c, j) for j in range(blocks)]) if c != 1 else None for c in range(3)]
        weight = rub[r : r + ROWS]
        for j in range(blocks):
            field = [ld(c, j) for c in range(3)]
            current = (
                dy[2][j] - (ld(1, j, dz=1) - ld(1, j, dz=-1)),
                (ld(0, j, dz=1) - ld(0, j, dz=-1)) - (ld(2, j, dx=1) - ld(2, j, dx=-1)),
                (ld(1, j, dx=1) - ld(1, j, dx=-1)) - dy[0][j],
            )
            square = dot(field, field)
            scale = weight * (0.0625 / jnp.maximum(0.25 * square, 1.0))
            both = dot(current, field)
            yield j, [scale * (field[c] * both - current[c] * square) for c in range(3)]

    halo = HALO - 2
    induced(ap, HALO, halo, True)

    def first_step(x, _):
        for r in windows(BASE - halo, top + halo):
            for j, change in pushed(x + 1, r):
                for c in range(2):
                    an[c, x, j, r : r + ROWS, :] = ap[c, x + HALO - halo, j, r : r + ROWS, :] + change[c]
                an[2, x, j, r : r + ROWS, :] = change[2]
        return 0

    lax.fori_loop(0, cx + 2 * halo, first_step, 0, unroll=2)
    induced(an, halo, 0, False)

    def last_step(x, _):
        for z in range(0, cz, ROWS):
            for j, change in pushed(x + 1, BASE + z):
                cut = slice(j * LANES, (j + 1) * LANES)
                for c in range(3):
                    potential[c, x, z : z + ROWS, cut] = (
                        an[c, x + halo, j, BASE + z : BASE + z + ROWS, :] + change[c]
                    )
        return 0

    lax.fori_loop(0, cx, last_step, 0, unroll=2)
    matrix = dealing(ny, True)
    for out in (relaxed, potential):
        out[...] = dealt(out[...].reshape(3 * cx * cz, ny), matrix).reshape(3, cx, cz, ny)


def pack_kernel(cells, count, *refs):
    columns, (face_za, face_zb, sums0, above, corner_a, corner_b) = refs[:count], refs[count:]
    cx = above.shape[0]
    even_x = is_even("gx")
    place = lax.axis_index("gz")
    rate = half_rate(sums0, cells)

    def total(x, _):
        column = jnp.zeros(columns[0].shape[1:], jnp.float32)
        for level, part in enumerate(columns):
            column = column + jnp.where((place >> level) % 2 == 0, part[x], 0.0)
        above[x] = column[2:4] + rate * column[0:2]
        return 0

    lax.fori_loop(0, cx, total, 0)

    def plane(x, _):
        for c in range(2):
            packed = []
            for at in (x, x + cx - HALO):
                a, b = [face[(2 + c) * cx + at] + rate * face[c * cx + at] for face in (face_za, face_zb)]
                low, high = sorted_out("gz", a, b)
                packed.append(jnp.concatenate([above[at, c : c + 1], high[0 : HALO - 1], low], axis=0))
            corner_a[c, x] = jnp.where(even_x, packed[1], packed[0])
            corner_b[c, x] = jnp.where(even_x, packed[0], packed[1])
        return 0

    lax.fori_loop(0, HALO, plane, 0)


def call(kernel, outs, *args, scratch=(), cost=0, limit=8, outside=0):
    shapes = [jax.ShapeDtypeStruct(shape, jnp.float32) for shape in outs]
    return pl.pallas_call(
        kernel,
        out_shape=shapes,
        in_specs=[
            pl.BlockSpec(memory_space=pltpu.HBM if k < outside else pltpu.VMEM) for k in range(len(args))
        ],
        out_specs=[pl.BlockSpec(memory_space=pltpu.VMEM)] * len(outs),
        scratch_shapes=[pltpu.VMEM(item, jnp.float32) if isinstance(item, tuple) else item for item in scratch],
        compiler_params=pltpu.CompilerParams(vmem_limit_bytes=limit * 1024 * 1024),
        cost_estimate=pl.CostEstimate(flops=cost, bytes_accessed=cost // 10, transcendentals=0),
    )(*args)


def body(magnetic, friction):
    _, cx, cz, ny = magnetic.shape
    blocks = ny // LANES
    height = cz + 2 * BASE
    count_z, count_x = lax.axis_size("gz"), lax.axis_size("gx")
    devices = count_z * count_x
    cells = cx * cz * ny * devices
    work = cx * cz * ny * 200

    def padded(components, layers):
        return (components, cx + 2 * layers, blocks, height, LANES)

    tiles = (devices, ROWS, LANES)
    core = (3, cx, cz, ny)
    rubbed = jnp.broadcast_to(friction[:, None], (cz, LANES))

    magnetic, *faces = call(
        entry_kernel,
        [core, *[(3, HALO, cz, ny)] * 2, *[(3, cx, HALO, ny)] * 2],
        magnetic,
        scratch=[core, pltpu.SemaphoreType.DMA((3,))],
        outside=1,
        cost=work,
        limit=16,
    )
    faces_x = swapped(faces[:2], "gx")
    faces_z = swapped(faces[2:], "gz")
    corners = swapped(edges(jnp.concatenate(faces_z, axis=2), "gx", 1), "gx")
    bp, fp, sums = call(
        first_kernel,
        [padded(3, HALO), padded(3, HALO - 2), tiles],
        magnetic,
        *faces_x,
        *faces_z,
        *corners,
        scratch=[padded(11, HALO - 1)],
        cost=2 * work,
        limit=18,
    )
    core_b, core_f, *faces, sums = call(
        functools.partial(second_kernel, cells),
        [core, core, (4, HALO, cz, ny), (4, HALO, cz, ny), (5 * cx + 1, HALO, ny), (4 * cx + 1, HALO, ny), tiles],
        bp,
        fp,
        shared(sums),
        rubbed,
        scratch=[padded(3, HALO - 2), padded(11, 1)],
        cost=work,
        limit=19,
    )
    faces_z = swapped(faces[2:], "gz")
    faces_x = swapped(faces[:2], "gx")
    sums = shared(sums)
    columns = [faces_z[0][4 * cx + 1 :]]
    group = faces[2][4 * cx + 1 :] + columns[0]
    stride = 2
    while stride < count_z:
        columns.append(lax.ppermute(group, "gz", [(i, i ^ stride) for i in range(count_z)]))
        stride *= 2
        if stride < count_z:
            group = group + columns[-1]
    above, *corners = call(
        functools.partial(pack_kernel, cells, len(columns)),
        [(cx, 2, ny), (2, HALO, 2 * HALO, ny), (2, HALO, 2 * HALO, ny)],
        *columns,
        *faces_z,
        sums,
        cost=work // 50,
    )
    corners = swapped(corners, "gx")
    return tuple(
        call(
            functools.partial(third_kernel, cells),
            [core, core],
            core_b,
            core_f,
            sums,
            rubbed,
            *faces_x,
            *faces_z,
            above,
            *corners,
            scratch=[padded(2, HALO), padded(3, HALO - 1), padded(3, HALO - 2), (height, LANES)],
            cost=work,
            limit=16,
        )
    )


def solution(mesh):
    return jax.shard_map(
        body,
        mesh=mesh,
        in_specs=(P(None, "gx", "gz", "runs"), P("gz")),
        out_specs=(P(None, "gx", "gz", "runs"), P(None, "gx", "gz", "runs")),
        check_vma=False,
    )
```

```python
import functools

import jax
import jax.numpy as jnp
from jax import lax
from jax.experimental import pallas as pl
from jax.experimental.pallas import tpu as pltpu
from jax.sharding import PartitionSpec as P

DESCENTS = 2
RELAX = 2

step_scale = 0.5
time_step = 0.2

LANES = 128
ROWS = 8
HALO = 4
BASE = 8


AXES = ("runs", "gz", "gx")


def pairings(axis):
    sizes = [lax.axis_size(name) for name in AXES]
    along = AXES.index(axis)
    places = [(r, z, x) for r in range(sizes[0]) for z in range(sizes[1]) for x in range(sizes[2])]

    def flat(place):
        return (place[0] * sizes[1] + place[1]) * sizes[2] + place[2]

    def moved(place, name, to):
        return tuple(to if name == other else at for other, at in zip(AXES, place))

    first, second = [], []
    for place in places:
        at = place[along]
        if at ^ 1 < sizes[along]:
            first.append((flat(place), flat(moved(place, axis, at ^ 1))))
        to = at + 1 if at % 2 else at - 1
        if 0 <= to < sizes[along]:
            second.append((flat(place), flat(moved(place, axis, to))))
        elif sizes[0] % 2 == 0:
            second.append((flat(place), flat(moved(place, "runs", place[0] ^ 1))))
    return first, second


def is_even(axis):
    return lax.axis_index(axis) % 2 == 0


def edges(cells, axis, dim):
    far = cells.shape[dim] - HALO
    even = is_even(axis)
    first = lax.dynamic_slice_in_dim(cells, jnp.where(even, far, 0), HALO, dim)
    second = lax.dynamic_slice_in_dim(cells, jnp.where(even, 0, far), HALO, dim)
    return first, second


def swapped(pair, axis):
    first, second = pairings(axis)
    return lax.ppermute(pair[0], AXES, first), lax.ppermute(pair[1], AXES, second)


def sorted_out(axis, first, second):
    at = lax.axis_index(axis)
    even = at % 2 == 0
    low = jnp.where(at > 0, jnp.where(even, second, first), 0.0)
    high = jnp.where(at < lax.axis_size(axis) - 1, jnp.where(even, first, second), 0.0)
    return low, high


def shared(tile_copies):
    return lax.all_to_all(tile_copies, ("gz", "gx"), 0, 0)


def y_diff(blocks):
    wide = [pltpu.roll(blocks[-1], 1, 1), *blocks, pltpu.roll(blocks[0], LANES - 1, 1)]
    return [wide[j + 2] - wide[j] for j in range(len(blocks))]


def dealing(ny, back):
    blocks = ny // LANES
    source = lax.broadcasted_iota(jnp.int32, (ny, ny), 0)
    target = lax.broadcasted_iota(jnp.int32, (ny, ny), 1)
    if back:
        source, target = target, source
    return ((target % LANES) * blocks + target // LANES == source).astype(jnp.bfloat16)


def dealt(value, matrix):
    rows = value.shape[0]
    high = value.astype(jnp.bfloat16)
    rest = (value - high.astype(jnp.float32)).astype(jnp.bfloat16)
    both = jnp.dot(jnp.concatenate([high, rest], axis=0), matrix, preferred_element_type=jnp.float32)
    return both[:rows] + both[rows:]


def cross(a, b):
    return (a[1] * b[2] - a[2] * b[1], a[2] * b[0] - a[0] * b[2], a[0] * b[1] - a[1] * b[0])


def dot(a, b):
    return a[0] * b[0] + a[1] * b[1] + a[2] * b[2]


def row_index():
    return lax.broadcasted_iota(jnp.int32, (ROWS, LANES), 0)


def windows(low, high):
    return [low + ROWS * w for w in range(-(-(high - low) // ROWS))]


def own_place(cx, cz):
    return (
        lax.axis_index("gx") * cx,
        lax.axis_size("gx") * cx,
        lax.axis_index("gz") * cz,
        lax.axis_size("gz") * cz,
    )


def descent_stages(bp, plane_of, planes, halo, cz, blocks, omega_ref):
    def plane(x, _):
        at = plane_of(x)
        for r in windows(BASE - halo - 1, BASE + cz + halo + 1):
            def ld(c, j, dx=0, dz=0):
                return bp[c, at + dx, j, r + dz : r + dz + ROWS, :]

            dy = [y_diff([ld(c, j) for j in range(blocks)]) for c in range(3)]
            for j in range(blocks):
                field = [ld(c, j) for c in range(3)]
                dx = [ld(c, j, dx=1) - ld(c, j, dx=-1) for c in range(3)]
                dz = [ld(c, j, dz=1) - ld(c, j, dz=-1) for c in range(3)]
                current = (dy[2][j] - dz[1], dz[0] - dx[2], dx[1] - dy[0][j])
                spread = dx[0] + dy[1][j] + dz[2]
                square = jnp.maximum(dot(field, field), 1.0)
                inverse = 0.5 / square
                lorentz = cross(current, field)
                omega = [(lorentz[c] - spread * field[c]) * inverse for c in range(3)]
                twist = cross(omega, field)
                along = dot(omega, field)
                for k, value in enumerate([*twist, along, *omega, *current, spread]):
                    omega_ref[k, x, j, r : r + ROWS, :] = value
        return 0

    lax.fori_loop(0, planes, plane, 0, unroll=2)


def doubled_force(bp, bat, omega_ref, at, r, blocks):
    def ld(k, j, dx=0, dz=0):
        return omega_ref[k, at + dx, j, r + dz : r + dz + ROWS, :]

    dy = {k: y_diff([ld(k, j) for j in range(blocks)]) for k in (0, 2, 3)}
    for j in range(blocks):
        field = [bp[c, bat, j, r : r + ROWS, :] for c in range(3)]
        omega = [ld(4 + c, j) for c in range(3)]
        current = [ld(7 + c, j) for c in range(3)]
        spread = ld(10, j)

        def dx(k):
            return ld(k, j, dx=1) - ld(k, j, dx=-1)

        def dz(k):
            return ld(k, j, dz=1) - ld(k, j, dz=-1)

        curled = (dy[2][j] - dz(1) - dx(3), dz(0) - dx(2) - dy[3][j], dx(1) - dy[0][j] - dz(3))
        bent = cross(omega, current)
        size = dot(omega, omega)
        twice = size + size
        force = [curled[c] - bent[c] + omega[c] * spread + twice * field[c] for c in range(3)]
        yield j, force, field, size, spread


def density_of(field, size, spread):
    square = dot(field, field)
    return size * jnp.maximum(square, 1.0) + 0.25 * (spread * spread) * jnp.maximum(1.0 - square, 0.0)


def store_sums(sums_ref, functional, slope, rows):
    functional = jnp.sum(functional, axis=0, keepdims=True)
    slope = jnp.sum(slope, axis=0, keepdims=True)
    tile = jnp.where(rows == 0, functional, jnp.where(rows == 1, slope, 0.0))
    for k in range(sums_ref.shape[0]):
        sums_ref[k] = tile


def half_rate(sums_ref, cells):
    total = sums_ref[0]
    for k in range(1, sums_ref.shape[0]):
        total = total + sums_ref[k]
    functional = jnp.sum(total[0:1], axis=1, keepdims=True) / cells
    slope = jnp.sum(total[1:2], axis=1, keepdims=True) * 0.25 / cells
    return (0.5 * step_scale) * functional / (slope + 1e-6)


def entry_kernel(magnetic, core, face_xa, face_xb, face_za, face_zb):
    _, cx, cz, ny = magnetic.shape
    even_x, even_z = is_even("gx"), is_even("gz")
    matrix = dealing(ny, False)
    for c in range(3):
        value = dealt(magnetic[c].reshape(cx * cz, ny), matrix).reshape(cx, cz, ny)
        core[c] = value
        low, high = value[:HALO], value[cx - HALO :]
        face_xa[c] = jnp.where(even_x, high, low)
        face_xb[c] = jnp.where(even_x, low, high)
        low, high = value[:, :HALO], value[:, cz - HALO :]
        face_za[c] = jnp.where(even_z, high, low)
        face_zb[c] = jnp.where(even_z, low, high)


def first_forces(bp, plane_of, omega_ref, omega_of, fp, planes, x_of, cx, cz, blocks, rows, sums):
    halo = HALO - 2
    x_first, x_all, z_first, z_all = own_place(cx, cz)

    def plane(x, sums):
        functional, slope = sums
        own = x_of(x)
        own_x = (own >= 0) & (own < cx)
        inside_x = (own + x_first >= 0) & (own + x_first < x_all)
        for r in windows(BASE - halo, BASE + cz + halo):
            height = rows + (r - BASE)
            owned = (height >= 0) & (height < cz) & own_x
            inside = (height + z_first >= 0) & (height + z_first < z_all) & inside_x
            for j, force, field, size, spread in doubled_force(bp, plane_of(x), omega_ref, omega_of(x), r, blocks):
                functional = functional + jnp.where(owned, density_of(field, size, spread), 0.0)
                slope = slope + jnp.where(owned, dot(force, force), 0.0)
                for c in range(3):
                    fp[c, x, j, r : r + ROWS, :] = jnp.where(inside, force[c], 0.0)
        return functional, slope

    return lax.fori_loop(0, planes, plane, sums, unroll=4)


def z_halos(bp, c, plane, j, top, a, b):
    low, high = sorted_out("gz", a, b)
    bp[c, plane, j, BASE - HALO : BASE, :] = low
    bp[c, plane, j, top : top + HALO, :] = high


def inner_kernel(core, face_za, face_zb, bp, fp, sums_ref, omega_ref):
    _, cx, cz, ny = core.shape
    blocks = ny // LANES
    halo = HALO - 2

    def own(x, _):
        for c in range(3):
            for j in range(blocks):
                cut = slice(j * LANES, (j + 1) * LANES)
                for z in range(0, cz, ROWS):
                    bp[c, x, j, BASE + z : BASE + z + ROWS, :] = core[c, x, z : z + ROWS, cut]
                z_halos(bp, c, x, j, BASE + cz, face_za[c, x, :, cut], face_zb[c, x, :, cut])
        return 0

    lax.fori_loop(0, cx, own, 0)
    descent_stages(bp, lambda x: x + 1, cx - 2, halo, cz, blocks, omega_ref)
    zero = jnp.zeros((ROWS, LANES), jnp.float32)
    sums_ref[0], sums_ref[1] = first_forces(
        bp,
        lambda x: x + 2,
        omega_ref,
        lambda x: x + 1,
        fp,
        cx - 4,
        lambda x: x + 2,
        cx,
        cz,
        blocks,
        row_index(),
        (zero, zero),
    )


def outer_kernel(own, part, face_xa, face_xb, corner_a, corner_b, bp, fp, sums_ref, omega_ref):
    _, cx, blocks, _, _ = own.shape
    cz = face_xa.shape[2]
    halo = HALO - 2
    rows = row_index()
    top = BASE + cz

    def rim(x, _):
        for c in range(3):
            for j in range(blocks):
                cut = slice(j * LANES, (j + 1) * LANES)
                planes = (x, x + 3 * HALO)
                for r in range(0, top + BASE, ROWS):
                    bp[c, x + HALO, j, r : r + ROWS, :] = own[c, x, j, r : r + ROWS, :]
                    bp[c, x + 2 * HALO, j, r : r + ROWS, :] = own[c, x + cx - HALO, j, r : r + ROWS, :]
                for z in range(0, cz, ROWS):
                    span = slice(z, z + ROWS)
                    both = sorted_out("gx", face_xa[c, x, span, cut], face_xb[c, x, span, cut])
                    for plane, value in zip(planes, both):
                        bp[c, plane, j, BASE + z : BASE + z + ROWS, :] = value
                both = sorted_out("gx", corner_a[c, x, :, cut], corner_b[c, x, :, cut])
                for plane, value in zip(planes, both):
                    z_halos(bp, c, plane, j, top, value[:HALO], value[HALO:])
        return 0

    lax.fori_loop(0, HALO, rim, 0)
    descent_stages(bp, lambda x: x + 1 + jnp.where(x >= 6, 2, 0), 12, halo, cz, blocks, omega_ref)
    functional, slope = first_forces(
        bp,
        lambda x: x + 2 + jnp.where(x >= 4, 4, 0),
        omega_ref,
        lambda x: x + 1 + jnp.where(x >= 4, 2, 0),
        fp,
        8,
        lambda x: x - 2 + jnp.where(x >= 4, cx - 4, 0),
        cx,
        cz,
        blocks,
        rows,
        (part[0], part[1]),
    )
    store_sums(sums_ref, functional, slope, rows)


def second_kernel(
    cells, own_b, inner_f, outer_b, outer_f, sums0, friction, core_b, core_f, face_xa, face_xb, face_za, face_zb, sums_ref, bp, omega_ref
):
    _, cx, cz, ny = core_b.shape
    blocks = ny // LANES
    rows = row_index()
    even_x, even_z = is_even("gx"), is_even("gz")
    rate = half_rate(sums0, cells)
    halo = HALO - 2

    def step(x, field, at, force, there):
        for c in range(3):
            for j in range(blocks):
                for r in range(0, cz + 2 * BASE, ROWS):
                    bp[c, x, j, r : r + ROWS, :] = (
                        field[c, at, j, r : r + ROWS, :] + rate * force[c, there, j, r : r + ROWS, :]
                    )

    def inner_step(x, _):
        step(x + 4, own_b, x + 2, inner_f, x)
        return 0

    lax.fori_loop(0, cx - 4, inner_step, 0, unroll=2)
    for k in range(2):
        step(k, outer_b, k + 2, outer_f, k)
        step(k + 2, own_b, k, outer_f, k + 2)
        step(k + cx, own_b, k + cx - 2, outer_f, k + 4)
        step(k + cx + 2, outer_b, k + 12, outer_f, k + 6)
    descent_stages(bp, lambda x: x + 1, cx + 2, 0, cz, blocks, omega_ref)

    def plane(x, sums):
        functional, slope = sums
        for z in range(0, cz, ROWS):
            r = BASE + z
            for j, force, field, size, spread in doubled_force(bp, x + halo, omega_ref, x + 1, r, blocks):
                cut = slice(j * LANES, (j + 1) * LANES)
                functional = functional + density_of(field, size, spread)
                slope = slope + dot(force, force)
                for c in range(3):
                    core_b[c, x, z : z + ROWS, cut] = field[c]
                    core_f[c, x, z : z + ROWS, cut] = force[c]
        for j in range(blocks):
            cut = slice(j * LANES, (j + 1) * LANES)
            for k, (source, c) in enumerate(((core_f, 0), (core_f, 1), (core_b, 0), (core_b, 1))):
                low, high = source[c, x, 0:HALO, cut], source[c, x, cz - HALO : cz, cut]
                face_za[k * cx + x, :, cut] = jnp.where(even_z, high, low)
                face_zb[k * cx + x, :, cut] = jnp.where(even_z, low, high)
                column = source[c, x, 0:ROWS, cut]
                for z in range(ROWS, cz, ROWS):
                    column = column + source[c, x, z : z + ROWS, cut]
                face_za[4 * cx + 1 + x, k : k + 1, cut] = jnp.sum(column, axis=0, keepdims=True)
        return functional, slope

    zero = jnp.zeros((ROWS, LANES), jnp.float32)
    functional, slope = lax.fori_loop(0, cx, plane, (zero, zero), unroll=4)
    store_sums(sums_ref, functional, slope, rows)

    def faces(x, _):
        for j in range(blocks):
            cut = slice(j * LANES, (j + 1) * LANES)
            for k, (source, c) in enumerate(((core_f, 0), (core_f, 1), (core_b, 0), (core_b, 1))):
                for z in range(0, cz, ROWS):
                    low = source[c, x, z : z + ROWS, cut]
                    high = source[c, x + cx - HALO, z : z + ROWS, cut]
                    face_xa[k, x, z : z + ROWS, cut] = jnp.where(even_x, high, low)
                    face_xb[k, x, z : z + ROWS, cut] = jnp.where(even_x, low, high)
        return 0

    lax.fori_loop(0, HALO, faces, 0)
    for j in range(blocks):
        cut = slice(j * LANES, (j + 1) * LANES)
        low, high = friction[0:HALO], friction[cz - HALO : cz]
        face_za[4 * cx, :, cut] = jnp.where(even_z, high, low)
        face_zb[4 * cx, :, cut] = jnp.where(even_z, low, high)


def suffix(value, rows):
    for reach in (1, 2, 4):
        value = value + jnp.where(rows < ROWS - reach, pltpu.roll(value, ROWS - reach, 0), 0.0)
    return value


def prefix(value, rows):
    for reach in (1, 2, 4):
        value = value + jnp.where(rows >= reach, pltpu.roll(value, reach, 0), 0.0)
    return value


def column(ap, c, plane, j, low, own, high, beyond, rows):
    sign = 1.0 if c == 0 else -1.0
    out = 1 - c
    top = BASE + ROWS * len(own)
    ap[out, plane, j, top : top + HALO, :] = high
    value = ap[out, plane, j, top : top + ROWS, :]
    ap[out, plane, j, top : top + ROWS, :] = sign * (beyond - (prefix(value, rows) - value))
    carry = beyond
    for k in reversed(range(len(own))):
        value = suffix(own[k], rows) + carry
        ap[out, plane, j, BASE + k * ROWS : BASE + (k + 1) * ROWS, :] = sign * value
        carry = value[0:1]
    ap[out, plane, j, BASE - HALO : BASE, :] = low
    value = suffix(ap[out, plane, j, 0:BASE, :], rows) + carry
    ap[out, plane, j, 0:BASE, :] = jnp.where(lax.axis_index("gz") > 0, sign * value, 0.0)


def induced(a_ref, bm, planes, halo, at_of, out_of, own_of, flat, cx, cz, blocks, rows):
    x_first, x_all, z_first, z_all = own_place(cx, cz)

    def plane(x, _):
        at, out = at_of(x), out_of(x)
        there = x_first + own_of(x)
        inside_x = (there >= 0) & (there < x_all)
        for r in windows(BASE - halo, BASE + cz + halo):
            height = rows + (r - BASE) + z_first
            inside = (height >= 0) & (height < z_all) & inside_x

            def ld(c, j, dx=0, dz=0):
                return a_ref[c, at + dx, j, r + dz : r + dz + ROWS, :]

            dy = {c: y_diff([ld(c, j) for j in range(blocks)]) for c in ((0,) if flat else (0, 2))}
            for j in range(blocks):
                curl_x = ld(1, j, dz=-1) - ld(1, j, dz=1)
                curl_y = ld(0, j, dz=1) - ld(0, j, dz=-1)
                curl_z = ld(1, j, dx=1) - ld(1, j, dx=-1) - dy[0][j]
                if not flat:
                    curl_x = curl_x + dy[2][j]
                    curl_y = curl_y - (ld(2, j, dx=1) - ld(2, j, dx=-1))
                for c, value in enumerate((curl_x, curl_y, curl_z)):
                    bm[c, out, j, r : r + ROWS, :] = jnp.where(inside, value, 0.0)
        return 0

    lax.fori_loop(0, planes, plane, 0, unroll=4)


def pushed(bm, x, r, rub, blocks):
    def ld(c, j, dx=0, dz=0):
        return bm[c, x + dx, j, r + dz : r + dz + ROWS, :]

    dy = [y_diff([ld(c, j) for j in range(blocks)]) if c != 1 else None for c in range(3)]
    weight = rub[r : r + ROWS]
    for j in range(blocks):
        field = [ld(c, j) for c in range(3)]
        current = (
            dy[2][j] - (ld(1, j, dz=1) - ld(1, j, dz=-1)),
            (ld(0, j, dz=1) - ld(0, j, dz=-1)) - (ld(2, j, dx=1) - ld(2, j, dx=-1)),
            (ld(1, j, dx=1) - ld(1, j, dx=-1)) - dy[0][j],
        )
        square = dot(field, field)
        scale = weight * (0.0625 / jnp.maximum(0.25 * square, 1.0))
        both = dot(current, field)
        yield j, [scale * (field[c] * both - current[c] * square) for c in range(3)]


def first_push(ap, bm, an, rub, planes, at_of, out_of, cz, blocks):
    def plane(x, _):
        halo = HALO - 2
        for r in windows(BASE - halo, BASE + cz + halo):
            for j, change in pushed(bm, at_of(x), r, rub, blocks):
                for c in range(2):
                    an[c, out_of(x), j, r : r + ROWS, :] = ap[c, x + 2, j, r : r + ROWS, :] + change[c]
                an[2, out_of(x), j, r : r + ROWS, :] = change[2]
        return 0

    lax.fori_loop(0, planes, plane, 0, unroll=2)


def last_push(an, bm, out, rub, planes, at_of, cz, blocks):
    def plane(x, _):
        for z in range(0, cz, ROWS):
            for j, change in pushed(bm, at_of(x), BASE + z, rub, blocks):
                cut = slice(j * LANES, (j + 1) * LANES)
                for c in range(3):
                    out[c, x, z : z + ROWS, cut] = an[c, x + 2, j, BASE + z : BASE + z + ROWS, :] + change[c]
        return 0

    lax.fori_loop(0, planes, plane, 0, unroll=2)


def middle_kernel(
    cells, core_b, core_f, sums0, friction, face_za, face_zb, above, relaxed, ap, bm, an, bn, inner, rub
):
    _, cx, cz, ny = core_b.shape
    blocks = ny // LANES
    rows = row_index()
    _, _, z_first, z_all = own_place(cx, cz)
    rate = half_rate(sums0, cells)
    top = BASE + cz

    rub[BASE:top] = friction[...]
    low, high = sorted_out("gz", face_za[4 * cx, :, :LANES], face_zb[4 * cx, :, :LANES])
    rub[BASE - HALO : BASE] = low
    rub[top : top + HALO] = high
    for r in range(0, cz + 2 * BASE, ROWS):
        height = rows + (r - BASE) + z_first
        inside = (height >= 0) & (height < z_all)
        rub[r : r + ROWS] = jnp.where(inside, time_step / rub[r : r + ROWS], 0.0)

    def own_plane(x, _):
        for j in range(blocks):
            cut = slice(j * LANES, (j + 1) * LANES)
            for c in range(3):
                own = [
                    core_b[c, x, z : z + ROWS, cut] + rate * core_f[c, x, z : z + ROWS, cut]
                    for z in range(0, cz, ROWS)
                ]
                for z in range(0, cz, ROWS):
                    relaxed[c, x, z : z + ROWS, cut] = own[z // ROWS]
                if c == 2:
                    continue
                a, b = [
                    face[(2 + c) * cx + x, :, cut] + rate * face[c * cx + x, :, cut] for face in (face_za, face_zb)
                ]
                low, high = sorted_out("gz", a, b)
                column(ap, c, x, j, low, own, high, above[x, c : c + 1, cut], rows)
        return 0

    lax.fori_loop(0, cx, own_plane, 0, unroll=2)
    matrix = dealing(ny, True)
    relaxed[...] = dealt(relaxed[...].reshape(3 * cx * cz, ny), matrix).reshape(relaxed.shape)
    induced(ap, bm, cx - 2, HALO - 1, lambda x: x + 1, lambda x: x, lambda x: x + 1, True, cx, cz, blocks, rows)
    first_push(ap, bm, an, rub, cx - 4, lambda x: x + 1, lambda x: x, cz, blocks)
    induced(an, bn, cx - 6, 1, lambda x: x + 1, lambda x: x, lambda x: x + 3, False, cx, cz, blocks, rows)
    last_push(an, bn, inner, rub, cx - 8, lambda x: x + 1, cz, blocks)
    inner[...] = dealt(inner[...].reshape(-1, ny), matrix).reshape(inner.shape)


def ends_kernel(
    cells, sums0, face_xa, face_xb, corner_a, corner_b, own_ap, own_bm, own_an, own_bn, inner, rub, potential, ap, bm, an, rim
):
    _, cx, cz, ny = potential.shape
    blocks = ny // LANES
    rows = row_index()
    rate = half_rate(sums0, cells)

    def rim_plane(x, _):
        for j in range(blocks):
            cut = slice(j * LANES, (j + 1) * LANES)
            for c in range(2):
                own = []
                for z in range(0, cz, ROWS):
                    span = slice(z, z + ROWS)
                    a, b = [face[2 + c, x, span, cut] + rate * face[c, x, span, cut] for face in (face_xa, face_xb)]
                    own.append(sorted_out("gx", a, b))
                corners = sorted_out("gx", corner_a[c, x, :, cut], corner_b[c, x, :, cut])
                for side, plane in enumerate((x, x + 2 * HALO)):
                    corner = corners[side]
                    high = jnp.concatenate([corner[1:4], corner[3:4]], 0)
                    column(ap, c, plane, j, corner[4:8], [pair[side] for pair in own], high, corner[0:1], rows)
        return 0

    lax.fori_loop(0, HALO, rim_plane, 0)

    def borrow(into, source, low, high):
        for k in range(2):
            for c in range(source.shape[0]):
                into[c, 4 + k] = source[c, low + k]
                into[c, 6 + k] = source[c, high + k]

    def at_of(x):
        return x + 1 + jnp.where(x >= 4, 2, 0)

    def out_of(x):
        return x + jnp.where(x >= 4, 4, 0)

    borrow(ap, own_ap, 0, cx - 2)
    induced(ap, bm, 8, HALO - 1, at_of, out_of, lambda x: x - 3 + jnp.where(x >= 4, cx - 2, 0), True, cx, cz, blocks, rows)
    borrow(bm, own_bm, 0, cx - 4)
    first_push(ap, bm, an, rub, 8, at_of, out_of, cz, blocks)
    borrow(an, own_an, 0, cx - 6)
    induced(an, bm, 8, 1, at_of, out_of, lambda x: x - 1 + jnp.where(x >= 4, cx - 6, 0), False, cx, cz, blocks, rows)
    borrow(bm, own_bn, 0, cx - 8)
    last_push(an, bm, rim, rub, 8, at_of, cz, blocks)
    ends = dealt(rim[...].reshape(-1, ny), dealing(ny, True)).reshape(rim.shape)
    potential[:, :HALO] = ends[:, :HALO]
    potential[:, cx - HALO :] = ends[:, HALO:]
    potential[:, HALO : cx - HALO] = inner[...]


def pack_kernel(cells, count, *refs):
    columns, (face_za, face_zb, sums0, above, corner_a, corner_b) = refs[:count], refs[count:]
    cx = above.shape[0]
    even_x = is_even("gx")
    place = lax.axis_index("gz")
    rate = half_rate(sums0, cells)

    def total(x, _):
        column = jnp.zeros(columns[0].shape[1:], jnp.float32)
        for level, part in enumerate(columns):
            column = column + jnp.where((place >> level) % 2 == 0, part[x], 0.0)
        above[x] = column[2:4] + rate * column[0:2]
        return 0

    lax.fori_loop(0, cx, total, 0)

    def plane(x, _):
        for c in range(2):
            packed = []
            for at in (x, x + cx - HALO):
                a, b = [face[(2 + c) * cx + at] + rate * face[c * cx + at] for face in (face_za, face_zb)]
                low, high = sorted_out("gz", a, b)
                packed.append(jnp.concatenate([above[at, c : c + 1], high[0 : HALO - 1], low], axis=0))
            corner_a[c, x] = jnp.where(even_x, packed[1], packed[0])
            corner_b[c, x] = jnp.where(even_x, packed[0], packed[1])
        return 0

    lax.fori_loop(0, HALO, plane, 0)


def call(kernel, outs, *args, scratch=(), cost=0, limit=8, outside=0):
    shapes = [jax.ShapeDtypeStruct(shape, jnp.float32) for shape in outs]
    return pl.pallas_call(
        kernel,
        out_shape=shapes,
        in_specs=[
            pl.BlockSpec(memory_space=pltpu.HBM if k < outside else pltpu.VMEM) for k in range(len(args))
        ],
        out_specs=[pl.BlockSpec(memory_space=pltpu.VMEM)] * len(outs),
        scratch_shapes=[pltpu.VMEM(item, jnp.float32) if isinstance(item, tuple) else item for item in scratch],
        compiler_params=pltpu.CompilerParams(vmem_limit_bytes=limit * 1024 * 1024),
        cost_estimate=pl.CostEstimate(flops=cost, bytes_accessed=cost // 10, transcendentals=0),
    )(*args)


def body(magnetic, friction):
    _, cx, cz, ny = magnetic.shape
    blocks = ny // LANES
    height = cz + 2 * BASE
    count_z, count_x = lax.axis_size("gz"), lax.axis_size("gx")
    devices = count_z * count_x
    cells = cx * cz * ny * devices
    work = cx * cz * ny * 200

    def planes_of(components, planes):
        return (components, planes, blocks, height, LANES)

    def padded(components, layers):
        return planes_of(components, cx + 2 * layers)

    tiles = (devices, ROWS, LANES)
    core = (3, cx, cz, ny)
    rubbed = jnp.broadcast_to(friction[:, None], (cz, LANES))

    magnetic, *faces = call(
        entry_kernel,
        [core, *[(3, HALO, cz, ny)] * 2, *[(3, cx, HALO, ny)] * 2],
        magnetic,
        cost=work,
        limit=8,
    )
    faces_x = swapped(faces[:2], "gx")
    faces_z = swapped(faces[2:], "gz")
    corners = swapped(edges(jnp.concatenate(faces_z, axis=2), "gx", 1), "gx")
    own_b, inner_f, part = call(
        inner_kernel,
        [padded(3, 0), padded(3, -2), (2, ROWS, LANES)],
        magnetic,
        *faces_z,
        scratch=[padded(11, -1)],
        cost=work,
        limit=13,
    )
    outer_b, outer_f, sums = call(
        outer_kernel,
        [planes_of(3, 4 * HALO), planes_of(3, 8), tiles],
        own_b,
        part,
        *faces_x,
        *corners,
        scratch=[planes_of(11, 12)],
        cost=work,
        limit=12,
    )
    core_b, core_f, *faces, sums = call(
        functools.partial(second_kernel, cells),
        [core, core, (4, HALO, cz, ny), (4, HALO, cz, ny), (5 * cx + 1, HALO, ny), (4 * cx + 1, HALO, ny), tiles],
        own_b,
        inner_f,
        outer_b,
        outer_f,
        shared(sums),
        rubbed,
        scratch=[padded(3, HALO - 2), padded(11, 1)],
        cost=work,
        limit=19,
    )
    faces_z = swapped(faces[2:], "gz")
    faces_x = swapped(faces[:2], "gx")
    sums = shared(sums)
    columns = [faces_z[0][4 * cx + 1 :]]
    group = faces[2][4 * cx + 1 :] + columns[0]
    stride = 2
    while stride < count_z:
        columns.append(lax.ppermute(group, "gz", [(i, i ^ stride) for i in range(count_z)]))
        stride *= 2
        if stride < count_z:
            group = group + columns[-1]
    above, *corners = call(
        functools.partial(pack_kernel, cells, len(columns)),
        [(cx, 2, ny), (2, HALO, 2 * HALO, ny), (2, HALO, 2 * HALO, ny)],
        *columns,
        *faces_z,
        sums,
        cost=work // 50,
    )
    corners = swapped(corners, "gx")
    relaxed, *shares = call(
        functools.partial(middle_kernel, cells),
        [core, padded(2, 0), padded(3, -1), padded(3, -2), padded(3, -3), (3, cx - 2 * HALO, cz, ny), (height, LANES)],
        core_b,
        core_f,
        sums,
        rubbed,
        *faces_z,
        above,
        cost=work,
        limit=8,
    )
    (potential,) = call(
        functools.partial(ends_kernel, cells),
        [core],
        sums,
        *faces_x,
        *corners,
        *shares,
        scratch=[planes_of(2, 12), planes_of(3, 12), planes_of(3, 12), (3, 2 * HALO, cz, ny)],
        cost=work,
        limit=14,
    )
    return relaxed, potential


def solution(mesh):
    return jax.shard_map(
        body,
        mesh=mesh,
        in_specs=(P(None, "gx", "gz", "runs"), P("gz")),
        out_specs=(P(None, "gx", "gz", "runs"), P(None, "gx", "gz", "runs")),
        check_vma=False,
    )
```

```python
import functools

import jax
import jax.numpy as jnp
from jax import lax
from jax.experimental import pallas as pl
from jax.experimental.pallas import tpu as pltpu
from jax.sharding import PartitionSpec as P

DESCENTS = 2
RELAX = 2

step_scale = 0.5
time_step = 0.2

LANES = 128
ROWS = 8
HALO = 4
BASE = 8


AXES = ("runs", "gz", "gx")


def pairings(axis):
    sizes = [lax.axis_size(name) for name in AXES]
    along = AXES.index(axis)
    places = [(r, z, x) for r in range(sizes[0]) for z in range(sizes[1]) for x in range(sizes[2])]

    def flat(place):
        return (place[0] * sizes[1] + place[1]) * sizes[2] + place[2]

    def moved(place, name, to):
        return tuple(to if name == other else at for other, at in zip(AXES, place))

    first, second = [], []
    for place in places:
        at = place[along]
        if at ^ 1 < sizes[along]:
            first.append((flat(place), flat(moved(place, axis, at ^ 1))))
        to = at + 1 if at % 2 else at - 1
        if 0 <= to < sizes[along]:
            second.append((flat(place), flat(moved(place, axis, to))))
        else:
            idle = "gz" if axis == "gx" else "runs"
            at = place[AXES.index(idle)] ^ 1
            if at < sizes[AXES.index(idle)]:
                second.append((flat(place), flat(moved(place, idle, at))))
    return first, second


def is_even(axis):
    return lax.axis_index(axis) % 2 == 0


def swapped(pair, axis):
    first, second = pairings(axis)
    return lax.ppermute(pair[0], AXES, first), lax.ppermute(pair[1], AXES, second)


def sorted_out(axis, first, second):
    at = lax.axis_index(axis)
    even = at % 2 == 0
    low = jnp.where(at > 0, jnp.where(even, second, first), 0.0)
    high = jnp.where(at < lax.axis_size(axis) - 1, jnp.where(even, first, second), 0.0)
    return low, high


def shared(tile_copies):
    return lax.all_to_all(tile_copies, ("gz", "gx"), 0, 0)


def y_diff(blocks):
    wide = [pltpu.roll(blocks[-1], 1, 1), *blocks, pltpu.roll(blocks[0], LANES - 1, 1)]
    return [wide[j + 2] - wide[j] for j in range(len(blocks))]


def dealing(ny, back):
    blocks = ny // LANES
    source = lax.broadcasted_iota(jnp.int32, (ny, ny), 0)
    target = lax.broadcasted_iota(jnp.int32, (ny, ny), 1)
    if back:
        source, target = target, source
    return ((target % LANES) * blocks + target // LANES == source).astype(jnp.bfloat16)


def dealt(value, matrix):
    rows = value.shape[0]
    high = value.astype(jnp.bfloat16)
    rest = (value - high.astype(jnp.float32)).astype(jnp.bfloat16)
    both = jnp.dot(jnp.concatenate([high, rest], axis=0), matrix, preferred_element_type=jnp.float32)
    return both[:rows] + both[rows:]


def cross(a, b):
    return (a[1] * b[2] - a[2] * b[1], a[2] * b[0] - a[0] * b[2], a[0] * b[1] - a[1] * b[0])


def dot(a, b):
    return a[0] * b[0] + a[1] * b[1] + a[2] * b[2]


def row_index():
    return lax.broadcasted_iota(jnp.int32, (ROWS, LANES), 0)


def windows(low, high):
    return [low + ROWS * w for w in range(-(-(high - low) // ROWS))]


def own_place(cx, cz):
    return (
        lax.axis_index("gx") * cx,
        lax.axis_size("gx") * cx,
        lax.axis_index("gz") * cz,
        lax.axis_size("gz") * cz,
    )


def descent_stages(bp, plane_of, planes, halo, cz, blocks, omega_ref):
    def plane(x, _):
        at = plane_of(x)
        for r in windows(BASE - halo - 1, BASE + cz + halo + 1):
            def ld(c, j, dx=0, dz=0):
                return bp[c, at + dx, j, r + dz : r + dz + ROWS, :]

            dy = [y_diff([ld(c, j) for j in range(blocks)]) for c in range(3)]
            for j in range(blocks):
                field = [ld(c, j) for c in range(3)]
                dx = [ld(c, j, dx=1) - ld(c, j, dx=-1) for c in range(3)]
                dz = [ld(c, j, dz=1) - ld(c, j, dz=-1) for c in range(3)]
                current = (dy[2][j] - dz[1], dz[0] - dx[2], dx[1] - dy[0][j])
                spread = dx[0] + dy[1][j] + dz[2]
                square = jnp.maximum(dot(field, field), 1.0)
                inverse = 0.5 / square
                lorentz = cross(current, field)
                omega = [(lorentz[c] - spread * field[c]) * inverse for c in range(3)]
                twist = cross(omega, field)
                along = dot(omega, field)
                for k, value in enumerate([*twist, along, *omega, *current, spread]):
                    omega_ref[k, x, j, r : r + ROWS, :] = value
        return 0

    lax.fori_loop(0, planes, plane, 0, unroll=2)


def doubled_force(bp, bat, omega_ref, at, r, blocks):
    def ld(k, j, dx=0, dz=0):
        return omega_ref[k, at + dx, j, r + dz : r + dz + ROWS, :]

    dy = {k: y_diff([ld(k, j) for j in range(blocks)]) for k in (0, 2, 3)}
    for j in range(blocks):
        field = [bp[c, bat, j, r : r + ROWS, :] for c in range(3)]
        omega = [ld(4 + c, j) for c in range(3)]
        current = [ld(7 + c, j) for c in range(3)]
        spread = ld(10, j)

        def dx(k):
            return ld(k, j, dx=1) - ld(k, j, dx=-1)

        def dz(k):
            return ld(k, j, dz=1) - ld(k, j, dz=-1)

        curled = (dy[2][j] - dz(1) - dx(3), dz(0) - dx(2) - dy[3][j], dx(1) - dy[0][j] - dz(3))
        bent = cross(omega, current)
        size = dot(omega, omega)
        twice = size + size
        force = [curled[c] - bent[c] + omega[c] * spread + twice * field[c] for c in range(3)]
        yield j, force, field, size, spread


def density_of(field, size, spread):
    square = dot(field, field)
    return size * jnp.maximum(square, 1.0) + 0.25 * (spread * spread) * jnp.maximum(1.0 - square, 0.0)


def store_sums(sums_ref, functional, slope, rows):
    functional = jnp.sum(functional, axis=0, keepdims=True)
    slope = jnp.sum(slope, axis=0, keepdims=True)
    tile = jnp.where(rows == 0, functional, jnp.where(rows == 1, slope, 0.0))
    for k in range(sums_ref.shape[0]):
        sums_ref[k] = tile


def half_rate(sums_ref, cells):
    total = sums_ref[0]
    for k in range(1, sums_ref.shape[0]):
        total = total + sums_ref[k]
    functional = jnp.sum(total[0:1], axis=1, keepdims=True) / cells
    slope = jnp.sum(total[1:2], axis=1, keepdims=True) * 0.25 / cells
    return (0.5 * step_scale) * functional / (slope + 1e-6)


def entry_kernel(magnetic, core, face_xa, face_xb, face_za, face_zb):
    _, cx, cz, ny = magnetic.shape
    even_x, even_z = is_even("gx"), is_even("gz")
    matrix = dealing(ny, False)
    for c in range(3):
        value = dealt(magnetic[c].reshape(cx * cz, ny), matrix).reshape(cx, cz, ny)
        core[c] = value
        low, high = value[:HALO], value[cx - HALO :]
        face_xa[c] = jnp.where(even_x, high, low)
        face_xb[c] = jnp.where(even_x, low, high)
        low, high = value[:, :HALO], value[:, cz - HALO :]
        face_za[c] = jnp.where(even_z, high, low)
        face_zb[c] = jnp.where(even_z, low, high)


def first_forces(bp, plane_of, omega_ref, omega_of, fp, planes, x_of, cx, cz, blocks, rows, sums):
    halo = HALO - 2
    x_first, x_all, z_first, z_all = own_place(cx, cz)

    def plane(x, sums):
        functional, slope = sums
        own = x_of(x)
        own_x = (own >= 0) & (own < cx)
        inside_x = (own + x_first >= 0) & (own + x_first < x_all)
        for r in windows(BASE - halo, BASE + cz + halo):
            height = rows + (r - BASE)
            owned = (height >= 0) & (height < cz) & own_x
            inside = (height + z_first >= 0) & (height + z_first < z_all) & inside_x
            for j, force, field, size, spread in doubled_force(bp, plane_of(x), omega_ref, omega_of(x), r, blocks):
                functional = functional + jnp.where(owned, density_of(field, size, spread), 0.0)
                slope = slope + jnp.where(owned, dot(force, force), 0.0)
                for c in range(3):
                    fp[c, x, j, r : r + ROWS, :] = jnp.where(inside, force[c], 0.0)
        return functional, slope

    return lax.fori_loop(0, planes, plane, sums, unroll=4)


def corner_row(d):
    return sum(HALO - k for k in range(1, d))


def corner_rows(corner, first, d):
    high, low = [corner[at : at + HALO - d] for at in (first + corner_row(d), first + corner_row(HALO) + corner_row(d))]
    none = jnp.zeros((d, LANES), jnp.float32)
    if d == HALO:
        return none, none
    return jnp.concatenate([high, none], 0), jnp.concatenate([none, low], 0)


def corners_kernel(face_za, face_zb, corner_a, corner_b):
    _, cx, _, ny = face_za.shape
    even_x = is_even("gx")
    for j in range(ny // LANES):
        cut = slice(j * LANES, (j + 1) * LANES)
        packed = []
        for edge in (lambda d: d - 1, lambda d: cx - d):
            pieces = []
            for c in range(3):
                rims = [sorted_out("gz", face_za[c, edge(d), :, cut], face_zb[c, edge(d), :, cut]) for d in range(1, HALO)]
                pieces += [high[: HALO - d] for d, (_, high) in enumerate(rims, 1)]
                pieces += [low[d:] for d, (low, _) in enumerate(rims, 1)]
            pieces.append(jnp.zeros((corner_a.shape[0] - 6 * corner_row(HALO), LANES), jnp.float32))
            packed.append(jnp.concatenate(pieces, axis=0))
        corner_a[:, cut] = jnp.where(even_x, packed[1], packed[0])
        corner_b[:, cut] = jnp.where(even_x, packed[0], packed[1])


def z_halos(bp, c, plane, j, top, a, b):
    low, high = sorted_out("gz", a, b)
    bp[c, plane, j, BASE - HALO : BASE, :] = low
    bp[c, plane, j, top : top + HALO, :] = high


def inner_kernel(core, face_za, face_zb, bp, fp, sums_ref, omega_ref):
    _, cx, cz, ny = core.shape
    blocks = ny // LANES
    halo = HALO - 2

    def own(x, _):
        for c in range(3):
            for j in range(blocks):
                cut = slice(j * LANES, (j + 1) * LANES)
                for z in range(0, cz, ROWS):
                    bp[c, x, j, BASE + z : BASE + z + ROWS, :] = core[c, x, z : z + ROWS, cut]
                z_halos(bp, c, x, j, BASE + cz, face_za[c, x, :, cut], face_zb[c, x, :, cut])
        return 0

    lax.fori_loop(0, cx, own, 0)
    descent_stages(bp, lambda x: x + 1, cx - 2, halo, cz, blocks, omega_ref)
    zero = jnp.zeros((ROWS, LANES), jnp.float32)
    sums_ref[0], sums_ref[1] = first_forces(
        bp,
        lambda x: x + 2,
        omega_ref,
        lambda x: x + 1,
        fp,
        cx - 4,
        lambda x: x + 2,
        cx,
        cz,
        blocks,
        row_index(),
        (zero, zero),
    )


def outer_kernel(own, part, face_xa, face_xb, corner_a, corner_b, bp, fp, sums_ref, omega_ref):
    _, cx, blocks, _, _ = own.shape
    cz = face_xa.shape[2]
    halo = HALO - 2
    rows = row_index()
    top = BASE + cz

    def copied(x, _):
        for c in range(3):
            for j in range(blocks):
                for r in range(0, top + BASE, ROWS):
                    bp[c, x + HALO, j, r : r + ROWS, :] = own[c, x, j, r : r + ROWS, :]
                    bp[c, x + 2 * HALO, j, r : r + ROWS, :] = own[c, x + cx - HALO, j, r : r + ROWS, :]
        return 0

    lax.fori_loop(0, HALO, copied, 0)
    for d in range(1, HALO + 1):
        for c in range(3):
            for j in range(blocks):
                cut = slice(j * LANES, (j + 1) * LANES)
                corners = sorted_out("gx", corner_a[:, cut], corner_b[:, cut])
                for side, (plane, k) in enumerate(((HALO - d, HALO - d), (3 * HALO + d - 1, d - 1))):
                    for z in range(0, cz, ROWS):
                        span = slice(z, z + ROWS)
                        value = sorted_out("gx", face_xa[c, k, span, cut], face_xb[c, k, span, cut])[side]
                        bp[c, plane, j, BASE + z : BASE + z + ROWS, :] = value
                    high, low = corner_rows(corners[side], 2 * c * corner_row(HALO), d)
                    bp[c, plane, j, BASE - HALO : BASE, :] = low
                    bp[c, plane, j, top : top + HALO, :] = high
    descent_stages(bp, lambda x: x + 1 + jnp.where(x >= 6, 2, 0), 12, halo, cz, blocks, omega_ref)
    functional, slope = first_forces(
        bp,
        lambda x: x + 2 + jnp.where(x >= 4, 4, 0),
        omega_ref,
        lambda x: x + 1 + jnp.where(x >= 4, 2, 0),
        fp,
        8,
        lambda x: x - 2 + jnp.where(x >= 4, cx - 4, 0),
        cx,
        cz,
        blocks,
        rows,
        (part[0], part[1]),
    )
    store_sums(sums_ref, functional, slope, rows)


def second_kernel(
    cells, own_b, inner_f, outer_b, outer_f, sums0, core_b, core_f, bp, sums_ref, omega_ref
):
    _, cx, cz, ny = core_b.shape
    blocks = ny // LANES
    rows = row_index()
    even_x, even_z = is_even("gx"), is_even("gz")
    rate = half_rate(sums0, cells)
    halo = HALO - 2

    def step(x, field, at, force, there):
        for c in range(3):
            for j in range(blocks):
                for r in range(0, cz + 2 * BASE, ROWS):
                    bp[c, x, j, r : r + ROWS, :] = (
                        field[c, at, j, r : r + ROWS, :] + rate * force[c, there, j, r : r + ROWS, :]
                    )

    def inner_step(x, _):
        step(x + 4, own_b, x + 2, inner_f, x)
        return 0

    lax.fori_loop(0, cx - 4, inner_step, 0, unroll=2)
    for k in range(2):
        step(k, outer_b, k + 2, outer_f, k)
        step(k + 2, own_b, k, outer_f, k + 2)
        step(k + cx, own_b, k + cx - 2, outer_f, k + 4)
        step(k + cx + 2, outer_b, k + 12, outer_f, k + 6)
    descent_stages(bp, lambda x: x + 1, cx + 2, 0, cz, blocks, omega_ref)

    def plane(x, sums):
        functional, slope = sums
        for z in range(0, cz, ROWS):
            r = BASE + z
            for j, force, field, size, spread in doubled_force(bp, x + halo, omega_ref, x + 1, r, blocks):
                cut = slice(j * LANES, (j + 1) * LANES)
                functional = functional + density_of(field, size, spread)
                slope = slope + dot(force, force)
                for c in range(3):
                    core_b[c, x, z : z + ROWS, cut] = field[c]
                    core_f[c, x, z : z + ROWS, cut] = force[c]
        return functional, slope

    zero = jnp.zeros((ROWS, LANES), jnp.float32)
    functional, slope = lax.fori_loop(0, cx, plane, (zero, zero), unroll=4)
    store_sums(sums_ref, functional, slope, rows)


LAYERS = [(0, 0, d) for d in (1, 2, 3, 4)] + [(0, 1, d) for d in (1, 2, 3)] + [(1, 0, 3), (1, 0, 4), (1, 1, 3)]


def faces_kernel(core_b, core_f, friction, face_xa, face_xb, face_za, face_zb):
    _, cx, cz, ny = core_b.shape
    blocks = ny // LANES
    even_x, even_z = is_even("gx"), is_even("gz")

    def plane(x, _):
        for j in range(blocks):
            cut = slice(j * LANES, (j + 1) * LANES)
            for c in range(2):
                low, high = core_f[c, x, 0:HALO, cut], core_f[c, x, cz - HALO : cz, cut]
                face_za[c * cx + x, :, cut] = jnp.where(even_z, high, low)
                face_zb[c * cx + x, :, cut] = jnp.where(even_z, low, high)
                low, high = core_b[c, x, 2:4, cut], core_b[c, x, cz - 4 : cz - 2, cut]
                face_za[2 * cx + x, 2 * c : 2 * c + 2, cut] = jnp.where(even_z, high, low)
                face_zb[2 * cx + x, 2 * c : 2 * c + 2, cut] = jnp.where(even_z, low, high)
            for k, (source, c) in enumerate(((core_f, 0), (core_f, 1), (core_b, 0), (core_b, 1))):
                value = source[c, x, 0:ROWS, cut]
                for z in range(ROWS, cz, ROWS):
                    value = value + source[c, x, z : z + ROWS, cut]
                face_za[3 * cx + 1 + x, k : k + 1, cut] = jnp.sum(value, axis=0, keepdims=True)
        return 0

    lax.fori_loop(0, cx, plane, 0, unroll=4)
    for j in range(blocks):
        cut = slice(j * LANES, (j + 1) * LANES)
        for k, (which, c, d) in enumerate(LAYERS):
            source = (core_f, core_b)[which]
            for z in range(0, cz, ROWS):
                low, high = source[c, d - 1, z : z + ROWS, cut], source[c, cx - d, z : z + ROWS, cut]
                face_xa[k, z : z + ROWS, cut] = jnp.where(even_x, high, low)
                face_xb[k, z : z + ROWS, cut] = jnp.where(even_x, low, high)
        low, high = friction[0:HALO], friction[cz - HALO : cz]
        face_za[3 * cx, :, cut] = jnp.where(even_z, high, low)
        face_zb[3 * cx, :, cut] = jnp.where(even_z, low, high)


def z_rims(face_za, face_zb, bp, rate, cx, cz, c, x, j):
    cut = slice(j * LANES, (j + 1) * LANES)
    top = BASE + cz
    force = sorted_out("gz", face_za[c * cx + x, :, cut], face_zb[c * cx + x, :, cut])
    span = slice(2 * c, 2 * c + 2)
    far = sorted_out("gz", face_za[2 * cx + x, span, cut], face_zb[2 * cx + x, span, cut])
    low = jnp.concatenate([far[0], bp[c, x + 2, j, BASE - 2 : BASE, :]], axis=0)
    high = jnp.concatenate([bp[c, x + 2, j, top : top + 2, :], far[1]], axis=0)
    return low + rate * force[0], high + rate * force[1]


def suffix(value, rows):
    for reach in (1, 2, 4):
        value = value + jnp.where(rows < ROWS - reach, pltpu.roll(value, ROWS - reach, 0), 0.0)
    return value


def prefix(value, rows):
    for reach in (1, 2, 4):
        value = value + jnp.where(rows >= reach, pltpu.roll(value, reach, 0), 0.0)
    return value


def column(ap, c, plane, j, low, own, high, beyond, rows):
    sign = 1.0 if c == 0 else -1.0
    out = 1 - c
    top = BASE + ROWS * len(own)
    ap[out, plane, j, top : top + HALO, :] = high
    value = ap[out, plane, j, top : top + ROWS, :]
    ap[out, plane, j, top : top + ROWS, :] = sign * (beyond - (prefix(value, rows) - value))
    carry = beyond
    for k in reversed(range(len(own))):
        value = suffix(own[k], rows) + carry
        ap[out, plane, j, BASE + k * ROWS : BASE + (k + 1) * ROWS, :] = sign * value
        carry = value[0:1]
    ap[out, plane, j, BASE - HALO : BASE, :] = low
    value = suffix(ap[out, plane, j, 0:BASE, :], rows) + carry
    ap[out, plane, j, 0:BASE, :] = jnp.where(lax.axis_index("gz") > 0, sign * value, 0.0)


def induced(a_ref, bm, planes, halo, at_of, out_of, own_of, flat, cx, cz, blocks, rows):
    x_first, x_all, z_first, z_all = own_place(cx, cz)

    def plane(x, _):
        at, out = at_of(x), out_of(x)
        there = x_first + own_of(x)
        inside_x = (there >= 0) & (there < x_all)
        for r in windows(BASE - halo, BASE + cz + halo):
            height = rows + (r - BASE) + z_first
            inside = (height >= 0) & (height < z_all) & inside_x

            def ld(c, j, dx=0, dz=0):
                return a_ref[c, at + dx, j, r + dz : r + dz + ROWS, :]

            dy = {c: y_diff([ld(c, j) for j in range(blocks)]) for c in ((0,) if flat else (0, 2))}
            for j in range(blocks):
                curl_x = ld(1, j, dz=-1) - ld(1, j, dz=1)
                curl_y = ld(0, j, dz=1) - ld(0, j, dz=-1)
                curl_z = ld(1, j, dx=1) - ld(1, j, dx=-1) - dy[0][j]
                if not flat:
                    curl_x = curl_x + dy[2][j]
                    curl_y = curl_y - (ld(2, j, dx=1) - ld(2, j, dx=-1))
                for c, value in enumerate((curl_x, curl_y, curl_z)):
                    bm[c, out, j, r : r + ROWS, :] = jnp.where(inside, value, 0.0)
        return 0

    lax.fori_loop(0, planes, plane, 0, unroll=4)


def pushed(bm, x, r, rub, blocks):
    def ld(c, j, dx=0, dz=0):
        return bm[c, x + dx, j, r + dz : r + dz + ROWS, :]

    dy = [y_diff([ld(c, j) for j in range(blocks)]) if c != 1 else None for c in range(3)]
    weight = rub[r : r + ROWS]
    for j in range(blocks):
        field = [ld(c, j) for c in range(3)]
        current = (
            dy[2][j] - (ld(1, j, dz=1) - ld(1, j, dz=-1)),
            (ld(0, j, dz=1) - ld(0, j, dz=-1)) - (ld(2, j, dx=1) - ld(2, j, dx=-1)),
            (ld(1, j, dx=1) - ld(1, j, dx=-1)) - dy[0][j],
        )
        square = dot(field, field)
        scale = weight * (0.0625 / jnp.maximum(0.25 * square, 1.0))
        both = dot(current, field)
        yield j, [scale * (field[c] * both - current[c] * square) for c in range(3)]


def first_push(ap, bm, an, rub, planes, at_of, out_of, cz, blocks):
    def plane(x, _):
        halo = HALO - 2
        for r in windows(BASE - halo, BASE + cz + halo):
            for j, change in pushed(bm, at_of(x), r, rub, blocks):
                for c in range(2):
                    an[c, out_of(x), j, r : r + ROWS, :] = ap[c, x + 2, j, r : r + ROWS, :] + change[c]
                an[2, out_of(x), j, r : r + ROWS, :] = change[2]
        return 0

    lax.fori_loop(0, planes, plane, 0, unroll=2)


def last_push(an, bm, out, rub, planes, at_of, cz, blocks):
    def plane(x, _):
        for z in range(0, cz, ROWS):
            for j, change in pushed(bm, at_of(x), BASE + z, rub, blocks):
                cut = slice(j * LANES, (j + 1) * LANES)
                for c in range(3):
                    out[c, x, z : z + ROWS, cut] = an[c, x + 2, j, BASE + z : BASE + z + ROWS, :] + change[c]
        return 0

    lax.fori_loop(0, planes, plane, 0, unroll=2)


def middle_kernel(
    cells, core_b, core_f, bp, sums0, friction, face_za, face_zb, above, relaxed, ap, bm, an, bn, inner, rub
):
    _, cx, cz, ny = core_b.shape
    blocks = ny // LANES
    rows = row_index()
    _, _, z_first, z_all = own_place(cx, cz)
    rate = half_rate(sums0, cells)
    top = BASE + cz

    rub[BASE:top] = friction[...]
    low, high = sorted_out("gz", face_za[3 * cx, :, :LANES], face_zb[3 * cx, :, :LANES])
    rub[BASE - HALO : BASE] = low
    rub[top : top + HALO] = high
    for r in range(0, cz + 2 * BASE, ROWS):
        height = rows + (r - BASE) + z_first
        inside = (height >= 0) & (height < z_all)
        rub[r : r + ROWS] = jnp.where(inside, time_step / rub[r : r + ROWS], 0.0)

    def own_plane(x, _):
        for j in range(blocks):
            cut = slice(j * LANES, (j + 1) * LANES)
            for c in range(3):
                own = [
                    core_b[c, x, z : z + ROWS, cut] + rate * core_f[c, x, z : z + ROWS, cut]
                    for z in range(0, cz, ROWS)
                ]
                for z in range(0, cz, ROWS):
                    relaxed[c, x, z : z + ROWS, cut] = own[z // ROWS]
                if c == 2:
                    continue
                low, high = z_rims(face_za, face_zb, bp, rate, cx, cz, c, x, j)
                column(ap, c, x, j, low, own, high, above[x, c : c + 1, cut], rows)
        return 0

    lax.fori_loop(0, cx, own_plane, 0, unroll=2)
    matrix = dealing(ny, True)
    relaxed[...] = dealt(relaxed[...].reshape(3 * cx * cz, ny), matrix).reshape(relaxed.shape)
    induced(ap, bm, cx - 2, HALO - 1, lambda x: x + 1, lambda x: x, lambda x: x + 1, True, cx, cz, blocks, rows)
    first_push(ap, bm, an, rub, cx - 4, lambda x: x + 1, lambda x: x, cz, blocks)
    induced(an, bn, cx - 6, 1, lambda x: x + 1, lambda x: x, lambda x: x + 3, False, cx, cz, blocks, rows)
    last_push(an, bn, inner, rub, cx - 8, lambda x: x + 1, cz, blocks)
    inner[...] = dealt(inner[...].reshape(-1, ny), matrix).reshape(inner.shape)


def ends_kernel(
    cells, bp, sums0, face_xa, face_xb, corner_a, corner_b, own_ap, own_bm, own_an, own_bn, inner, rub, potential, ap, bm, an, rim
):
    _, cx, cz, ny = potential.shape
    blocks = ny // LANES
    rows = row_index()
    rate = half_rate(sums0, cells)

    for d in range(1, HALO + 1):
        for c in range(2):
            if (0, c, d) not in LAYERS:
                continue
            for j in range(blocks):
                cut = slice(j * LANES, (j + 1) * LANES)

                def layer(which, span):
                    k = LAYERS.index((which, c, d))
                    return sorted_out("gx", face_xa[k, span, cut], face_xb[k, span, cut])

                own = ([], [])
                for z in range(0, cz, ROWS):
                    force = layer(0, slice(z, z + ROWS))
                    if d <= 2:
                        field = [bp[c, at, j, BASE + z : BASE + z + ROWS, :] for at in (2 - d, cx + 1 + d)]
                    else:
                        field = layer(1, slice(z, z + ROWS))
                    for side in range(2):
                        own[side].append(field[side] + rate * force[side])
                corners = sorted_out("gx", corner_a[c, :, cut], corner_b[c, :, cut])
                for side, plane in enumerate((HALO - d, 2 * HALO + d - 1)):
                    corner = corners[side]
                    high, low = corner_rows(corner, HALO, d)
                    column(ap, c, plane, j, low, own[side], high, corner[d - 1 : d], rows)

    def borrow(into, source, low, high):
        for k in range(2):
            for c in range(source.shape[0]):
                into[c, 4 + k] = source[c, low + k]
                into[c, 6 + k] = source[c, high + k]

    def at_of(x):
        return x + 1 + jnp.where(x >= 4, 2, 0)

    def out_of(x):
        return x + jnp.where(x >= 4, 4, 0)

    borrow(ap, own_ap, 0, cx - 2)
    induced(ap, bm, 8, HALO - 1, at_of, out_of, lambda x: x - 3 + jnp.where(x >= 4, cx - 2, 0), True, cx, cz, blocks, rows)
    borrow(bm, own_bm, 0, cx - 4)
    first_push(ap, bm, an, rub, 8, at_of, out_of, cz, blocks)
    borrow(an, own_an, 0, cx - 6)
    induced(an, bm, 8, 1, at_of, out_of, lambda x: x - 1 + jnp.where(x >= 4, cx - 6, 0), False, cx, cz, blocks, rows)
    borrow(bm, own_bn, 0, cx - 8)
    last_push(an, bm, rim, rub, 8, at_of, cz, blocks)
    ends = dealt(rim[...].reshape(-1, ny), dealing(ny, True)).reshape(rim.shape)
    potential[:, :HALO] = ends[:, :HALO]
    potential[:, cx - HALO :] = ends[:, HALO:]
    potential[:, HALO : cx - HALO] = inner[...]


def pack_kernel(cells, count, *refs):
    columns, (face_za, face_zb, bp, sums0, above, corner_a, corner_b) = refs[:count], refs[count:]
    cx, _, ny = above.shape
    cz = bp.shape[3] - 2 * BASE
    even_x = is_even("gx")
    place = lax.axis_index("gz")
    rate = half_rate(sums0, cells)

    def total(x, _):
        column = jnp.zeros(columns[0].shape[1:], jnp.float32)
        for level, part in enumerate(columns):
            column = column + jnp.where((place >> level) % 2 == 0, part[x], 0.0)
        above[x] = column[2:4] + rate * column[0:2]
        return 0

    lax.fori_loop(0, cx, total, 0, unroll=4)
    for c in range(2):
        for j in range(ny // LANES):
            cut = slice(j * LANES, (j + 1) * LANES)
            packed = []
            for edge in (lambda d: d - 1, lambda d: cx - d):
                rims = [z_rims(face_za, face_zb, bp, rate, cx, cz, c, edge(d), j) for d in range(1, HALO)]
                pieces = [above[edge(d), c : c + 1, cut] for d in range(1, HALO + 1)]
                pieces += [high[: HALO - d] for d, (_, high) in enumerate(rims, 1)]
                pieces += [low[d:] for d, (low, _) in enumerate(rims, 1)]
                packed.append(jnp.concatenate(pieces, axis=0))
            corner_a[c, :, cut] = jnp.where(even_x, packed[1], packed[0])
            corner_b[c, :, cut] = jnp.where(even_x, packed[0], packed[1])


def call(kernel, outs, *args, scratch=(), cost=0, limit=8, outside=0):
    shapes = [jax.ShapeDtypeStruct(shape, jnp.float32) for shape in outs]
    return pl.pallas_call(
        kernel,
        out_shape=shapes,
        in_specs=[
            pl.BlockSpec(memory_space=pltpu.HBM if k < outside else pltpu.VMEM) for k in range(len(args))
        ],
        out_specs=[pl.BlockSpec(memory_space=pltpu.VMEM)] * len(outs),
        scratch_shapes=[pltpu.VMEM(item, jnp.float32) if isinstance(item, tuple) else item for item in scratch],
        compiler_params=pltpu.CompilerParams(vmem_limit_bytes=limit * 1024 * 1024),
        cost_estimate=pl.CostEstimate(flops=cost, bytes_accessed=cost // 10, transcendentals=0),
    )(*args)


def body(magnetic, friction):
    _, cx, cz, ny = magnetic.shape
    blocks = ny // LANES
    height = cz + 2 * BASE
    count_z, count_x = lax.axis_size("gz"), lax.axis_size("gx")
    devices = count_z * count_x
    cells = cx * cz * ny * devices
    work = cx * cz * ny * 200

    def planes_of(components, planes):
        return (components, planes, blocks, height, LANES)

    def padded(components, layers):
        return planes_of(components, cx + 2 * layers)

    tiles = (devices, ROWS, LANES)
    core = (3, cx, cz, ny)
    rubbed = jnp.broadcast_to(friction[:, None], (cz, LANES))

    magnetic, *faces = call(
        entry_kernel,
        [core, *[(3, HALO, cz, ny)] * 2, *[(3, cx, HALO, ny)] * 2],
        magnetic,
        cost=work,
        limit=8,
    )
    faces_x = swapped(faces[:2], "gx")
    faces_z = swapped(faces[2:], "gz")
    corners = call(
        corners_kernel,
        [(-(-6 * corner_row(HALO) // ROWS) * ROWS, ny)] * 2,
        *faces_z,
        cost=work // 50,
    )
    corners = swapped(corners, "gx")
    own_b, inner_f, part = call(
        inner_kernel,
        [padded(3, 0), padded(3, -2), (2, ROWS, LANES)],
        magnetic,
        *faces_z,
        scratch=[padded(11, -1)],
        cost=work,
        limit=13,
    )
    outer_b, outer_f, sums = call(
        outer_kernel,
        [planes_of(3, 4 * HALO), planes_of(3, 8), tiles],
        own_b,
        part,
        *faces_x,
        *corners,
        scratch=[planes_of(11, 12)],
        cost=work,
        limit=12,
    )
    core_b, core_f, bp, sums = call(
        functools.partial(second_kernel, cells),
        [core, core, padded(3, HALO - 2), tiles],
        own_b,
        inner_f,
        outer_b,
        outer_f,
        shared(sums),
        scratch=[padded(11, 1)],
        cost=work,
        limit=15,
    )
    faces = call(
        faces_kernel,
        [*[(len(LAYERS), cz, ny)] * 2, (4 * cx + 1, HALO, ny), (3 * cx + 1, HALO, ny)],
        core_b,
        core_f,
        rubbed,
        cost=work,
    )
    faces_z = swapped(faces[2:], "gz")
    faces_x = swapped(faces[:2], "gx")
    sums = shared(sums)
    columns = [faces_z[0][3 * cx + 1 :]]
    group = faces[2][3 * cx + 1 :] + columns[0]
    stride = 2
    while stride < count_z:
        columns.append(lax.ppermute(group, "gz", [(i, i ^ stride) for i in range(count_z)]))
        stride *= 2
        if stride < count_z:
            group = group + columns[-1]
    above, *corners = call(
        functools.partial(pack_kernel, cells, len(columns)),
        [(cx, 2, ny), *[(2, HALO + 2 * corner_row(HALO), ny)] * 2],
        *columns,
        *faces_z,
        bp,
        sums,
        cost=work // 50,
    )
    corners = swapped(corners, "gx")
    relaxed, *shares = call(
        functools.partial(middle_kernel, cells),
        [core, padded(2, 0), padded(3, -1), padded(3, -2), padded(3, -3), (3, cx - 2 * HALO, cz, ny), (height, LANES)],
        core_b,
        core_f,
        bp,
        sums,
        rubbed,
        *faces_z,
        above,
        cost=work,
        limit=8,
    )
    (potential,) = call(
        functools.partial(ends_kernel, cells),
        [core],
        bp,
        sums,
        *faces_x,
        *corners,
        *shares,
        scratch=[planes_of(2, 12), planes_of(3, 12), planes_of(3, 12), (3, 2 * HALO, cz, ny)],
        cost=work,
        limit=14,
    )
    return relaxed, potential


def solution(mesh):
    return jax.shard_map(
        body,
        mesh=mesh,
        in_specs=(P(None, "gx", "gz", "runs"), P("gz")),
        out_specs=(P(None, "gx", "gz", "runs"), P(None, "gx", "gz", "runs")),
        check_vma=False,
    )
```

```python
import functools

import jax
import jax.numpy as jnp
from jax import lax
from jax.experimental import pallas as pl
from jax.experimental.pallas import tpu as pltpu
from jax.sharding import PartitionSpec as P

DESCENTS = 2
RELAX = 2

step_scale = 0.5
time_step = 0.2

LANES = 128
ROWS = 8
HALO = 4
BASE = 8


AXES = ("runs", "gz", "gx")


def pairings(axis):
    sizes = [lax.axis_size(name) for name in AXES]
    along = AXES.index(axis)
    places = [(r, z, x) for r in range(sizes[0]) for z in range(sizes[1]) for x in range(sizes[2])]

    def flat(place):
        return (place[0] * sizes[1] + place[1]) * sizes[2] + place[2]

    def moved(place, name, to):
        return tuple(to if name == other else at for other, at in zip(AXES, place))

    first, second = [], []
    for place in places:
        at = place[along]
        if at ^ 1 < sizes[along]:
            first.append((flat(place), flat(moved(place, axis, at ^ 1))))
        to = at + 1 if at % 2 else at - 1
        if 0 <= to < sizes[along]:
            second.append((flat(place), flat(moved(place, axis, to))))
        else:
            idle = "gz" if axis == "gx" else "runs"
            at = place[AXES.index(idle)] ^ 1
            if at < sizes[AXES.index(idle)]:
                second.append((flat(place), flat(moved(place, idle, at))))
    return first, second


def is_even(axis):
    return lax.axis_index(axis) % 2 == 0


def swapped(pair, axis):
    first, second = pairings(axis)
    return lax.ppermute(pair[0], AXES, first), lax.ppermute(pair[1], AXES, second)


def sorted_out(axis, first, second):
    at = lax.axis_index(axis)
    even = at % 2 == 0
    low = jnp.where(at > 0, jnp.where(even, second, first), 0.0)
    high = jnp.where(at < lax.axis_size(axis) - 1, jnp.where(even, first, second), 0.0)
    return low, high


def shared(tile_copies):
    return lax.all_to_all(tile_copies, ("gz", "gx"), 0, 0)


def y_diff(blocks):
    wide = [pltpu.roll(blocks[-1], 1, 1), *blocks, pltpu.roll(blocks[0], LANES - 1, 1)]
    return [wide[j + 2] - wide[j] for j in range(len(blocks))]


def dealing(ny, back):
    blocks = ny // LANES
    source = lax.broadcasted_iota(jnp.int32, (ny, ny), 0)
    target = lax.broadcasted_iota(jnp.int32, (ny, ny), 1)
    if back:
        source, target = target, source
    return ((target % LANES) * blocks + target // LANES == source).astype(jnp.bfloat16)


def dealt(value, matrix):
    rows = value.shape[0]
    high = value.astype(jnp.bfloat16)
    rest = (value - high.astype(jnp.float32)).astype(jnp.bfloat16)
    both = jnp.dot(jnp.concatenate([high, rest], axis=0), matrix, preferred_element_type=jnp.float32)
    return both[:rows] + both[rows:]


def dot(a, b):
    return a[0] * b[0] + a[1] * b[1] + a[2] * b[2]


def row_index():
    return lax.broadcasted_iota(jnp.int32, (ROWS, LANES), 0)


def windows(low, high):
    return [low + ROWS * w for w in range(-(-(high - low) // ROWS))]


def own_place(cx, cz):
    return (
        lax.axis_index("gx") * cx,
        lax.axis_size("gx") * cx,
        lax.axis_index("gz") * cz,
        lax.axis_size("gz") * cz,
    )


def row_mask(rows, r, cz):
    height = rows + (r - BASE)
    return None if BASE <= r and r + ROWS <= BASE + cz else (height >= 0) & (height < cz)


def masked(value, *conditions):
    for condition in conditions:
        if condition is not None:
            value = jnp.where(condition, value, 0.0)
    return value


def descent_stages(bp, plane_of, planes, halo, cz, blocks, parts_ref, counted, functional, rows):
    def plane(x, functional):
        at = plane_of(x)
        for r in windows(BASE - halo - 1, BASE + cz + halo + 1):
            own = row_mask(rows, r, cz)

            def ld(c, j, dx=0, dz=0):
                return bp[c, at + dx, j, r + dz : r + dz + ROWS, :]

            dy = [y_diff([ld(c, j) for j in range(blocks)]) for c in range(3)]
            for j in range(blocks):
                field = [ld(c, j) for c in range(3)]
                dx = [ld(c, j, dx=1) - ld(c, j, dx=-1) for c in range(3)]
                dz = [ld(c, j, dz=1) - ld(c, j, dz=-1) for c in range(3)]
                current = (dy[2][j] - dz[1], dz[0] - dx[2], dx[1] - dy[0][j])
                spread = dx[0] + dy[1][j] + dz[2]
                square = dot(field, field)
                inverse = 1.0 / jnp.maximum(square, 1.0)
                capped = jnp.minimum(square, 1.0)
                along = dot(current, field)
                ratio = along * inverse
                bulk = dot(current, current)
                spread_square = spread * spread
                pull = (bulk + spread_square) * inverse * (1.0 - capped) + ratio * ratio
                density = bulk * capped - ratio * along + spread_square
                functional = functional + masked(density, own, None if counted is None else counted(x))
                twist = [ratio * field[c] - capped * current[c] for c in range(3)]
                local = [ratio * current[c] - pull * field[c] for c in range(3)]
                for k, value in enumerate([*twist, capped * spread, *local]):
                    parts_ref[k, x, j, r : r + ROWS, :] = value
        return functional

    return lax.fori_loop(0, planes, plane, functional, unroll=2)


def forces(parts_ref, at, r, blocks):
    def ld(k, j, dx=0, dz=0):
        return parts_ref[k, at + dx, j, r + dz : r + dz + ROWS, :]

    dy = {k: y_diff([ld(k, j) for j in range(blocks)]) for k in (0, 2, 3)}
    for j in range(blocks):

        def dx(k):
            return ld(k, j, dx=1) - ld(k, j, dx=-1)

        def dz(k):
            return ld(k, j, dz=1) - ld(k, j, dz=-1)

        yield j, [
            (dy[2][j] - dz(1)) + (dx(3) + ld(4, j)),
            (dz(0) - dx(2)) + (dy[3][j] + ld(5, j)),
            (dx(1) - dy[0][j]) + (dz(3) + ld(6, j)),
        ]


def store_sums(sums_ref, functional, slope, rows):
    functional = jnp.sum(functional, axis=0, keepdims=True)
    slope = jnp.sum(slope, axis=0, keepdims=True)
    tile = jnp.where(rows == 0, functional, jnp.where(rows == 1, slope, 0.0))
    for k in range(sums_ref.shape[0]):
        sums_ref[k] = tile


def rate_of(sums_ref, cells):
    total = sums_ref[0]
    for k in range(1, sums_ref.shape[0]):
        total = total + sums_ref[k]
    functional = jnp.sum(total[0:1], axis=1, keepdims=True) * 0.25 / cells
    slope = jnp.sum(total[1:2], axis=1, keepdims=True) * 0.0625 / cells
    return (0.25 * step_scale) * functional / (slope + 1e-6)


def entry_kernel(magnetic, core, face_xa, face_xb, face_za, face_zb):
    _, cx, cz, ny = magnetic.shape
    even_x, even_z = is_even("gx"), is_even("gz")
    matrix = dealing(ny, False)
    for c in range(3):
        value = dealt(magnetic[c].reshape(cx * cz, ny), matrix).reshape(cx, cz, ny)
        core[c] = value
        low, high = value[:HALO], value[cx - HALO :]
        face_xa[c] = jnp.where(even_x, high, low)
        face_xb[c] = jnp.where(even_x, low, high)
        low, high = value[:, :HALO], value[:, cz - HALO :]
        face_za[c] = jnp.where(even_z, high, low)
        face_zb[c] = jnp.where(even_z, low, high)


def first_forces(parts_ref, parts_of, fp, planes, x_of, cx, cz, blocks, rows, slope):
    halo = HALO - 2
    x_first, x_all, z_first, z_all = own_place(cx, cz)

    def plane(x, slope):
        own_x = inside_x = None
        if x_of is not None:
            own = x_of(x)
            own_x = (own >= 0) & (own < cx)
            inside_x = (own + x_first >= 0) & (own + x_first < x_all)
        for r in windows(BASE - halo, BASE + cz + halo):
            own_z = row_mask(rows, r, cz)
            height = rows + (r - BASE) + z_first
            inside_z = None if own_z is None else (height >= 0) & (height < z_all)
            for j, force in forces(parts_ref, parts_of(x), r, blocks):
                slope = slope + masked(dot(force, force), own_z, own_x)
                for c in range(3):
                    fp[c, x, j, r : r + ROWS, :] = masked(force[c], inside_z, inside_x)
        return slope

    return lax.fori_loop(0, planes, plane, slope, unroll=4)


def z_halos(bp, c, plane, j, top, a, b):
    low, high = sorted_out("gz", a, b)
    bp[c, plane, j, BASE - HALO : BASE, :] = low
    bp[c, plane, j, top : top + HALO, :] = high


def corner_row(d):
    return sum(HALO - k for k in range(1, d))


def corner_rows(corner, first, d):
    high, low = [corner[at : at + HALO - d] for at in (first + corner_row(d), first + corner_row(HALO) + corner_row(d))]
    none = jnp.zeros((d, LANES), jnp.float32)
    if d == HALO:
        return none, none
    return jnp.concatenate([high, none], 0), jnp.concatenate([none, low], 0)


def corners_kernel(face_za, face_zb, corner_a, corner_b):
    _, cx, _, ny = face_za.shape
    even_x = is_even("gx")
    for j in range(ny // LANES):
        cut = slice(j * LANES, (j + 1) * LANES)
        packed = []
        for edge in (lambda d: d - 1, lambda d: cx - d):
            pieces = []
            for c in range(3):
                rims = [sorted_out("gz", face_za[c, edge(d), :, cut], face_zb[c, edge(d), :, cut]) for d in range(1, HALO)]
                pieces += [high[: HALO - d] for d, (_, high) in enumerate(rims, 1)]
                pieces += [low[d:] for d, (low, _) in enumerate(rims, 1)]
            pieces.append(jnp.zeros((corner_a.shape[0] - 6 * corner_row(HALO), LANES), jnp.float32))
            packed.append(jnp.concatenate(pieces, axis=0))
        corner_a[:, cut] = jnp.where(even_x, packed[1], packed[0])
        corner_b[:, cut] = jnp.where(even_x, packed[0], packed[1])


def z_halos(bp, c, plane, j, top, a, b):
    low, high = sorted_out("gz", a, b)
    bp[c, plane, j, BASE - HALO : BASE, :] = low
    bp[c, plane, j, top : top + HALO, :] = high


def inner_kernel(core, face_za, face_zb, bp, fp, sums_ref, parts_ref):
    _, cx, cz, ny = core.shape
    blocks = ny // LANES
    halo = HALO - 2

    def own(x, _):
        for c in range(3):
            for j in range(blocks):
                cut = slice(j * LANES, (j + 1) * LANES)
                for z in range(0, cz, ROWS):
                    bp[c, x, j, BASE + z : BASE + z + ROWS, :] = core[c, x, z : z + ROWS, cut]
                z_halos(bp, c, x, j, BASE + cz, face_za[c, x, :, cut], face_zb[c, x, :, cut])
        return 0

    lax.fori_loop(0, cx, own, 0)
    rows = row_index()
    zero = jnp.zeros((ROWS, LANES), jnp.float32)
    sums_ref[0] = descent_stages(bp, lambda x: x + 1, cx - 2, halo, cz, blocks, parts_ref, None, zero, rows)
    sums_ref[1] = first_forces(parts_ref, lambda x: x + 1, fp, cx - 4, None, cx, cz, blocks, rows, zero)


def outer_kernel(own, part, face_xa, face_xb, corner_a, corner_b, bp, fp, sums_ref, parts_ref):
    _, cx, blocks, _, _ = own.shape
    cz = face_xa.shape[2]
    halo = HALO - 2
    rows = row_index()
    top = BASE + cz

    def copied(x, _):
        for c in range(3):
            for j in range(blocks):
                for r in range(0, top + BASE, ROWS):
                    bp[c, x + HALO, j, r : r + ROWS, :] = own[c, x, j, r : r + ROWS, :]
                    bp[c, x + 2 * HALO, j, r : r + ROWS, :] = own[c, x + cx - HALO, j, r : r + ROWS, :]
        return 0

    lax.fori_loop(0, HALO, copied, 0)
    for d in range(1, HALO + 1):
        for c in range(3):
            for j in range(blocks):
                cut = slice(j * LANES, (j + 1) * LANES)
                corners = sorted_out("gx", corner_a[:, cut], corner_b[:, cut])
                for side, (plane, k) in enumerate(((HALO - d, HALO - d), (3 * HALO + d - 1, d - 1))):
                    for z in range(0, cz, ROWS):
                        span = slice(z, z + ROWS)
                        value = sorted_out("gx", face_xa[c, k, span, cut], face_xb[c, k, span, cut])[side]
                        bp[c, plane, j, BASE + z : BASE + z + ROWS, :] = value
                    high, low = corner_rows(corners[side], 2 * c * corner_row(HALO), d)
                    bp[c, plane, j, BASE - HALO : BASE, :] = low
                    bp[c, plane, j, top : top + HALO, :] = high
    functional = descent_stages(
        bp,
        lambda x: x + 1 + jnp.where(x >= 6, 2, 0),
        12,
        halo,
        cz,
        blocks,
        parts_ref,
        lambda x: (x == 3) | (x == 8),
        part[0],
        rows,
    )
    slope = first_forces(
        parts_ref,
        lambda x: x + 1 + jnp.where(x >= 4, 2, 0),
        fp,
        8,
        lambda x: x - 2 + jnp.where(x >= 4, cx - 4, 0),
        cx,
        cz,
        blocks,
        rows,
        part[1],
    )
    store_sums(sums_ref, functional, slope, rows)


def second_kernel(
    cells, own_b, inner_f, outer_b, outer_f, sums0, core_b, core_f, bp, sums_ref, parts_ref
):
    _, cx, cz, ny = core_b.shape
    blocks = ny // LANES
    rows = row_index()
    even_x, even_z = is_even("gx"), is_even("gz")
    rate = rate_of(sums0, cells)
    halo = HALO - 2

    def step(x, field, at, force, there):
        for c in range(3):
            for j in range(blocks):
                for r in range(0, cz + 2 * BASE, ROWS):
                    bp[c, x, j, r : r + ROWS, :] = (
                        field[c, at, j, r : r + ROWS, :] + rate * force[c, there, j, r : r + ROWS, :]
                    )

    def inner_step(x, _):
        step(x + 4, own_b, x + 2, inner_f, x)
        return 0

    lax.fori_loop(0, cx - 4, inner_step, 0, unroll=2)
    for k in range(2):
        step(k, outer_b, k + 2, outer_f, k)
        step(k + 2, own_b, k, outer_f, k + 2)
        step(k + cx, own_b, k + cx - 2, outer_f, k + 4)
        step(k + cx + 2, outer_b, k + 12, outer_f, k + 6)
    zero = jnp.zeros((ROWS, LANES), jnp.float32)
    functional = descent_stages(
        bp,
        lambda x: x + 1,
        cx + 2,
        0,
        cz,
        blocks,
        parts_ref,
        lambda x: (x >= 1) & (x <= cx),
        zero,
        rows,
    )

    def plane(x, slope):
        for z in range(0, cz, ROWS):
            r = BASE + z
            for j, force in forces(parts_ref, x + 1, r, blocks):
                cut = slice(j * LANES, (j + 1) * LANES)
                slope = slope + dot(force, force)
                for c in range(3):
                    core_b[c, x, z : z + ROWS, cut] = bp[c, x + halo, j, r : r + ROWS, :]
                    core_f[c, x, z : z + ROWS, cut] = force[c]
        return slope

    slope = lax.fori_loop(0, cx, plane, zero, unroll=4)
    store_sums(sums_ref, functional, slope, rows)


LAYERS = [(0, 0, d) for d in (1, 2, 3, 4)] + [(0, 1, d) for d in (1, 2, 3)] + [(1, 0, 3), (1, 0, 4), (1, 1, 3)]


def faces_kernel(core_b, core_f, friction, face_xa, face_xb, face_za, face_zb):
    _, cx, cz, ny = core_b.shape
    blocks = ny // LANES
    even_x, even_z = is_even("gx"), is_even("gz")

    def plane(x, _):
        for j in range(blocks):
            cut = slice(j * LANES, (j + 1) * LANES)
            for c in range(2):
                low, high = core_f[c, x, 0:HALO, cut], core_f[c, x, cz - HALO : cz, cut]
                face_za[c * cx + x, :, cut] = jnp.where(even_z, high, low)
                face_zb[c * cx + x, :, cut] = jnp.where(even_z, low, high)
                low, high = core_b[c, x, 2:4, cut], core_b[c, x, cz - 4 : cz - 2, cut]
                face_za[2 * cx + x, 2 * c : 2 * c + 2, cut] = jnp.where(even_z, high, low)
                face_zb[2 * cx + x, 2 * c : 2 * c + 2, cut] = jnp.where(even_z, low, high)
            for k, (source, c) in enumerate(((core_f, 0), (core_f, 1), (core_b, 0), (core_b, 1))):
                value = source[c, x, 0:ROWS, cut]
                for z in range(ROWS, cz, ROWS):
                    value = value + source[c, x, z : z + ROWS, cut]
                face_za[3 * cx + 1 + x, k : k + 1, cut] = jnp.sum(value, axis=0, keepdims=True)
        return 0

    lax.fori_loop(0, cx, plane, 0, unroll=4)
    for j in range(blocks):
        cut = slice(j * LANES, (j + 1) * LANES)
        for k, (which, c, d) in enumerate(LAYERS):
            source = (core_f, core_b)[which]
            for z in range(0, cz, ROWS):
                low, high = source[c, d - 1, z : z + ROWS, cut], source[c, cx - d, z : z + ROWS, cut]
                face_xa[k, z : z + ROWS, cut] = jnp.where(even_x, high, low)
                face_xb[k, z : z + ROWS, cut] = jnp.where(even_x, low, high)
        low, high = friction[0:HALO], friction[cz - HALO : cz]
        face_za[3 * cx, :, cut] = jnp.where(even_z, high, low)
        face_zb[3 * cx, :, cut] = jnp.where(even_z, low, high)


def z_rims(face_za, face_zb, bp, rate, cx, cz, c, x, j):
    cut = slice(j * LANES, (j + 1) * LANES)
    top = BASE + cz
    force = sorted_out("gz", face_za[c * cx + x, :, cut], face_zb[c * cx + x, :, cut])
    span = slice(2 * c, 2 * c + 2)
    far = sorted_out("gz", face_za[2 * cx + x, span, cut], face_zb[2 * cx + x, span, cut])
    low = jnp.concatenate([far[0], bp[c, x + 2, j, BASE - 2 : BASE, :]], axis=0)
    high = jnp.concatenate([bp[c, x + 2, j, top : top + 2, :], far[1]], axis=0)
    return low + rate * force[0], high + rate * force[1]


def suffix(value, rows):
    for reach in (1, 2, 4):
        value = value + jnp.where(rows < ROWS - reach, pltpu.roll(value, ROWS - reach, 0), 0.0)
    return value


def prefix(value, rows):
    for reach in (1, 2, 4):
        value = value + jnp.where(rows >= reach, pltpu.roll(value, reach, 0), 0.0)
    return value


def column(ap, c, plane, j, low, own, high, beyond, rows):
    sign = 1.0 if c == 0 else -1.0
    out = 1 - c
    top = BASE + ROWS * len(own)
    ap[out, plane, j, top : top + HALO, :] = high
    value = ap[out, plane, j, top : top + ROWS, :]
    ap[out, plane, j, top : top + ROWS, :] = sign * (beyond - (prefix(value, rows) - value))
    carry = beyond
    for k in reversed(range(len(own))):
        value = suffix(own[k], rows) + carry
        ap[out, plane, j, BASE + k * ROWS : BASE + (k + 1) * ROWS, :] = sign * value
        carry = value[0:1]
    ap[out, plane, j, BASE - HALO : BASE, :] = low
    value = suffix(ap[out, plane, j, 0:BASE, :], rows) + carry
    ap[out, plane, j, 0:BASE, :] = jnp.where(lax.axis_index("gz") > 0, sign * value, 0.0)


def induced(a_ref, bm, planes, halo, at_of, out_of, own_of, flat, cx, cz, blocks, rows):
    x_first, x_all, z_first, z_all = own_place(cx, cz)

    def plane(x, _):
        at, out = at_of(x), out_of(x)
        inside_x = None
        if own_of is not None:
            there = x_first + own_of(x)
            inside_x = (there >= 0) & (there < x_all)
        for r in windows(BASE - halo, BASE + cz + halo):
            height = rows + (r - BASE) + z_first
            inside_z = None if row_mask(rows, r, cz) is None else (height >= 0) & (height < z_all)

            def ld(c, j, dx=0, dz=0):
                return a_ref[c, at + dx, j, r + dz : r + dz + ROWS, :]

            dy = {c: y_diff([ld(c, j) for j in range(blocks)]) for c in ((0,) if flat else (0, 2))}
            for j in range(blocks):
                curl_x = ld(1, j, dz=-1) - ld(1, j, dz=1)
                curl_y = ld(0, j, dz=1) - ld(0, j, dz=-1)
                curl_z = ld(1, j, dx=1) - ld(1, j, dx=-1) - dy[0][j]
                if not flat:
                    curl_x = curl_x + dy[2][j]
                    curl_y = curl_y - (ld(2, j, dx=1) - ld(2, j, dx=-1))
                for c, value in enumerate((curl_x, curl_y, curl_z)):
                    bm[c, out, j, r : r + ROWS, :] = masked(value, inside_z, inside_x)
        return 0

    lax.fori_loop(0, planes, plane, 0, unroll=4)


def pushed(bm, x, r, rub, blocks):
    def ld(c, j, dx=0, dz=0):
        return bm[c, x + dx, j, r + dz : r + dz + ROWS, :]

    dy = [y_diff([ld(c, j) for j in range(blocks)]) if c != 1 else None for c in range(3)]
    weight = rub[r : r + ROWS]
    for j in range(blocks):
        field = [ld(c, j) for c in range(3)]
        current = (
            dy[2][j] - (ld(1, j, dz=1) - ld(1, j, dz=-1)),
            (ld(0, j, dz=1) - ld(0, j, dz=-1)) - (ld(2, j, dx=1) - ld(2, j, dx=-1)),
            (ld(1, j, dx=1) - ld(1, j, dx=-1)) - dy[0][j],
        )
        square = dot(field, field)
        scale = weight * (0.0625 / jnp.maximum(0.25 * square, 1.0))
        both = dot(current, field)
        yield j, [scale * (field[c] * both - current[c] * square) for c in range(3)]


def first_push(ap, bm, an, rub, planes, at_of, out_of, cz, blocks):
    def plane(x, _):
        halo = HALO - 2
        for r in windows(BASE - halo, BASE + cz + halo):
            for j, change in pushed(bm, at_of(x), r, rub, blocks):
                for c in range(2):
                    an[c, out_of(x), j, r : r + ROWS, :] = ap[c, x + 2, j, r : r + ROWS, :] + change[c]
                an[2, out_of(x), j, r : r + ROWS, :] = change[2]
        return 0

    lax.fori_loop(0, planes, plane, 0, unroll=2)


def last_push(an, bm, out, rub, planes, at_of, cz, blocks):
    def plane(x, _):
        for z in range(0, cz, ROWS):
            for j, change in pushed(bm, at_of(x), BASE + z, rub, blocks):
                cut = slice(j * LANES, (j + 1) * LANES)
                for c in range(3):
                    out[c, x, z : z + ROWS, cut] = an[c, x + 2, j, BASE + z : BASE + z + ROWS, :] + change[c]
        return 0

    lax.fori_loop(0, planes, plane, 0, unroll=2)


def middle_kernel(
    cells, core_b, core_f, bp, sums0, friction, face_za, face_zb, above, out, ap, bm, an, bn, inner, rub, relaxed, sent
):
    _, cx, cz, ny = core_b.shape
    blocks = ny // LANES
    rows = row_index()
    _, _, z_first, z_all = own_place(cx, cz)
    rate = rate_of(sums0, cells)
    top = BASE + cz

    rub[BASE:top] = friction[...]
    low, high = sorted_out("gz", face_za[3 * cx, :, :LANES], face_zb[3 * cx, :, :LANES])
    rub[BASE - HALO : BASE] = low
    rub[top : top + HALO] = high
    for r in range(0, cz + 2 * BASE, ROWS):
        height = rows + (r - BASE) + z_first
        inside = (height >= 0) & (height < z_all)
        rub[r : r + ROWS] = jnp.where(inside, time_step / rub[r : r + ROWS], 0.0)

    def own_plane(x, _):
        for j in range(blocks):
            cut = slice(j * LANES, (j + 1) * LANES)
            for c in range(3):
                own = [
                    core_b[c, x, z : z + ROWS, cut] + rate * core_f[c, x, z : z + ROWS, cut]
                    for z in range(0, cz, ROWS)
                ]
                for z in range(0, cz, ROWS):
                    relaxed[c, x, z : z + ROWS, cut] = own[z // ROWS]
                if c == 2:
                    continue
                low, high = z_rims(face_za, face_zb, bp, rate, cx, cz, c, x, j)
                column(ap, c, x, j, low, own, high, above[x, c : c + 1, cut], rows)
        return 0

    lax.fori_loop(0, cx, own_plane, 0, unroll=2)
    matrix = dealing(ny, True)
    relaxed[...] = dealt(relaxed[...].reshape(3 * cx * cz, ny), matrix).reshape(relaxed.shape)
    copy = pltpu.make_async_copy(relaxed, out, sent)
    copy.start()
    induced(ap, bm, cx - 2, HALO - 1, lambda x: x + 1, lambda x: x, None, True, cx, cz, blocks, rows)
    first_push(ap, bm, an, rub, cx - 4, lambda x: x + 1, lambda x: x, cz, blocks)
    induced(an, bn, cx - 6, 1, lambda x: x + 1, lambda x: x, None, False, cx, cz, blocks, rows)
    last_push(an, bn, inner, rub, cx - 8, lambda x: x + 1, cz, blocks)
    inner[...] = dealt(inner[...].reshape(-1, ny), matrix).reshape(inner.shape)
    copy.wait()


def ends_kernel(
    cells, bp, sums0, face_xa, face_xb, corner_a, corner_b, own_ap, own_bm, own_an, own_bn, inner, rub, potential, ap, bm, an, rim, sent
):
    _, cx, cz, ny = potential.shape
    blocks = ny // LANES
    rows = row_index()
    copies = [pltpu.make_async_copy(inner, potential.at[:, HALO : cx - HALO], sent.at[0])]
    copies[0].start()
    rate = rate_of(sums0, cells)

    for d in range(1, HALO + 1):
        for c in range(2):
            if (0, c, d) not in LAYERS:
                continue
            for j in range(blocks):
                cut = slice(j * LANES, (j + 1) * LANES)

                def layer(which, span):
                    k = LAYERS.index((which, c, d))
                    return sorted_out("gx", face_xa[k, span, cut], face_xb[k, span, cut])

                own = ([], [])
                for z in range(0, cz, ROWS):
                    force = layer(0, slice(z, z + ROWS))
                    if d <= 2:
                        field = [bp[c, at, j, BASE + z : BASE + z + ROWS, :] for at in (2 - d, cx + 1 + d)]
                    else:
                        field = layer(1, slice(z, z + ROWS))
                    for side in range(2):
                        own[side].append(field[side] + rate * force[side])
                corners = sorted_out("gx", corner_a[c, :, cut], corner_b[c, :, cut])
                for side, plane in enumerate((HALO - d, 2 * HALO + d - 1)):
                    corner = corners[side]
                    high, low = corner_rows(corner, HALO, d)
                    column(ap, c, plane, j, low, own[side], high, corner[d - 1 : d], rows)

    def borrow(into, source, low, high):
        for k in range(2):
            for c in range(source.shape[0]):
                into[c, 4 + k] = source[c, low + k]
                into[c, 6 + k] = source[c, high + k]

    def at_of(x):
        return x + 1 + jnp.where(x >= 4, 2, 0)

    def out_of(x):
        return x + jnp.where(x >= 4, 4, 0)

    borrow(ap, own_ap, 0, cx - 2)
    induced(ap, bm, 8, HALO - 1, at_of, out_of, lambda x: x - 3 + jnp.where(x >= 4, cx - 2, 0), True, cx, cz, blocks, rows)
    borrow(bm, own_bm, 0, cx - 4)
    first_push(ap, bm, an, rub, 8, at_of, out_of, cz, blocks)
    borrow(an, own_an, 0, cx - 6)
    induced(an, bm, 8, 1, at_of, out_of, lambda x: x - 1 + jnp.where(x >= 4, cx - 6, 0), False, cx, cz, blocks, rows)
    borrow(bm, own_bn, 0, cx - 8)
    last_push(an, bm, rim, rub, 8, at_of, cz, blocks)
    rim[...] = dealt(rim[...].reshape(-1, ny), dealing(ny, True)).reshape(rim.shape)
    copies.append(pltpu.make_async_copy(rim.at[:, :HALO], potential.at[:, :HALO], sent.at[1]))
    copies.append(pltpu.make_async_copy(rim.at[:, HALO:], potential.at[:, cx - HALO :], sent.at[2]))
    for copy in copies[1:]:
        copy.start()
    for copy in copies:
        copy.wait()


def pack_kernel(cells, count, *refs):
    columns, (face_za, face_zb, bp, sums0, above, corner_a, corner_b) = refs[:count], refs[count:]
    cx, _, ny = above.shape
    cz = bp.shape[3] - 2 * BASE
    even_x = is_even("gx")
    place = lax.axis_index("gz")
    rate = rate_of(sums0, cells)

    def total(x, _):
        column = jnp.zeros(columns[0].shape[1:], jnp.float32)
        for level, part in enumerate(columns):
            column = column + jnp.where((place >> level) % 2 == 0, part[x], 0.0)
        above[x] = column[2:4] + rate * column[0:2]
        return 0

    lax.fori_loop(0, cx, total, 0, unroll=4)
    for c in range(2):
        for j in range(ny // LANES):
            cut = slice(j * LANES, (j + 1) * LANES)
            packed = []
            for edge in (lambda d: d - 1, lambda d: cx - d):
                rims = [z_rims(face_za, face_zb, bp, rate, cx, cz, c, edge(d), j) for d in range(1, HALO)]
                pieces = [above[edge(d), c : c + 1, cut] for d in range(1, HALO + 1)]
                pieces += [high[: HALO - d] for d, (_, high) in enumerate(rims, 1)]
                pieces += [low[d:] for d, (low, _) in enumerate(rims, 1)]
                packed.append(jnp.concatenate(pieces, axis=0))
            corner_a[c, :, cut] = jnp.where(even_x, packed[1], packed[0])
            corner_b[c, :, cut] = jnp.where(even_x, packed[0], packed[1])


def call(kernel, outs, *args, scratch=(), cost=0, limit=8, outside_out=0):
    shapes = [jax.ShapeDtypeStruct(shape, jnp.float32) for shape in outs]
    return pl.pallas_call(
        kernel,
        out_shape=shapes,
        in_specs=[pl.BlockSpec(memory_space=pltpu.VMEM)] * len(args),
        out_specs=[pl.BlockSpec(memory_space=pl.ANY if k < outside_out else pltpu.VMEM) for k in range(len(outs))],
        scratch_shapes=[pltpu.VMEM(item, jnp.float32) if isinstance(item, tuple) else item for item in scratch],
        compiler_params=pltpu.CompilerParams(vmem_limit_bytes=limit * 1024 * 1024),
        cost_estimate=pl.CostEstimate(flops=cost, bytes_accessed=cost // 10, transcendentals=0),
    )(*args)


def body(magnetic, friction):
    _, cx, cz, ny = magnetic.shape
    blocks = ny // LANES
    height = cz + 2 * BASE
    count_z, count_x = lax.axis_size("gz"), lax.axis_size("gx")
    devices = count_z * count_x
    cells = cx * cz * ny * devices
    work = cx * cz * ny * 200

    def planes_of(components, planes):
        return (components, planes, blocks, height, LANES)

    def padded(components, layers):
        return planes_of(components, cx + 2 * layers)

    tiles = (devices, ROWS, LANES)
    core = (3, cx, cz, ny)
    rubbed = jnp.broadcast_to(friction[:, None], (cz, LANES))

    magnetic, *faces = call(
        entry_kernel,
        [core, *[(3, HALO, cz, ny)] * 2, *[(3, cx, HALO, ny)] * 2],
        magnetic,
        cost=work,
        limit=8,
    )
    faces_x = swapped(faces[:2], "gx")
    faces_z = swapped(faces[2:], "gz")
    corners = call(
        corners_kernel,
        [(-(-6 * corner_row(HALO) // ROWS) * ROWS, ny)] * 2,
        *faces_z,
        cost=work // 50,
    )
    corners = swapped(corners, "gx")
    own_b, inner_f, part = call(
        inner_kernel,
        [padded(3, 0), padded(3, -2), (2, ROWS, LANES)],
        magnetic,
        *faces_z,
        scratch=[padded(7, -1)],
        cost=work,
        limit=9,
    )
    outer_b, outer_f, sums = call(
        outer_kernel,
        [planes_of(3, 4 * HALO), planes_of(3, 8), tiles],
        own_b,
        part,
        *faces_x,
        *corners,
        scratch=[planes_of(7, 12)],
        cost=work,
        limit=9,
    )
    core_b, core_f, bp, sums = call(
        functools.partial(second_kernel, cells),
        [core, core, padded(3, HALO - 2), tiles],
        own_b,
        inner_f,
        outer_b,
        outer_f,
        shared(sums),
        scratch=[padded(7, 1)],
        cost=work,
        limit=11,
    )
    faces = call(
        faces_kernel,
        [*[(len(LAYERS), cz, ny)] * 2, (4 * cx + 1, HALO, ny), (3 * cx + 1, HALO, ny)],
        core_b,
        core_f,
        rubbed,
        cost=work,
    )
    faces_z = swapped(faces[2:], "gz")
    faces_x = swapped(faces[:2], "gx")
    sums = shared(sums)
    columns = [faces_z[0][3 * cx + 1 :]]
    group = faces[2][3 * cx + 1 :] + columns[0]
    stride = 2
    while stride < count_z:
        columns.append(lax.ppermute(group, "gz", [(i, i ^ stride) for i in range(count_z)]))
        stride *= 2
        if stride < count_z:
            group = group + columns[-1]
    above, *corners = call(
        functools.partial(pack_kernel, cells, len(columns)),
        [(cx, 2, ny), *[(2, HALO + 2 * corner_row(HALO), ny)] * 2],
        *columns,
        *faces_z,
        bp,
        sums,
        cost=work // 50,
    )
    corners = swapped(corners, "gx")
    relaxed, *shares = call(
        functools.partial(middle_kernel, cells),
        [core, padded(2, 0), padded(3, -1), padded(3, -2), padded(3, -3), (3, cx - 2 * HALO, cz, ny), (height, LANES)],
        core_b,
        core_f,
        bp,
        sums,
        rubbed,
        *faces_z,
        above,
        scratch=[core, pltpu.SemaphoreType.DMA],
        outside_out=1,
        cost=work,
        limit=8,
    )
    (potential,) = call(
        functools.partial(ends_kernel, cells),
        [core],
        bp,
        sums,
        *faces_x,
        *corners,
        *shares,
        scratch=[planes_of(2, 12), planes_of(3, 12), planes_of(3, 12), (3, 2 * HALO, cz, ny), pltpu.SemaphoreType.DMA((3,))],
        outside_out=1,
        cost=work,
        limit=14,
    )
    return relaxed, potential


def solution(mesh):
    return jax.shard_map(
        body,
        mesh=mesh,
        in_specs=(P(None, "gx", "gz", "runs"), P("gz")),
        out_specs=(P(None, "gx", "gz", "runs"), P(None, "gx", "gz", "runs")),
        check_vma=False,
    )
```

```python
import functools

import jax
import jax.numpy as jnp
from jax import lax
from jax.experimental import pallas as pl
from jax.experimental.pallas import tpu as pltpu
from jax.sharding import PartitionSpec as P

DESCENTS = 2
RELAX = 2

step_scale = 0.5
time_step = 0.2

LANES = 128
ROWS = 8
HALO = 4
NEAR = HALO // 2
BASE = 8


AXES = ("runs", "gz", "gx")


def pairings(axis):
    sizes = [lax.axis_size(name) for name in AXES]
    along = AXES.index(axis)
    places = [(r, z, x) for r in range(sizes[0]) for z in range(sizes[1]) for x in range(sizes[2])]

    def flat(place):
        return (place[0] * sizes[1] + place[1]) * sizes[2] + place[2]

    def moved(place, name, to):
        return tuple(to if name == other else at for other, at in zip(AXES, place))

    first, second = [], []
    for place in places:
        at = place[along]
        if at ^ 1 < sizes[along]:
            first.append((flat(place), flat(moved(place, axis, at ^ 1))))
        to = at + 1 if at % 2 else at - 1
        if 0 <= to < sizes[along]:
            second.append((flat(place), flat(moved(place, axis, to))))
        else:
            idle = "gz" if axis == "gx" else "runs"
            at = place[AXES.index(idle)] ^ 1
            if at < sizes[AXES.index(idle)]:
                second.append((flat(place), flat(moved(place, idle, at))))
    return first, second


def is_even(axis):
    return lax.axis_index(axis) % 2 == 0


def swapped(pair, axis):
    first, second = pairings(axis)
    return lax.ppermute(pair[0], AXES, first), lax.ppermute(pair[1], AXES, second)


def sorted_out(axis, first, second):
    at = lax.axis_index(axis)
    even = at % 2 == 0
    low = jnp.where(at > 0, jnp.where(even, second, first), 0.0)
    high = jnp.where(at < lax.axis_size(axis) - 1, jnp.where(even, first, second), 0.0)
    return low, high


def shared(tile_copies):
    return lax.all_to_all(tile_copies, ("gz", "gx"), 0, 0)


def y_diff(blocks):
    wide = [pltpu.roll(blocks[-1], 1, 1), *blocks, pltpu.roll(blocks[0], LANES - 1, 1)]
    return [wide[j + 2] - wide[j] for j in range(len(blocks))]


def dealing(ny, back):
    blocks = ny // LANES
    source = lax.broadcasted_iota(jnp.int32, (ny, ny), 0)
    target = lax.broadcasted_iota(jnp.int32, (ny, ny), 1)
    if back:
        source, target = target, source
    return ((target % LANES) * blocks + target // LANES == source).astype(jnp.bfloat16)


def dealt(value, matrix):
    rows = value.shape[0]
    high = value.astype(jnp.bfloat16)
    rest = (value - high.astype(jnp.float32)).astype(jnp.bfloat16)
    both = jnp.dot(jnp.concatenate([high, rest], axis=0), matrix, preferred_element_type=jnp.float32)
    return both[:rows] + both[rows:]


def dot(a, b):
    return a[0] * b[0] + a[1] * b[1] + a[2] * b[2]


def row_index():
    return lax.broadcasted_iota(jnp.int32, (ROWS, LANES), 0)


def windows(low, high):
    return [low + ROWS * w for w in range(-(-(high - low) // ROWS))]


def own_place(cx, cz):
    return (
        lax.axis_index("gx") * cx,
        lax.axis_size("gx") * cx,
        lax.axis_index("gz") * cz,
        lax.axis_size("gz") * cz,
    )


def row_mask(rows, r, cz):
    height = rows + (r - BASE)
    return None if BASE <= r and r + ROWS <= BASE + cz else (height >= 0) & (height < cz)


def masked(value, *conditions):
    for condition in conditions:
        if condition is not None:
            value = jnp.where(condition, value, 0.0)
    return value


def descent_stages(bp, plane_of, planes, halo, cz, blocks, parts_ref, counted, functional, rows):
    def plane(x, functional):
        at = plane_of(x)
        for r in windows(BASE - halo - 1, BASE + cz + halo + 1):
            own = row_mask(rows, r, cz)

            def ld(c, j, dx=0, dz=0):
                return bp[c, at + dx, j, r + dz : r + dz + ROWS, :]

            dy = [y_diff([ld(c, j) for j in range(blocks)]) for c in range(3)]
            for j in range(blocks):
                field = [ld(c, j) for c in range(3)]
                dx = [ld(c, j, dx=1) - ld(c, j, dx=-1) for c in range(3)]
                dz = [ld(c, j, dz=1) - ld(c, j, dz=-1) for c in range(3)]
                current = (dy[2][j] - dz[1], dz[0] - dx[2], dx[1] - dy[0][j])
                spread = dx[0] + dy[1][j] + dz[2]
                square = dot(field, field)
                inverse = 1.0 / jnp.maximum(square, 1.0)
                capped = jnp.minimum(square, 1.0)
                along = dot(current, field)
                ratio = along * inverse
                bulk = dot(current, current)
                spread_square = spread * spread
                pull = (bulk + spread_square) * inverse * (1.0 - capped) + ratio * ratio
                density = bulk * capped - ratio * along + spread_square
                functional = functional + masked(density, own, None if counted is None else counted(x))
                twist = [ratio * field[c] - capped * current[c] for c in range(3)]
                local = [ratio * current[c] - pull * field[c] for c in range(3)]
                for k, value in enumerate([*twist, capped * spread, *local]):
                    parts_ref[k, x, j, r : r + ROWS, :] = value
        return functional

    return lax.fori_loop(0, planes, plane, functional, unroll=2)


def forces(parts_ref, at, r, blocks):
    def ld(k, j, dx=0, dz=0):
        return parts_ref[k, at + dx, j, r + dz : r + dz + ROWS, :]

    dy = {k: y_diff([ld(k, j) for j in range(blocks)]) for k in (0, 2, 3)}
    for j in range(blocks):

        def dx(k):
            return ld(k, j, dx=1) - ld(k, j, dx=-1)

        def dz(k):
            return ld(k, j, dz=1) - ld(k, j, dz=-1)

        yield j, [
            (dy[2][j] - dz(1)) + (dx(3) + ld(4, j)),
            (dz(0) - dx(2)) + (dy[3][j] + ld(5, j)),
            (dx(1) - dy[0][j]) + (dz(3) + ld(6, j)),
        ]


def store_sums(sums_ref, functional, slope, rows):
    functional = jnp.sum(functional, axis=0, keepdims=True)
    slope = jnp.sum(slope, axis=0, keepdims=True)
    tile = jnp.where(rows == 0, functional, jnp.where(rows == 1, slope, 0.0))
    for k in range(sums_ref.shape[0]):
        sums_ref[k] = tile


def rate_of(sums_ref, cells):
    total = sums_ref[0]
    for k in range(1, sums_ref.shape[0]):
        total = total + sums_ref[k]
    functional = jnp.sum(total[0:1], axis=1, keepdims=True) * 0.25 / cells
    slope = jnp.sum(total[1:2], axis=1, keepdims=True) * 0.0625 / cells
    return (0.25 * step_scale) * functional / (slope + 1e-6)


def entry_kernel(magnetic, core, face_xa, face_xb, face_za, face_zb):
    _, cx, cz, ny = magnetic.shape
    even_x, even_z = is_even("gx"), is_even("gz")
    matrix = dealing(ny, False)
    for c in range(3):
        value = dealt(magnetic[c].reshape(cx * cz, ny), matrix).reshape(cx, cz, ny)
        core[c] = value
        low, high = value[:NEAR], value[cx - NEAR :]
        face_xa[c] = jnp.where(even_x, high, low)
        face_xb[c] = jnp.where(even_x, low, high)
        low, high = value[:, :HALO], value[:, cz - HALO :]
        face_za[c] = jnp.where(even_z, high, low)
        face_zb[c] = jnp.where(even_z, low, high)


def first_forces(parts_ref, parts_of, fp, planes, cz, blocks, rows, slope):
    halo = HALO - 2
    z_first, z_all = lax.axis_index("gz") * cz, lax.axis_size("gz") * cz

    def plane(x, slope):
        for r in windows(BASE - halo, BASE + cz + halo):
            own = row_mask(rows, r, cz)
            height = rows + (r - BASE) + z_first
            inside = None if own is None else (height >= 0) & (height < z_all)
            for j, force in forces(parts_ref, parts_of(x), r, blocks):
                slope = slope + masked(dot(force, force), own)
                for c in range(3):
                    fp[c, x, j, r : r + ROWS, :] = masked(force[c], inside)
        return slope

    return lax.fori_loop(0, planes, plane, slope, unroll=4)


def z_halos(bp, c, plane, j, top, a, b):
    low, high = sorted_out("gz", a, b)
    bp[c, plane, j, BASE - HALO : BASE, :] = low
    bp[c, plane, j, top : top + HALO, :] = high


def corner_row(d):
    return sum(HALO - k for k in range(1, d))


def corner_rows(corner, first, d, reach):
    none = jnp.zeros((d, LANES), jnp.float32)
    if d == HALO:
        return none, none
    high, low = [corner[at : at + HALO - d] for at in (first + corner_row(d), first + corner_row(reach + 1) + corner_row(d))]
    return jnp.concatenate([high, none], 0), jnp.concatenate([none, low], 0)


def corners_kernel(face_za, face_zb, corner_a, corner_b):
    _, cx, _, ny = face_za.shape
    even_x = is_even("gx")
    for j in range(ny // LANES):
        cut = slice(j * LANES, (j + 1) * LANES)
        packed = []
        for edge in (lambda d: d - 1, lambda d: cx - d):
            pieces = []
            for c in range(3):
                rims = [sorted_out("gz", face_za[c, edge(d), :, cut], face_zb[c, edge(d), :, cut]) for d in range(1, NEAR + 1)]
                pieces += [high[: HALO - d] for d, (_, high) in enumerate(rims, 1)]
                pieces += [low[d:] for d, (low, _) in enumerate(rims, 1)]
            pieces.append(jnp.zeros((corner_a.shape[0] - 6 * corner_row(NEAR + 1), LANES), jnp.float32))
            packed.append(jnp.concatenate(pieces, axis=0))
        corner_a[:, cut] = jnp.where(even_x, packed[1], packed[0])
        corner_b[:, cut] = jnp.where(even_x, packed[0], packed[1])


def z_halos(bp, c, plane, j, top, a, b):
    low, high = sorted_out("gz", a, b)
    bp[c, plane, j, BASE - HALO : BASE, :] = low
    bp[c, plane, j, top : top + HALO, :] = high


def inner_kernel(core, face_za, face_zb, bp, fp, sums_ref, parts_ref):
    _, cx, cz, ny = core.shape
    blocks = ny // LANES
    halo = HALO - 2

    def own(x, _):
        for c in range(3):
            for j in range(blocks):
                cut = slice(j * LANES, (j + 1) * LANES)
                for z in range(0, cz, ROWS):
                    bp[c, x, j, BASE + z : BASE + z + ROWS, :] = core[c, x, z : z + ROWS, cut]
                z_halos(bp, c, x, j, BASE + cz, face_za[c, x, :, cut], face_zb[c, x, :, cut])
        return 0

    lax.fori_loop(0, cx, own, 0)
    rows = row_index()
    zero = jnp.zeros((ROWS, LANES), jnp.float32)
    sums_ref[0] = descent_stages(bp, lambda x: x + 1, cx - 2, halo, cz, blocks, parts_ref, None, zero, rows)
    sums_ref[1] = first_forces(parts_ref, lambda x: x + 1, fp, cx - 4, cz, blocks, rows, zero)


def outer_kernel(own, part, face_xa, face_xb, corner_a, corner_b, bp, fp, sums_ref, rim_a, rim_b, parts_ref):
    _, cx, blocks, _, _ = own.shape
    cz = face_xa.shape[2]
    halo = HALO - 2
    rows = row_index()
    top = BASE + cz
    end = NEAR + HALO

    def copied(x, _):
        for c in range(3):
            for j in range(blocks):
                for r in range(0, top + BASE, ROWS):
                    bp[c, x + NEAR, j, r : r + ROWS, :] = own[c, x, j, r : r + ROWS, :]
                    bp[c, x + end, j, r : r + ROWS, :] = own[c, x + cx - HALO, j, r : r + ROWS, :]
        return 0

    lax.fori_loop(0, HALO, copied, 0)
    for d in range(1, NEAR + 1):
        for c in range(3):
            for j in range(blocks):
                cut = slice(j * LANES, (j + 1) * LANES)
                corners = sorted_out("gx", corner_a[:, cut], corner_b[:, cut])
                for side, (plane, k) in enumerate(((NEAR - d, NEAR - d), (end + HALO + d - 1, d - 1))):
                    for z in range(0, cz, ROWS):
                        span = slice(z, z + ROWS)
                        value = sorted_out("gx", face_xa[c, k, span, cut], face_xb[c, k, span, cut])[side]
                        bp[c, plane, j, BASE + z : BASE + z + ROWS, :] = value
                    high, low = corner_rows(corners[side], 2 * c * corner_row(NEAR + 1), d, NEAR)
                    bp[c, plane, j, BASE - HALO : BASE, :] = low
                    bp[c, plane, j, top : top + HALO, :] = high
    functional = descent_stages(
        bp,
        lambda x: x + 1 + jnp.where(x >= 4, 2, 0),
        8,
        halo,
        cz,
        blocks,
        parts_ref,
        lambda x: (x == 1) | (x == 6),
        part[0],
        rows,
    )
    slope = first_forces(parts_ref, lambda x: x + 1 + jnp.where(x >= 2, 2, 0), fp, 4, cz, blocks, rows, part[1])
    store_sums(sums_ref, functional, slope, rows)
    even = is_even("gx")
    for c in range(3):
        for j in range(blocks):
            cut = slice(j * LANES, (j + 1) * LANES)

            def send(at, count, low, high):
                rim_a[at : at + count, cut] = jnp.where(even, high, low)
                rim_b[at : at + count, cut] = jnp.where(even, low, high)

            for d in range(1, NEAR + 1):
                for z in range(0, cz, ROWS):
                    span = slice(BASE + z, BASE + z + ROWS)
                    send((c * NEAR + d - 1) * cz + z, ROWS, fp[c, d - 1, j, span, :], fp[c, 2 * NEAR - d, j, span, :])
            for k, r in enumerate((BASE - 1, top)):
                row = slice(r, r + 1)
                send(3 * NEAR * cz + 2 * c + k, 1, fp[c, 0, j, row, :], fp[c, 2 * NEAR - 1, j, row, :])


def second_kernel(
    cells, own_b, inner_f, outer_b, outer_f, rim_a, rim_b, sums0, core_b, core_f, bp, sums_ref, parts_ref
):
    _, cx, cz, ny = core_b.shape
    blocks = ny // LANES
    rows = row_index()
    even_x, even_z = is_even("gx"), is_even("gz")
    rate = rate_of(sums0, cells)
    halo = HALO - 2

    def step(x, field, at, force, there):
        for c in range(3):
            for j in range(blocks):
                for r in range(0, cz + 2 * BASE, ROWS):
                    bp[c, x, j, r : r + ROWS, :] = (
                        field[c, at, j, r : r + ROWS, :] + rate * force[c, there, j, r : r + ROWS, :]
                    )

    def inner_step(x, _):
        step(x + 4, own_b, x + 2, inner_f, x)
        return 0

    lax.fori_loop(0, cx - 4, inner_step, 0, unroll=2)
    for k in range(NEAR):
        step(k + halo, own_b, k, outer_f, k)
        step(k + cx, own_b, k + cx - NEAR, outer_f, k + NEAR)
    top = BASE + cz
    for d in range(1, NEAR + 1):
        for c in range(3):
            for j in range(blocks):
                cut = slice(j * LANES, (j + 1) * LANES)
                for side, (x, at) in enumerate(((halo - d, NEAR - d), (halo + cx + d - 1, 2 * HALO + NEAR + d - 1))):
                    for r in (0, top):
                        bp[c, x, j, r : r + ROWS, :] = outer_b[c, at, j, r : r + ROWS, :]
                    for z in range(0, cz, ROWS):
                        r, k = BASE + z, (c * NEAR + d - 1) * cz + z
                        force = sorted_out("gx", rim_a[k : k + ROWS, cut], rim_b[k : k + ROWS, cut])[side]
                        bp[c, x, j, r : r + ROWS, :] = outer_b[c, at, j, r : r + ROWS, :] + rate * force
                    if d > 1:
                        continue
                    for n, r in enumerate((BASE - 1, top)):
                        k = 3 * NEAR * cz + 2 * c + n
                        force = sorted_out("gx", rim_a[k : k + 1, cut], rim_b[k : k + 1, cut])[side]
                        bp[c, x, j, r : r + 1, :] = outer_b[c, at, j, r : r + 1, :] + rate * force
    zero = jnp.zeros((ROWS, LANES), jnp.float32)
    functional = descent_stages(
        bp,
        lambda x: x + 1,
        cx + 2,
        0,
        cz,
        blocks,
        parts_ref,
        lambda x: (x >= 1) & (x <= cx),
        zero,
        rows,
    )

    def plane(x, slope):
        for z in range(0, cz, ROWS):
            r = BASE + z
            for j, force in forces(parts_ref, x + 1, r, blocks):
                cut = slice(j * LANES, (j + 1) * LANES)
                slope = slope + dot(force, force)
                for c in range(3):
                    core_b[c, x, z : z + ROWS, cut] = bp[c, x + halo, j, r : r + ROWS, :]
                    core_f[c, x, z : z + ROWS, cut] = force[c]
        return slope

    slope = lax.fori_loop(0, cx, plane, zero, unroll=4)
    store_sums(sums_ref, functional, slope, rows)


LAYERS = [(0, 0, d) for d in (1, 2, 3, 4)] + [(0, 1, d) for d in (1, 2, 3)] + [(1, 0, 3), (1, 0, 4), (1, 1, 3)]


def faces_kernel(core_b, core_f, friction, face_xa, face_xb, face_za, face_zb):
    _, cx, cz, ny = core_b.shape
    blocks = ny // LANES
    even_x, even_z = is_even("gx"), is_even("gz")

    def plane(x, _):
        for j in range(blocks):
            cut = slice(j * LANES, (j + 1) * LANES)
            for c in range(2):
                low, high = core_f[c, x, 0:HALO, cut], core_f[c, x, cz - HALO : cz, cut]
                face_za[c * cx + x, :, cut] = jnp.where(even_z, high, low)
                face_zb[c * cx + x, :, cut] = jnp.where(even_z, low, high)
                low, high = core_b[c, x, 2:4, cut], core_b[c, x, cz - 4 : cz - 2, cut]
                face_za[2 * cx + x, 2 * c : 2 * c + 2, cut] = jnp.where(even_z, high, low)
                face_zb[2 * cx + x, 2 * c : 2 * c + 2, cut] = jnp.where(even_z, low, high)
            for k, (source, c) in enumerate(((core_f, 0), (core_f, 1), (core_b, 0), (core_b, 1))):
                value = source[c, x, 0:ROWS, cut]
                for z in range(ROWS, cz, ROWS):
                    value = value + source[c, x, z : z + ROWS, cut]
                face_za[3 * cx + 1 + x, k : k + 1, cut] = jnp.sum(value, axis=0, keepdims=True)
        return 0

    lax.fori_loop(0, cx, plane, 0, unroll=4)
    for j in range(blocks):
        cut = slice(j * LANES, (j + 1) * LANES)
        for k, (which, c, d) in enumerate(LAYERS):
            source = (core_f, core_b)[which]
            for z in range(0, cz, ROWS):
                low, high = source[c, d - 1, z : z + ROWS, cut], source[c, cx - d, z : z + ROWS, cut]
                face_xa[k, z : z + ROWS, cut] = jnp.where(even_x, high, low)
                face_xb[k, z : z + ROWS, cut] = jnp.where(even_x, low, high)
        low, high = friction[0:HALO], friction[cz - HALO : cz]
        face_za[3 * cx, :, cut] = jnp.where(even_z, high, low)
        face_zb[3 * cx, :, cut] = jnp.where(even_z, low, high)


def z_rims(face_za, face_zb, bp, rate, cx, cz, c, x, j):
    cut = slice(j * LANES, (j + 1) * LANES)
    top = BASE + cz
    force = sorted_out("gz", face_za[c * cx + x, :, cut], face_zb[c * cx + x, :, cut])
    span = slice(2 * c, 2 * c + 2)
    far = sorted_out("gz", face_za[2 * cx + x, span, cut], face_zb[2 * cx + x, span, cut])
    low = jnp.concatenate([far[0], bp[c, x + 2, j, BASE - 2 : BASE, :]], axis=0)
    high = jnp.concatenate([bp[c, x + 2, j, top : top + 2, :], far[1]], axis=0)
    return low + rate * force[0], high + rate * force[1]


def suffix(value, rows):
    for reach in (1, 2, 4):
        value = value + jnp.where(rows < ROWS - reach, pltpu.roll(value, ROWS - reach, 0), 0.0)
    return value


def prefix(value, rows):
    for reach in (1, 2, 4):
        value = value + jnp.where(rows >= reach, pltpu.roll(value, reach, 0), 0.0)
    return value


def column(ap, c, plane, j, low, own, high, beyond, rows):
    sign = 1.0 if c == 0 else -1.0
    out = 1 - c
    top = BASE + ROWS * len(own)
    ap[out, plane, j, top : top + HALO, :] = high
    value = ap[out, plane, j, top : top + ROWS, :]
    ap[out, plane, j, top : top + ROWS, :] = sign * (beyond - (prefix(value, rows) - value))
    carry = beyond
    for k in reversed(range(len(own))):
        value = suffix(own[k], rows) + carry
        ap[out, plane, j, BASE + k * ROWS : BASE + (k + 1) * ROWS, :] = sign * value
        carry = value[0:1]
    ap[out, plane, j, BASE - HALO : BASE, :] = low
    value = suffix(ap[out, plane, j, 0:BASE, :], rows) + carry
    ap[out, plane, j, 0:BASE, :] = jnp.where(lax.axis_index("gz") > 0, sign * value, 0.0)


def induced(a_ref, bm, planes, halo, at_of, out_of, own_of, flat, cx, cz, blocks, rows):
    x_first, x_all, z_first, z_all = own_place(cx, cz)

    def plane(x, _):
        at, out = at_of(x), out_of(x)
        inside_x = None
        if own_of is not None:
            there = x_first + own_of(x)
            inside_x = (there >= 0) & (there < x_all)
        for r in windows(BASE - halo, BASE + cz + halo):
            height = rows + (r - BASE) + z_first
            inside_z = None if row_mask(rows, r, cz) is None else (height >= 0) & (height < z_all)

            def ld(c, j, dx=0, dz=0):
                return a_ref[c, at + dx, j, r + dz : r + dz + ROWS, :]

            dy = {c: y_diff([ld(c, j) for j in range(blocks)]) for c in ((0,) if flat else (0, 2))}
            for j in range(blocks):
                curl_x = ld(1, j, dz=-1) - ld(1, j, dz=1)
                curl_y = ld(0, j, dz=1) - ld(0, j, dz=-1)
                curl_z = ld(1, j, dx=1) - ld(1, j, dx=-1) - dy[0][j]
                if not flat:
                    curl_x = curl_x + dy[2][j]
                    curl_y = curl_y - (ld(2, j, dx=1) - ld(2, j, dx=-1))
                for c, value in enumerate((curl_x, curl_y, curl_z)):
                    bm[c, out, j, r : r + ROWS, :] = masked(value, inside_z, inside_x)
        return 0

    lax.fori_loop(0, planes, plane, 0, unroll=4)


def pushed(bm, x, r, rub, blocks):
    def ld(c, j, dx=0, dz=0):
        return bm[c, x + dx, j, r + dz : r + dz + ROWS, :]

    dy = [y_diff([ld(c, j) for j in range(blocks)]) if c != 1 else None for c in range(3)]
    weight = rub[r : r + ROWS]
    for j in range(blocks):
        field = [ld(c, j) for c in range(3)]
        current = (
            dy[2][j] - (ld(1, j, dz=1) - ld(1, j, dz=-1)),
            (ld(0, j, dz=1) - ld(0, j, dz=-1)) - (ld(2, j, dx=1) - ld(2, j, dx=-1)),
            (ld(1, j, dx=1) - ld(1, j, dx=-1)) - dy[0][j],
        )
        square = dot(field, field)
        scale = weight * (0.0625 / jnp.maximum(0.25 * square, 1.0))
        both = dot(current, field)
        yield j, [scale * (field[c] * both - current[c] * square) for c in range(3)]


def first_push(ap, bm, an, rub, planes, at_of, out_of, cz, blocks):
    def plane(x, _):
        halo = HALO - 2
        for r in windows(BASE - halo, BASE + cz + halo):
            for j, change in pushed(bm, at_of(x), r, rub, blocks):
                for c in range(2):
                    an[c, out_of(x), j, r : r + ROWS, :] = ap[c, x + 2, j, r : r + ROWS, :] + change[c]
                an[2, out_of(x), j, r : r + ROWS, :] = change[2]
        return 0

    lax.fori_loop(0, planes, plane, 0, unroll=2)


def last_push(an, bm, out, rub, planes, at_of, cz, blocks):
    def plane(x, _):
        for z in range(0, cz, ROWS):
            for j, change in pushed(bm, at_of(x), BASE + z, rub, blocks):
                cut = slice(j * LANES, (j + 1) * LANES)
                for c in range(3):
                    out[c, x, z : z + ROWS, cut] = an[c, x + 2, j, BASE + z : BASE + z + ROWS, :] + change[c]
        return 0

    lax.fori_loop(0, planes, plane, 0, unroll=2)


def middle_kernel(
    cells, core_b, core_f, bp, sums0, friction, face_za, face_zb, above, out, ap, bm, an, bn, inner, rub, relaxed, sent
):
    _, cx, cz, ny = core_b.shape
    blocks = ny // LANES
    rows = row_index()
    _, _, z_first, z_all = own_place(cx, cz)
    rate = rate_of(sums0, cells)
    top = BASE + cz

    rub[BASE:top] = friction[...]
    low, high = sorted_out("gz", face_za[3 * cx, :, :LANES], face_zb[3 * cx, :, :LANES])
    rub[BASE - HALO : BASE] = low
    rub[top : top + HALO] = high
    for r in range(0, cz + 2 * BASE, ROWS):
        height = rows + (r - BASE) + z_first
        inside = (height >= 0) & (height < z_all)
        rub[r : r + ROWS] = jnp.where(inside, time_step / rub[r : r + ROWS], 0.0)

    def own_plane(x, _):
        for j in range(blocks):
            cut = slice(j * LANES, (j + 1) * LANES)
            for c in range(3):
                own = [
                    core_b[c, x, z : z + ROWS, cut] + rate * core_f[c, x, z : z + ROWS, cut]
                    for z in range(0, cz, ROWS)
                ]
                for z in range(0, cz, ROWS):
                    relaxed[c, x, z : z + ROWS, cut] = own[z // ROWS]
                if c == 2:
                    continue
                low, high = z_rims(face_za, face_zb, bp, rate, cx, cz, c, x, j)
                column(ap, c, x, j, low, own, high, above[x, c : c + 1, cut], rows)
        return 0

    lax.fori_loop(0, cx, own_plane, 0, unroll=2)
    matrix = dealing(ny, True)
    relaxed[...] = dealt(relaxed[...].reshape(3 * cx * cz, ny), matrix).reshape(relaxed.shape)
    copy = pltpu.make_async_copy(relaxed, out, sent)
    copy.start()
    induced(ap, bm, cx - 2, HALO - 1, lambda x: x + 1, lambda x: x, None, True, cx, cz, blocks, rows)
    first_push(ap, bm, an, rub, cx - 4, lambda x: x + 1, lambda x: x, cz, blocks)
    induced(an, bn, cx - 6, 1, lambda x: x + 1, lambda x: x, None, False, cx, cz, blocks, rows)
    last_push(an, bn, inner, rub, cx - 8, lambda x: x + 1, cz, blocks)
    inner[...] = dealt(inner[...].reshape(-1, ny), matrix).reshape(inner.shape)
    copy.wait()


def ends_kernel(
    cells, bp, sums0, face_xa, face_xb, corner_a, corner_b, own_ap, own_bm, own_an, own_bn, inner, rub, potential, ap, bm, an, rim, sent
):
    _, cx, cz, ny = potential.shape
    blocks = ny // LANES
    rows = row_index()
    copies = [pltpu.make_async_copy(inner, potential.at[:, HALO : cx - HALO], sent.at[0])]
    copies[0].start()
    rate = rate_of(sums0, cells)

    for d in range(1, HALO + 1):
        for c in range(2):
            if (0, c, d) not in LAYERS:
                continue
            for j in range(blocks):
                cut = slice(j * LANES, (j + 1) * LANES)

                def layer(which, span):
                    k = LAYERS.index((which, c, d))
                    return sorted_out("gx", face_xa[k, span, cut], face_xb[k, span, cut])

                own = ([], [])
                for z in range(0, cz, ROWS):
                    force = layer(0, slice(z, z + ROWS))
                    if d <= 2:
                        field = [bp[c, at, j, BASE + z : BASE + z + ROWS, :] for at in (2 - d, cx + 1 + d)]
                    else:
                        field = layer(1, slice(z, z + ROWS))
                    for side in range(2):
                        own[side].append(field[side] + rate * force[side])
                corners = sorted_out("gx", corner_a[c, :, cut], corner_b[c, :, cut])
                for side, plane in enumerate((HALO - d, 2 * HALO + d - 1)):
                    corner = corners[side]
                    high, low = corner_rows(corner, HALO, d, HALO - 1)
                    column(ap, c, plane, j, low, own[side], high, corner[d - 1 : d], rows)

    def borrow(into, source, low, high):
        for k in range(2):
            for c in range(source.shape[0]):
                into[c, 4 + k] = source[c, low + k]
                into[c, 6 + k] = source[c, high + k]

    def at_of(x):
        return x + 1 + jnp.where(x >= 4, 2, 0)

    def out_of(x):
        return x + jnp.where(x >= 4, 4, 0)

    borrow(ap, own_ap, 0, cx - 2)
    induced(ap, bm, 8, HALO - 1, at_of, out_of, lambda x: x - 3 + jnp.where(x >= 4, cx - 2, 0), True, cx, cz, blocks, rows)
    borrow(bm, own_bm, 0, cx - 4)
    first_push(ap, bm, an, rub, 8, at_of, out_of, cz, blocks)
    borrow(an, own_an, 0, cx - 6)
    induced(an, bm, 8, 1, at_of, out_of, lambda x: x - 1 + jnp.where(x >= 4, cx - 6, 0), False, cx, cz, blocks, rows)
    borrow(bm, own_bn, 0, cx - 8)
    last_push(an, bm, rim, rub, 8, at_of, cz, blocks)
    rim[...] = dealt(rim[...].reshape(-1, ny), dealing(ny, True)).reshape(rim.shape)
    copies.append(pltpu.make_async_copy(rim.at[:, :HALO], potential.at[:, :HALO], sent.at[1]))
    copies.append(pltpu.make_async_copy(rim.at[:, HALO:], potential.at[:, cx - HALO :], sent.at[2]))
    for copy in copies[1:]:
        copy.start()
    for copy in copies:
        copy.wait()


def pack_kernel(cells, count, *refs):
    columns, (face_za, face_zb, bp, sums0, above, corner_a, corner_b) = refs[:count], refs[count:]
    cx, _, ny = above.shape
    cz = bp.shape[3] - 2 * BASE
    even_x = is_even("gx")
    place = lax.axis_index("gz")
    rate = rate_of(sums0, cells)

    def total(x, _):
        column = jnp.zeros(columns[0].shape[1:], jnp.float32)
        for level, part in enumerate(columns):
            column = column + jnp.where((place >> level) % 2 == 0, part[x], 0.0)
        above[x] = column[2:4] + rate * column[0:2]
        return 0

    lax.fori_loop(0, cx, total, 0, unroll=4)
    for c in range(2):
        for j in range(ny // LANES):
            cut = slice(j * LANES, (j + 1) * LANES)
            packed = []
            for edge in (lambda d: d - 1, lambda d: cx - d):
                rims = [z_rims(face_za, face_zb, bp, rate, cx, cz, c, edge(d), j) for d in range(1, HALO)]
                pieces = [above[edge(d), c : c + 1, cut] for d in range(1, HALO + 1)]
                pieces += [high[: HALO - d] for d, (_, high) in enumerate(rims, 1)]
                pieces += [low[d:] for d, (low, _) in enumerate(rims, 1)]
                packed.append(jnp.concatenate(pieces, axis=0))
            corner_a[c, :, cut] = jnp.where(even_x, packed[1], packed[0])
            corner_b[c, :, cut] = jnp.where(even_x, packed[0], packed[1])


def call(kernel, outs, *args, scratch=(), cost=0, limit=8, outside_out=0):
    shapes = [jax.ShapeDtypeStruct(shape, jnp.float32) for shape in outs]
    return pl.pallas_call(
        kernel,
        out_shape=shapes,
        in_specs=[pl.BlockSpec(memory_space=pltpu.VMEM)] * len(args),
        out_specs=[pl.BlockSpec(memory_space=pl.ANY if k < outside_out else pltpu.VMEM) for k in range(len(outs))],
        scratch_shapes=[pltpu.VMEM(item, jnp.float32) if isinstance(item, tuple) else item for item in scratch],
        compiler_params=pltpu.CompilerParams(vmem_limit_bytes=limit * 1024 * 1024),
        cost_estimate=pl.CostEstimate(flops=cost, bytes_accessed=cost // 10, transcendentals=0),
    )(*args)


def body(magnetic, friction):
    _, cx, cz, ny = magnetic.shape
    blocks = ny // LANES
    height = cz + 2 * BASE
    count_z, count_x = lax.axis_size("gz"), lax.axis_size("gx")
    devices = count_z * count_x
    cells = cx * cz * ny * devices
    work = cx * cz * ny * 200

    def planes_of(components, planes):
        return (components, planes, blocks, height, LANES)

    def padded(components, layers):
        return planes_of(components, cx + 2 * layers)

    tiles = (devices, ROWS, LANES)
    core = (3, cx, cz, ny)
    rubbed = jnp.broadcast_to(friction[:, None], (cz, LANES))

    magnetic, *faces = call(
        entry_kernel,
        [core, *[(3, NEAR, cz, ny)] * 2, *[(3, cx, HALO, ny)] * 2],
        magnetic,
        cost=work,
        limit=8,
    )
    faces_x = swapped(faces[:2], "gx")
    faces_z = swapped(faces[2:], "gz")
    corners = call(
        corners_kernel,
        [(-(-6 * corner_row(NEAR + 1) // ROWS) * ROWS, ny)] * 2,
        *faces_z,
        cost=work // 50,
    )
    corners = swapped(corners, "gx")
    own_b, inner_f, part = call(
        inner_kernel,
        [padded(3, 0), padded(3, -2), (2, ROWS, LANES)],
        magnetic,
        *faces_z,
        scratch=[padded(7, -1)],
        cost=work,
        limit=9,
    )
    outer_b, outer_f, sums, *rims = call(
        outer_kernel,
        [planes_of(3, 2 * (NEAR + HALO)), planes_of(3, 2 * NEAR), tiles, *[(3 * NEAR * cz + ROWS, ny)] * 2],
        own_b,
        part,
        *faces_x,
        *corners,
        scratch=[planes_of(7, 8)],
        cost=work,
        limit=9,
    )
    rims = swapped(rims, "gx")
    core_b, core_f, bp, sums = call(
        functools.partial(second_kernel, cells),
        [core, core, padded(3, HALO - 2), tiles],
        own_b,
        inner_f,
        outer_b,
        outer_f,
        *rims,
        shared(sums),
        scratch=[padded(7, 1)],
        cost=work,
        limit=11,
    )
    faces = call(
        faces_kernel,
        [*[(len(LAYERS), cz, ny)] * 2, (4 * cx + 1, HALO, ny), (3 * cx + 1, HALO, ny)],
        core_b,
        core_f,
        rubbed,
        cost=work,
    )
    faces_z = swapped(faces[2:], "gz")
    faces_x = swapped(faces[:2], "gx")
    sums = shared(sums)
    columns = [faces_z[0][3 * cx + 1 :]]
    group = faces[2][3 * cx + 1 :] + columns[0]
    stride = 2
    while stride < count_z:
        columns.append(lax.ppermute(group, "gz", [(i, i ^ stride) for i in range(count_z)]))
        stride *= 2
        if stride < count_z:
            group = group + columns[-1]
    above, *corners = call(
        functools.partial(pack_kernel, cells, len(columns)),
        [(cx, 2, ny), *[(2, HALO + 2 * corner_row(HALO), ny)] * 2],
        *columns,
        *faces_z,
        bp,
        sums,
        cost=work // 50,
    )
    corners = swapped(corners, "gx")
    relaxed, *shares = call(
        functools.partial(middle_kernel, cells),
        [core, padded(2, 0), padded(3, -1), padded(3, -2), padded(3, -3), (3, cx - 2 * HALO, cz, ny), (height, LANES)],
        core_b,
        core_f,
        bp,
        sums,
        rubbed,
        *faces_z,
        above,
        scratch=[core, pltpu.SemaphoreType.DMA],
        outside_out=1,
        cost=work,
        limit=8,
    )
    (potential,) = call(
        functools.partial(ends_kernel, cells),
        [core],
        bp,
        sums,
        *faces_x,
        *corners,
        *shares,
        scratch=[planes_of(2, 12), planes_of(3, 12), planes_of(3, 12), (3, 2 * HALO, cz, ny), pltpu.SemaphoreType.DMA((3,))],
        outside_out=1,
        cost=work,
        limit=14,
    )
    return relaxed, potential


def solution(mesh):
    return jax.shard_map(
        body,
        mesh=mesh,
        in_specs=(P(None, "gx", "gz", "runs"), P("gz")),
        out_specs=(P(None, "gx", "gz", "runs"), P(None, "gx", "gz", "runs")),
        check_vma=False,
    )
```

```python
import functools

import jax
import jax.numpy as jnp
from jax import lax
from jax.experimental import pallas as pl
from jax.experimental.pallas import tpu as pltpu
from jax.sharding import PartitionSpec as P

DESCENTS = 2
RELAX = 2

step_scale = 0.5
time_step = 0.2

LANES = 128
ROWS = 8
HALO = 4
NEAR = HALO // 2
BASE = 8


AXES = ("runs", "gz", "gx")


def pairings(axis):
    sizes = [lax.axis_size(name) for name in AXES]
    along = AXES.index(axis)
    places = [(r, z, x) for r in range(sizes[0]) for z in range(sizes[1]) for x in range(sizes[2])]

    def flat(place):
        return (place[0] * sizes[1] + place[1]) * sizes[2] + place[2]

    def moved(place, name, to):
        return tuple(to if name == other else at for other, at in zip(AXES, place))

    first, second = [], []
    for place in places:
        at = place[along]
        if at ^ 1 < sizes[along]:
            first.append((flat(place), flat(moved(place, axis, at ^ 1))))
        to = at + 1 if at % 2 else at - 1
        if 0 <= to < sizes[along]:
            second.append((flat(place), flat(moved(place, axis, to))))
        else:
            idle = "gz" if axis == "gx" else "runs"
            at = place[AXES.index(idle)] ^ 1
            if at < sizes[AXES.index(idle)]:
                second.append((flat(place), flat(moved(place, idle, at))))
    return first, second


def is_even(axis):
    return lax.axis_index(axis) % 2 == 0


def swapped(pair, axis):
    first, second = pairings(axis)
    return lax.ppermute(pair[0], AXES, first), lax.ppermute(pair[1], AXES, second)


def sorted_out(axis, first, second):
    at = lax.axis_index(axis)
    even = at % 2 == 0
    low = jnp.where(at > 0, jnp.where(even, second, first), 0.0)
    high = jnp.where(at < lax.axis_size(axis) - 1, jnp.where(even, first, second), 0.0)
    return low, high


def shared(tile_copies):
    return lax.all_to_all(tile_copies, ("gz", "gx"), 0, 0)


def y_diff(blocks):
    wide = [pltpu.roll(blocks[-1], 1, 1), *blocks, pltpu.roll(blocks[0], LANES - 1, 1)]
    return [wide[j + 2] - wide[j] for j in range(len(blocks))]


def dealing(ny, back):
    blocks = ny // LANES
    source = lax.broadcasted_iota(jnp.int32, (ny, ny), 0)
    target = lax.broadcasted_iota(jnp.int32, (ny, ny), 1)
    if back:
        source, target = target, source
    return ((target % LANES) * blocks + target // LANES == source).astype(jnp.bfloat16)


def dealt(value, matrix):
    rows = value.shape[0]
    high = value.astype(jnp.bfloat16)
    rest = (value - high.astype(jnp.float32)).astype(jnp.bfloat16)
    both = jnp.dot(jnp.concatenate([high, rest], axis=0), matrix, preferred_element_type=jnp.float32)
    return both[:rows] + both[rows:]


def dot(a, b):
    return a[0] * b[0] + a[1] * b[1] + a[2] * b[2]


def row_index():
    return lax.broadcasted_iota(jnp.int32, (ROWS, LANES), 0)


def windows(low, high):
    return [low + ROWS * w for w in range(-(-(high - low) // ROWS))]


def own_place(cx, cz):
    return (
        lax.axis_index("gx") * cx,
        lax.axis_size("gx") * cx,
        lax.axis_index("gz") * cz,
        lax.axis_size("gz") * cz,
    )


def row_mask(rows, r, cz):
    height = rows + (r - BASE)
    return None if BASE <= r and r + ROWS <= BASE + cz else (height >= 0) & (height < cz)


def masked(value, *conditions):
    for condition in conditions:
        if condition is not None:
            value = jnp.where(condition, value, 0.0)
    return value


def descent_stages(bp, plane_of, planes, halo, cz, blocks, parts_ref, counted, functional, rows):
    def plane(x, functional):
        at = plane_of(x)
        for r in windows(BASE - halo - 1, BASE + cz + halo + 1):
            own = row_mask(rows, r, cz)

            def ld(c, j, dx=0, dz=0):
                return bp[c, at + dx, j, r + dz : r + dz + ROWS, :]

            dy = [y_diff([ld(c, j) for j in range(blocks)]) for c in range(3)]
            for j in range(blocks):
                field = [ld(c, j) for c in range(3)]
                dx = [ld(c, j, dx=1) - ld(c, j, dx=-1) for c in range(3)]
                dz = [ld(c, j, dz=1) - ld(c, j, dz=-1) for c in range(3)]
                current = (dy[2][j] - dz[1], dz[0] - dx[2], dx[1] - dy[0][j])
                spread = dx[0] + dy[1][j] + dz[2]
                square = dot(field, field)
                inverse = 1.0 / jnp.maximum(square, 1.0)
                capped = jnp.minimum(square, 1.0)
                along = dot(current, field)
                ratio = along * inverse
                bulk = dot(current, current)
                spread_square = spread * spread
                pull = (bulk + spread_square) * inverse * (1.0 - capped) + ratio * ratio
                density = bulk * capped - ratio * along + spread_square
                functional = functional + masked(density, own, None if counted is None else counted(x))
                twist = [ratio * field[c] - capped * current[c] for c in range(3)]
                local = [ratio * current[c] - pull * field[c] for c in range(3)]
                for k, value in enumerate([*twist, capped * spread, *local]):
                    parts_ref[k, x, j, r : r + ROWS, :] = value
        return functional

    return lax.fori_loop(0, planes, plane, functional, unroll=2)


def forces(parts_ref, at, r, blocks):
    def ld(k, j, dx=0, dz=0):
        return parts_ref[k, at + dx, j, r + dz : r + dz + ROWS, :]

    dy = {k: y_diff([ld(k, j) for j in range(blocks)]) for k in (0, 2, 3)}
    for j in range(blocks):

        def dx(k):
            return ld(k, j, dx=1) - ld(k, j, dx=-1)

        def dz(k):
            return ld(k, j, dz=1) - ld(k, j, dz=-1)

        yield j, [
            (dy[2][j] - dz(1)) + (dx(3) + ld(4, j)),
            (dz(0) - dx(2)) + (dy[3][j] + ld(5, j)),
            (dx(1) - dy[0][j]) + (dz(3) + ld(6, j)),
        ]


def store_sums(sums_ref, functional, slope, rows):
    functional = jnp.sum(functional, axis=0, keepdims=True)
    slope = jnp.sum(slope, axis=0, keepdims=True)
    tile = jnp.where(rows == 0, functional, jnp.where(rows == 1, slope, 0.0))
    for k in range(sums_ref.shape[0]):
        sums_ref[k] = tile


def rate_of(sums_ref, cells):
    total = sums_ref[0]
    for k in range(1, sums_ref.shape[0]):
        total = total + sums_ref[k]
    functional = jnp.sum(total[0:1], axis=1, keepdims=True) * 0.25 / cells
    slope = jnp.sum(total[1:2], axis=1, keepdims=True) * 0.0625 / cells
    return (0.25 * step_scale) * functional / (slope + 1e-6)


def entry_kernel(magnetic, core, face_xa, face_xb):
    _, cx, cz, ny = magnetic.shape
    even_x = is_even("gx")
    matrix = dealing(ny, False)
    for c in range(3):
        value = dealt(magnetic[c].reshape(cx * cz, ny), matrix).reshape(cx, cz, ny)
        core[c] = value
        low, high = value[:NEAR], value[cx - NEAR :]
        face_xa[c] = jnp.where(even_x, high, low)
        face_xb[c] = jnp.where(even_x, low, high)


def first_forces(parts_ref, parts_of, fp, planes, cz, blocks, rows, slope):
    halo = HALO - 2
    z_first, z_all = lax.axis_index("gz") * cz, lax.axis_size("gz") * cz

    def plane(x, slope):
        for r in windows(BASE - halo, BASE + cz + halo):
            own = row_mask(rows, r, cz)
            height = rows + (r - BASE) + z_first
            inside = None if own is None else (height >= 0) & (height < z_all)
            for j, force in forces(parts_ref, parts_of(x), r, blocks):
                slope = slope + masked(dot(force, force), own)
                for c in range(3):
                    fp[c, x, j, r : r + ROWS, :] = masked(force[c], inside)
        return slope

    return lax.fori_loop(0, planes, plane, slope, unroll=4)


def z_halos(bp, c, plane, j, top, a, b):
    low, high = sorted_out("gz", a, b)
    bp[c, plane, j, BASE - HALO : BASE, :] = low
    bp[c, plane, j, top : top + HALO, :] = high


def corner_row(d):
    return sum(HALO - k for k in range(1, d))


def corner_rows(corner, first, d, reach):
    none = jnp.zeros((d, LANES), jnp.float32)
    if d == HALO:
        return none, none
    high, low = [corner[at : at + HALO - d] for at in (first + corner_row(d), first + corner_row(reach + 1) + corner_row(d))]
    return jnp.concatenate([high, none], 0), jnp.concatenate([none, low], 0)


def corners_kernel(face_za, face_zb, corner_a, corner_b):
    _, cx, _, ny = face_za.shape
    even_x = is_even("gx")
    for j in range(ny // LANES):
        cut = slice(j * LANES, (j + 1) * LANES)
        packed = []
        for edge in (lambda d: d - 1, lambda d: cx - d):
            pieces = []
            for c in range(3):
                rims = [sorted_out("gz", face_za[c, edge(d), :, cut], face_zb[c, edge(d), :, cut]) for d in range(1, NEAR + 1)]
                pieces += [high[: HALO - d] for d, (_, high) in enumerate(rims, 1)]
                pieces += [low[d:] for d, (low, _) in enumerate(rims, 1)]
            pieces.append(jnp.zeros((corner_a.shape[0] - 6 * corner_row(NEAR + 1), LANES), jnp.float32))
            packed.append(jnp.concatenate(pieces, axis=0))
        corner_a[:, cut] = jnp.where(even_x, packed[1], packed[0])
        corner_b[:, cut] = jnp.where(even_x, packed[0], packed[1])


def z_halos(bp, c, plane, j, top, a, b):
    low, high = sorted_out("gz", a, b)
    bp[c, plane, j, BASE - HALO : BASE, :] = low
    bp[c, plane, j, top : top + HALO, :] = high


def inner_kernel(core, face_za, face_zb, bp, fp, sums_ref, parts_ref, faces):
    _, cx, cz, ny = core.shape
    blocks = ny // LANES
    halo = HALO - 2

    both = jnp.concatenate([face_za[...], face_zb[...]], axis=2)
    faces[...] = dealt(both.reshape(-1, ny), dealing(ny, False)).reshape(faces.shape)

    def own(x, _):
        for c in range(3):
            for j in range(blocks):
                cut = slice(j * LANES, (j + 1) * LANES)
                for z in range(0, cz, ROWS):
                    bp[c, x, j, BASE + z : BASE + z + ROWS, :] = core[c, x, z : z + ROWS, cut]
                z_halos(bp, c, x, j, BASE + cz, faces[c, x, :HALO, cut], faces[c, x, HALO:, cut])
        return 0

    lax.fori_loop(0, cx, own, 0)
    rows = row_index()
    zero = jnp.zeros((ROWS, LANES), jnp.float32)
    sums_ref[0] = descent_stages(bp, lambda x: x + 1, cx - 2, halo, cz, blocks, parts_ref, None, zero, rows)
    sums_ref[1] = first_forces(parts_ref, lambda x: x + 1, fp, cx - 4, cz, blocks, rows, zero)


def outer_kernel(own, part, face_xa, face_xb, corner_a, corner_b, bp, fp, sums_ref, rim_a, rim_b, parts_ref, corner):
    _, cx, blocks, _, _ = own.shape
    cz = face_xa.shape[2]
    halo = HALO - 2
    rows = row_index()
    top = BASE + cz
    end = NEAR + HALO

    def copied(x, _):
        for c in range(3):
            for j in range(blocks):
                for r in range(0, top + BASE, ROWS):
                    bp[c, x + NEAR, j, r : r + ROWS, :] = own[c, x, j, r : r + ROWS, :]
                    bp[c, x + end, j, r : r + ROWS, :] = own[c, x + cx - HALO, j, r : r + ROWS, :]
        return 0

    lax.fori_loop(0, HALO, copied, 0)
    ny = corner_a.shape[1]
    corner[...] = dealt(jnp.concatenate([corner_a[...], corner_b[...]], axis=0), dealing(ny, False))
    count = corner_a.shape[0]
    for d in range(1, NEAR + 1):
        for c in range(3):
            for j in range(blocks):
                cut = slice(j * LANES, (j + 1) * LANES)
                corners = sorted_out("gx", corner[:count, cut], corner[count:, cut])
                for side, (plane, k) in enumerate(((NEAR - d, NEAR - d), (end + HALO + d - 1, d - 1))):
                    for z in range(0, cz, ROWS):
                        span = slice(z, z + ROWS)
                        value = sorted_out("gx", face_xa[c, k, span, cut], face_xb[c, k, span, cut])[side]
                        bp[c, plane, j, BASE + z : BASE + z + ROWS, :] = value
                    high, low = corner_rows(corners[side], 2 * c * corner_row(NEAR + 1), d, NEAR)
                    bp[c, plane, j, BASE - HALO : BASE, :] = low
                    bp[c, plane, j, top : top + HALO, :] = high
    functional = descent_stages(
        bp,
        lambda x: x + 1 + jnp.where(x >= 4, 2, 0),
        8,
        halo,
        cz,
        blocks,
        parts_ref,
        lambda x: (x == 1) | (x == 6),
        part[0],
        rows,
    )
    slope = first_forces(parts_ref, lambda x: x + 1 + jnp.where(x >= 2, 2, 0), fp, 4, cz, blocks, rows, part[1])
    store_sums(sums_ref, functional, slope, rows)
    even = is_even("gx")
    for c in range(3):
        for j in range(blocks):
            cut = slice(j * LANES, (j + 1) * LANES)

            def send(at, count, low, high):
                rim_a[at : at + count, cut] = jnp.where(even, high, low)
                rim_b[at : at + count, cut] = jnp.where(even, low, high)

            for d in range(1, NEAR + 1):
                for z in range(0, cz, ROWS):
                    span = slice(BASE + z, BASE + z + ROWS)
                    send((c * NEAR + d - 1) * cz + z, ROWS, fp[c, d - 1, j, span, :], fp[c, 2 * NEAR - d, j, span, :])
            for k, r in enumerate((BASE - 1, top)):
                row = slice(r, r + 1)
                send(3 * NEAR * cz + 2 * c + k, 1, fp[c, 0, j, row, :], fp[c, 2 * NEAR - 1, j, row, :])


def second_kernel(
    cells, own_b, inner_f, outer_b, outer_f, rim_a, rim_b, sums0, core_b, core_f, bp, sums_ref, parts_ref
):
    _, cx, cz, ny = core_b.shape
    blocks = ny // LANES
    rows = row_index()
    even_x, even_z = is_even("gx"), is_even("gz")
    rate = rate_of(sums0, cells)
    halo = HALO - 2

    def step(x, field, at, force, there):
        for c in range(3):
            for j in range(blocks):
                for r in range(0, cz + 2 * BASE, ROWS):
                    bp[c, x, j, r : r + ROWS, :] = (
                        field[c, at, j, r : r + ROWS, :] + rate * force[c, there, j, r : r + ROWS, :]
                    )

    def inner_step(x, _):
        step(x + 4, own_b, x + 2, inner_f, x)
        return 0

    lax.fori_loop(0, cx - 4, inner_step, 0, unroll=2)
    for k in range(NEAR):
        step(k + halo, own_b, k, outer_f, k)
        step(k + cx, own_b, k + cx - NEAR, outer_f, k + NEAR)
    top = BASE + cz
    for d in range(1, NEAR + 1):
        for c in range(3):
            for j in range(blocks):
                cut = slice(j * LANES, (j + 1) * LANES)
                for side, (x, at) in enumerate(((halo - d, NEAR - d), (halo + cx + d - 1, 2 * HALO + NEAR + d - 1))):
                    for r in (0, top):
                        bp[c, x, j, r : r + ROWS, :] = outer_b[c, at, j, r : r + ROWS, :]
                    for z in range(0, cz, ROWS):
                        r, k = BASE + z, (c * NEAR + d - 1) * cz + z
                        force = sorted_out("gx", rim_a[k : k + ROWS, cut], rim_b[k : k + ROWS, cut])[side]
                        bp[c, x, j, r : r + ROWS, :] = outer_b[c, at, j, r : r + ROWS, :] + rate * force
                    if d > 1:
                        continue
                    for n, r in enumerate((BASE - 1, top)):
                        k = 3 * NEAR * cz + 2 * c + n
                        force = sorted_out("gx", rim_a[k : k + 1, cut], rim_b[k : k + 1, cut])[side]
                        bp[c, x, j, r : r + 1, :] = outer_b[c, at, j, r : r + 1, :] + rate * force
    zero = jnp.zeros((ROWS, LANES), jnp.float32)
    functional = descent_stages(
        bp,
        lambda x: x + 1,
        cx + 2,
        0,
        cz,
        blocks,
        parts_ref,
        lambda x: (x >= 1) & (x <= cx),
        zero,
        rows,
    )

    def plane(x, slope):
        for z in range(0, cz, ROWS):
            r = BASE + z
            for j, force in forces(parts_ref, x + 1, r, blocks):
                cut = slice(j * LANES, (j + 1) * LANES)
                slope = slope + dot(force, force)
                for c in range(3):
                    core_b[c, x, z : z + ROWS, cut] = bp[c, x + halo, j, r : r + ROWS, :]
                    core_f[c, x, z : z + ROWS, cut] = force[c]
        return slope

    slope = lax.fori_loop(0, cx, plane, zero, unroll=4)
    store_sums(sums_ref, functional, slope, rows)


LAYERS = [(0, 0, d) for d in (1, 2, 3, 4)] + [(0, 1, d) for d in (1, 2, 3)] + [(1, 0, 3), (1, 0, 4), (1, 1, 3)]


def faces_kernel(core_b, core_f, friction, face_xa, face_xb, face_za, face_zb):
    _, cx, cz, ny = core_b.shape
    blocks = ny // LANES
    even_x, even_z = is_even("gx"), is_even("gz")

    def plane(x, _):
        for j in range(blocks):
            cut = slice(j * LANES, (j + 1) * LANES)
            for c in range(2):
                low, high = core_f[c, x, 0:HALO, cut], core_f[c, x, cz - HALO : cz, cut]
                face_za[c * cx + x, :, cut] = jnp.where(even_z, high, low)
                face_zb[c * cx + x, :, cut] = jnp.where(even_z, low, high)
                low, high = core_b[c, x, 2:4, cut], core_b[c, x, cz - 4 : cz - 2, cut]
                face_za[2 * cx + x, 2 * c : 2 * c + 2, cut] = jnp.where(even_z, high, low)
                face_zb[2 * cx + x, 2 * c : 2 * c + 2, cut] = jnp.where(even_z, low, high)
            for k, (source, c) in enumerate(((core_f, 0), (core_f, 1), (core_b, 0), (core_b, 1))):
                value = source[c, x, 0:ROWS, cut]
                for z in range(ROWS, cz, ROWS):
                    value = value + source[c, x, z : z + ROWS, cut]
                face_za[3 * cx + 1 + x, k : k + 1, cut] = jnp.sum(value, axis=0, keepdims=True)
        return 0

    lax.fori_loop(0, cx, plane, 0, unroll=4)
    for j in range(blocks):
        cut = slice(j * LANES, (j + 1) * LANES)
        for k, (which, c, d) in enumerate(LAYERS):
            source = (core_f, core_b)[which]
            for z in range(0, cz, ROWS):
                low, high = source[c, d - 1, z : z + ROWS, cut], source[c, cx - d, z : z + ROWS, cut]
                face_xa[k, z : z + ROWS, cut] = jnp.where(even_x, high, low)
                face_xb[k, z : z + ROWS, cut] = jnp.where(even_x, low, high)
        low, high = friction[0:HALO], friction[cz - HALO : cz]
        face_za[3 * cx, :, cut] = jnp.where(even_z, high, low)
        face_zb[3 * cx, :, cut] = jnp.where(even_z, low, high)


def z_rims(face_za, face_zb, bp, rate, cx, cz, c, x, j):
    cut = slice(j * LANES, (j + 1) * LANES)
    top = BASE + cz
    force = sorted_out("gz", face_za[c * cx + x, :, cut], face_zb[c * cx + x, :, cut])
    span = slice(2 * c, 2 * c + 2)
    far = sorted_out("gz", face_za[2 * cx + x, span, cut], face_zb[2 * cx + x, span, cut])
    low = jnp.concatenate([far[0], bp[c, x + 2, j, BASE - 2 : BASE, :]], axis=0)
    high = jnp.concatenate([bp[c, x + 2, j, top : top + 2, :], far[1]], axis=0)
    return low + rate * force[0], high + rate * force[1]


def suffix(value, rows):
    for reach in (1, 2, 4):
        value = value + jnp.where(rows < ROWS - reach, pltpu.roll(value, ROWS - reach, 0), 0.0)
    return value


def prefix(value, rows):
    for reach in (1, 2, 4):
        value = value + jnp.where(rows >= reach, pltpu.roll(value, reach, 0), 0.0)
    return value


def column(ap, c, plane, j, low, own, high, beyond, rows):
    sign = 1.0 if c == 0 else -1.0
    out = 1 - c
    top = BASE + ROWS * len(own)
    ap[out, plane, j, top : top + HALO, :] = high
    value = ap[out, plane, j, top : top + ROWS, :]
    ap[out, plane, j, top : top + ROWS, :] = sign * (beyond - (prefix(value, rows) - value))
    carry = beyond
    for k in reversed(range(len(own))):
        value = suffix(own[k], rows) + carry
        ap[out, plane, j, BASE + k * ROWS : BASE + (k + 1) * ROWS, :] = sign * value
        carry = value[0:1]
    ap[out, plane, j, BASE - HALO : BASE, :] = low
    value = suffix(ap[out, plane, j, 0:BASE, :], rows) + carry
    ap[out, plane, j, 0:BASE, :] = jnp.where(lax.axis_index("gz") > 0, sign * value, 0.0)


def induced(a_ref, bm, planes, halo, at_of, out_of, own_of, flat, cx, cz, blocks, rows):
    x_first, x_all, z_first, z_all = own_place(cx, cz)

    def plane(x, _):
        at, out = at_of(x), out_of(x)
        inside_x = None
        if own_of is not None:
            there = x_first + own_of(x)
            inside_x = (there >= 0) & (there < x_all)
        for r in windows(BASE - halo, BASE + cz + halo):
            height = rows + (r - BASE) + z_first
            inside_z = None if row_mask(rows, r, cz) is None else (height >= 0) & (height < z_all)

            def ld(c, j, dx=0, dz=0):
                return a_ref[c, at + dx, j, r + dz : r + dz + ROWS, :]

            dy = {c: y_diff([ld(c, j) for j in range(blocks)]) for c in ((0,) if flat else (0, 2))}
            for j in range(blocks):
                curl_x = ld(1, j, dz=-1) - ld(1, j, dz=1)
                curl_y = ld(0, j, dz=1) - ld(0, j, dz=-1)
                curl_z = ld(1, j, dx=1) - ld(1, j, dx=-1) - dy[0][j]
                if not flat:
                    curl_x = curl_x + dy[2][j]
                    curl_y = curl_y - (ld(2, j, dx=1) - ld(2, j, dx=-1))
                for c, value in enumerate((curl_x, curl_y, curl_z)):
                    bm[c, out, j, r : r + ROWS, :] = masked(value, inside_z, inside_x)
        return 0

    lax.fori_loop(0, planes, plane, 0, unroll=4)


def pushed(bm, x, r, rub, blocks):
    def ld(c, j, dx=0, dz=0):
        return bm[c, x + dx, j, r + dz : r + dz + ROWS, :]

    dy = [y_diff([ld(c, j) for j in range(blocks)]) if c != 1 else None for c in range(3)]
    weight = rub[r : r + ROWS]
    for j in range(blocks):
        field = [ld(c, j) for c in range(3)]
        current = (
            dy[2][j] - (ld(1, j, dz=1) - ld(1, j, dz=-1)),
            (ld(0, j, dz=1) - ld(0, j, dz=-1)) - (ld(2, j, dx=1) - ld(2, j, dx=-1)),
            (ld(1, j, dx=1) - ld(1, j, dx=-1)) - dy[0][j],
        )
        square = dot(field, field)
        scale = weight * (0.0625 / jnp.maximum(0.25 * square, 1.0))
        both = dot(current, field)
        yield j, [scale * (field[c] * both - current[c] * square) for c in range(3)]


def first_push(ap, bm, an, rub, planes, at_of, out_of, cz, blocks):
    def plane(x, _):
        halo = HALO - 2
        for r in windows(BASE - halo, BASE + cz + halo):
            for j, change in pushed(bm, at_of(x), r, rub, blocks):
                for c in range(2):
                    an[c, out_of(x), j, r : r + ROWS, :] = ap[c, x + 2, j, r : r + ROWS, :] + change[c]
                an[2, out_of(x), j, r : r + ROWS, :] = change[2]
        return 0

    lax.fori_loop(0, planes, plane, 0, unroll=2)


def last_push(an, bm, out, rub, planes, at_of, cz, blocks):
    def plane(x, _):
        for z in range(0, cz, ROWS):
            for j, change in pushed(bm, at_of(x), BASE + z, rub, blocks):
                cut = slice(j * LANES, (j + 1) * LANES)
                for c in range(3):
                    out[c, x, z : z + ROWS, cut] = an[c, x + 2, j, BASE + z : BASE + z + ROWS, :] + change[c]
        return 0

    lax.fori_loop(0, planes, plane, 0, unroll=2)


def middle_kernel(
    cells, core_b, core_f, bp, sums0, friction, face_za, face_zb, above, out, ap, bm, an, bn, inner, rub, relaxed, sent
):
    _, cx, cz, ny = core_b.shape
    blocks = ny // LANES
    rows = row_index()
    _, _, z_first, z_all = own_place(cx, cz)
    rate = rate_of(sums0, cells)
    top = BASE + cz

    rub[BASE:top] = friction[...]
    low, high = sorted_out("gz", face_za[3 * cx, :, :LANES], face_zb[3 * cx, :, :LANES])
    rub[BASE - HALO : BASE] = low
    rub[top : top + HALO] = high
    for r in range(0, cz + 2 * BASE, ROWS):
        height = rows + (r - BASE) + z_first
        inside = (height >= 0) & (height < z_all)
        rub[r : r + ROWS] = jnp.where(inside, time_step / rub[r : r + ROWS], 0.0)

    def own_plane(x, _):
        for j in range(blocks):
            cut = slice(j * LANES, (j + 1) * LANES)
            for c in range(3):
                own = [
                    core_b[c, x, z : z + ROWS, cut] + rate * core_f[c, x, z : z + ROWS, cut]
                    for z in range(0, cz, ROWS)
                ]
                for z in range(0, cz, ROWS):
                    relaxed[c, x, z : z + ROWS, cut] = own[z // ROWS]
                if c == 2:
                    continue
                low, high = z_rims(face_za, face_zb, bp, rate, cx, cz, c, x, j)
                column(ap, c, x, j, low, own, high, above[x, c : c + 1, cut], rows)
        return 0

    lax.fori_loop(0, cx, own_plane, 0, unroll=2)
    matrix = dealing(ny, True)
    relaxed[...] = dealt(relaxed[...].reshape(3 * cx * cz, ny), matrix).reshape(relaxed.shape)
    copy = pltpu.make_async_copy(relaxed, out, sent)
    copy.start()
    induced(ap, bm, cx - 2, HALO - 1, lambda x: x + 1, lambda x: x, None, True, cx, cz, blocks, rows)
    first_push(ap, bm, an, rub, cx - 4, lambda x: x + 1, lambda x: x, cz, blocks)
    induced(an, bn, cx - 6, 1, lambda x: x + 1, lambda x: x, None, False, cx, cz, blocks, rows)
    last_push(an, bn, inner, rub, cx - 8, lambda x: x + 1, cz, blocks)
    inner[...] = dealt(inner[...].reshape(-1, ny), matrix).reshape(inner.shape)
    copy.wait()


def ends_kernel(
    cells, bp, sums0, face_xa, face_xb, corner_a, corner_b, own_ap, own_bm, own_an, own_bn, inner, rub, potential, ap, bm, an, rim, sent
):
    _, cx, cz, ny = potential.shape
    blocks = ny // LANES
    rows = row_index()
    copies = [pltpu.make_async_copy(inner, potential.at[:, HALO : cx - HALO], sent.at[0])]
    copies[0].start()
    rate = rate_of(sums0, cells)

    for d in range(1, HALO + 1):
        for c in range(2):
            if (0, c, d) not in LAYERS:
                continue
            for j in range(blocks):
                cut = slice(j * LANES, (j + 1) * LANES)

                def layer(which, span):
                    k = LAYERS.index((which, c, d))
                    return sorted_out("gx", face_xa[k, span, cut], face_xb[k, span, cut])

                own = ([], [])
                for z in range(0, cz, ROWS):
                    force = layer(0, slice(z, z + ROWS))
                    if d <= 2:
                        field = [bp[c, at, j, BASE + z : BASE + z + ROWS, :] for at in (2 - d, cx + 1 + d)]
                    else:
                        field = layer(1, slice(z, z + ROWS))
                    for side in range(2):
                        own[side].append(field[side] + rate * force[side])
                corners = sorted_out("gx", corner_a[c, :, cut], corner_b[c, :, cut])
                for side, plane in enumerate((HALO - d, 2 * HALO + d - 1)):
                    corner = corners[side]
                    high, low = corner_rows(corner, HALO, d, HALO - 1)
                    column(ap, c, plane, j, low, own[side], high, corner[d - 1 : d], rows)

    def borrow(into, source, low, high):
        for k in range(2):
            for c in range(source.shape[0]):
                into[c, 4 + k] = source[c, low + k]
                into[c, 6 + k] = source[c, high + k]

    def at_of(x):
        return x + 1 + jnp.where(x >= 4, 2, 0)

    def out_of(x):
        return x + jnp.where(x >= 4, 4, 0)

    borrow(ap, own_ap, 0, cx - 2)
    induced(ap, bm, 8, HALO - 1, at_of, out_of, lambda x: x - 3 + jnp.where(x >= 4, cx - 2, 0), True, cx, cz, blocks, rows)
    borrow(bm, own_bm, 0, cx - 4)
    first_push(ap, bm, an, rub, 8, at_of, out_of, cz, blocks)
    borrow(an, own_an, 0, cx - 6)
    induced(an, bm, 8, 1, at_of, out_of, lambda x: x - 1 + jnp.where(x >= 4, cx - 6, 0), False, cx, cz, blocks, rows)
    borrow(bm, own_bn, 0, cx - 8)
    last_push(an, bm, rim, rub, 8, at_of, cz, blocks)
    rim[...] = dealt(rim[...].reshape(-1, ny), dealing(ny, True)).reshape(rim.shape)
    copies.append(pltpu.make_async_copy(rim.at[:, :HALO], potential.at[:, :HALO], sent.at[1]))
    copies.append(pltpu.make_async_copy(rim.at[:, HALO:], potential.at[:, cx - HALO :], sent.at[2]))
    for copy in copies[1:]:
        copy.start()
    for copy in copies:
        copy.wait()


def pack_kernel(cells, count, *refs):
    columns, (face_za, face_zb, bp, sums0, above, corner_a, corner_b) = refs[:count], refs[count:]
    cx, _, ny = above.shape
    cz = bp.shape[3] - 2 * BASE
    even_x = is_even("gx")
    place = lax.axis_index("gz")
    rate = rate_of(sums0, cells)

    def total(x, _):
        column = jnp.zeros(columns[0].shape[1:], jnp.float32)
        for level, part in enumerate(columns):
            column = column + jnp.where((place >> level) % 2 == 0, part[x], 0.0)
        above[x] = column[2:4] + rate * column[0:2]
        return 0

    lax.fori_loop(0, cx, total, 0, unroll=4)
    for c in range(2):
        for j in range(ny // LANES):
            cut = slice(j * LANES, (j + 1) * LANES)
            packed = []
            for edge in (lambda d: d - 1, lambda d: cx - d):
                rims = [z_rims(face_za, face_zb, bp, rate, cx, cz, c, edge(d), j) for d in range(1, HALO)]
                pieces = [above[edge(d), c : c + 1, cut] for d in range(1, HALO + 1)]
                pieces += [high[: HALO - d] for d, (_, high) in enumerate(rims, 1)]
                pieces += [low[d:] for d, (low, _) in enumerate(rims, 1)]
                packed.append(jnp.concatenate(pieces, axis=0))
            corner_a[c, :, cut] = jnp.where(even_x, packed[1], packed[0])
            corner_b[c, :, cut] = jnp.where(even_x, packed[0], packed[1])


def call(kernel, outs, *args, scratch=(), cost=0, limit=8, outside_out=0):
    shapes = [jax.ShapeDtypeStruct(shape, jnp.float32) for shape in outs]
    return pl.pallas_call(
        kernel,
        out_shape=shapes,
        in_specs=[pl.BlockSpec(memory_space=pltpu.VMEM)] * len(args),
        out_specs=[pl.BlockSpec(memory_space=pl.ANY if k < outside_out else pltpu.VMEM) for k in range(len(outs))],
        scratch_shapes=[pltpu.VMEM(item, jnp.float32) if isinstance(item, tuple) else item for item in scratch],
        compiler_params=pltpu.CompilerParams(vmem_limit_bytes=limit * 1024 * 1024),
        cost_estimate=pl.CostEstimate(flops=cost, bytes_accessed=cost // 10, transcendentals=0),
    )(*args)


def body(magnetic, friction):
    _, cx, cz, ny = magnetic.shape
    blocks = ny // LANES
    height = cz + 2 * BASE
    count_z, count_x = lax.axis_size("gz"), lax.axis_size("gx")
    devices = count_z * count_x
    cells = cx * cz * ny * devices
    work = cx * cz * ny * 200

    def planes_of(components, planes):
        return (components, planes, blocks, height, LANES)

    def padded(components, layers):
        return planes_of(components, cx + 2 * layers)

    tiles = (devices, ROWS, LANES)
    core = (3, cx, cz, ny)
    rubbed = jnp.broadcast_to(friction[:, None], (cz, LANES))

    even, far = is_even("gz"), cz - HALO
    faces_z = [
        lax.dynamic_slice_in_dim(magnetic, jnp.where(even == first, far, 0), HALO, 2) for first in (True, False)
    ]
    faces_z = swapped(faces_z, "gz")
    magnetic, *faces_x = call(
        entry_kernel,
        [core, *[(3, NEAR, cz, ny)] * 2],
        magnetic,
        cost=work,
        limit=8,
    )
    faces_x = swapped(faces_x, "gx")
    corner = (-(-6 * corner_row(NEAR + 1) // ROWS) * ROWS, ny)
    corners = call(corners_kernel, [corner] * 2, *faces_z, cost=work // 50)
    corners = swapped(corners, "gx")
    own_b, inner_f, part = call(
        inner_kernel,
        [padded(3, 0), padded(3, -2), (2, ROWS, LANES)],
        magnetic,
        *faces_z,
        scratch=[padded(7, -1), (3, cx, 2 * HALO, ny)],
        cost=work,
        limit=13,
    )
    outer_b, outer_f, sums, *rims = call(
        outer_kernel,
        [planes_of(3, 2 * (NEAR + HALO)), planes_of(3, 2 * NEAR), tiles, *[(3 * NEAR * cz + ROWS, ny)] * 2],
        own_b,
        part,
        *faces_x,
        *corners,
        scratch=[planes_of(7, 8), (2 * corner[0], ny)],
        cost=work,
        limit=9,
    )
    rims = swapped(rims, "gx")
    core_b, core_f, bp, sums = call(
        functools.partial(second_kernel, cells),
        [core, core, padded(3, HALO - 2), tiles],
        own_b,
        inner_f,
        outer_b,
        outer_f,
        *rims,
        shared(sums),
        scratch=[padded(7, 1)],
        cost=work,
        limit=11,
    )
    faces = call(
        faces_kernel,
        [*[(len(LAYERS), cz, ny)] * 2, (4 * cx + 1, HALO, ny), (3 * cx + 1, HALO, ny)],
        core_b,
        core_f,
        rubbed,
        cost=work,
    )
    faces_z = swapped(faces[2:], "gz")
    faces_x = swapped(faces[:2], "gx")
    sums = shared(sums)
    columns = [faces_z[0][3 * cx + 1 :]]
    group = faces[2][3 * cx + 1 :] + columns[0]
    stride = 2
    while stride < count_z:
        columns.append(lax.ppermute(group, "gz", [(i, i ^ stride) for i in range(count_z)]))
        stride *= 2
        if stride < count_z:
            group = group + columns[-1]
    above, *corners = call(
        functools.partial(pack_kernel, cells, len(columns)),
        [(cx, 2, ny), *[(2, HALO + 2 * corner_row(HALO), ny)] * 2],
        *columns,
        *faces_z,
        bp,
        sums,
        cost=work // 50,
    )
    corners = swapped(corners, "gx")
    relaxed, *shares = call(
        functools.partial(middle_kernel, cells),
        [core, padded(2, 0), padded(3, -1), padded(3, -2), padded(3, -3), (3, cx - 2 * HALO, cz, ny), (height, LANES)],
        core_b,
        core_f,
        bp,
        sums,
        rubbed,
        *faces_z,
        above,
        scratch=[core, pltpu.SemaphoreType.DMA],
        outside_out=1,
        cost=work,
        limit=8,
    )
    (potential,) = call(
        functools.partial(ends_kernel, cells),
        [core],
        bp,
        sums,
        *faces_x,
        *corners,
        *shares,
        scratch=[planes_of(2, 12), planes_of(3, 12), planes_of(3, 12), (3, 2 * HALO, cz, ny), pltpu.SemaphoreType.DMA((3,))],
        outside_out=1,
        cost=work,
        limit=14,
    )
    return relaxed, potential


def solution(mesh):
    return jax.shard_map(
        body,
        mesh=mesh,
        in_specs=(P(None, "gx", "gz", "runs"), P("gz")),
        out_specs=(P(None, "gx", "gz", "runs"), P(None, "gx", "gz", "runs")),
        check_vma=False,
    )
```

```python
import functools

import jax
import jax.numpy as jnp
from jax import lax
from jax.experimental import pallas as pl
from jax.experimental.pallas import tpu as pltpu
from jax.sharding import PartitionSpec as P

DESCENTS = 2
RELAX = 2

step_scale = 0.5
time_step = 0.2

LANES = 128
ROWS = 8
HALO = 4
NEAR = HALO // 2
BASE = 8


AXES = ("runs", "gz", "gx")


def pairings(axis):
    sizes = [lax.axis_size(name) for name in AXES]
    along = AXES.index(axis)
    places = [(r, z, x) for r in range(sizes[0]) for z in range(sizes[1]) for x in range(sizes[2])]

    def flat(place):
        return (place[0] * sizes[1] + place[1]) * sizes[2] + place[2]

    def moved(place, name, to):
        return tuple(to if name == other else at for other, at in zip(AXES, place))

    first, second = [], []
    for place in places:
        at = place[along]
        if at ^ 1 < sizes[along]:
            first.append((flat(place), flat(moved(place, axis, at ^ 1))))
        to = at + 1 if at % 2 else at - 1
        if 0 <= to < sizes[along]:
            second.append((flat(place), flat(moved(place, axis, to))))
        else:
            idle = "gz" if axis == "gx" else "runs"
            at = place[AXES.index(idle)] ^ 1
            if at < sizes[AXES.index(idle)]:
                second.append((flat(place), flat(moved(place, idle, at))))
    return first, second


def is_even(axis):
    return lax.axis_index(axis) % 2 == 0


def swapped(pair, axis):
    first, second = pairings(axis)
    return lax.ppermute(pair[0], AXES, first), lax.ppermute(pair[1], AXES, second)


def sorted_out(axis, first, second):
    at = lax.axis_index(axis)
    even = at % 2 == 0
    low = jnp.where(at > 0, jnp.where(even, second, first), 0.0)
    high = jnp.where(at < lax.axis_size(axis) - 1, jnp.where(even, first, second), 0.0)
    return low, high


def shared(tile_copies):
    return lax.all_to_all(tile_copies, ("gz", "gx"), 0, 0)


def y_diff(blocks):
    wide = [pltpu.roll(blocks[-1], 1, 1), *blocks, pltpu.roll(blocks[0], LANES - 1, 1)]
    return [wide[j + 2] - wide[j] for j in range(len(blocks))]


def dealing(ny, back):
    blocks = ny // LANES
    source = lax.broadcasted_iota(jnp.int32, (ny, ny), 0)
    target = lax.broadcasted_iota(jnp.int32, (ny, ny), 1)
    if back:
        source, target = target, source
    return ((target % LANES) * blocks + target // LANES == source).astype(jnp.bfloat16)


def dealt(value, matrix):
    rows = value.shape[0]
    high = value.astype(jnp.bfloat16)
    rest = (value - high.astype(jnp.float32)).astype(jnp.bfloat16)
    both = jnp.dot(jnp.concatenate([high, rest], axis=0), matrix, preferred_element_type=jnp.float32)
    return both[:rows] + both[rows:]


def dot(a, b):
    return a[0] * b[0] + a[1] * b[1] + a[2] * b[2]


def row_index():
    return lax.broadcasted_iota(jnp.int32, (ROWS, LANES), 0)


def windows(low, high):
    return [low + ROWS * w for w in range(-(-(high - low) // ROWS))]


def own_place(cx, cz):
    return (
        lax.axis_index("gx") * cx,
        lax.axis_size("gx") * cx,
        lax.axis_index("gz") * cz,
        lax.axis_size("gz") * cz,
    )


def row_mask(rows, r, cz):
    height = rows + (r - BASE)
    return None if BASE <= r and r + ROWS <= BASE + cz else (height >= 0) & (height < cz)


def masked(value, *conditions):
    for condition in conditions:
        if condition is not None:
            value = jnp.where(condition, value, 0.0)
    return value


def descent_stages(bp, plane_of, planes, halo, cz, blocks, parts_ref, counted, functional, rows):
    def plane(x, functional):
        at = plane_of(x)
        for r in windows(BASE - halo - 1, BASE + cz + halo + 1):
            own = row_mask(rows, r, cz)

            def ld(c, j, dx=0, dz=0):
                return bp[c, at + dx, j, r + dz : r + dz + ROWS, :]

            dy = [y_diff([ld(c, j) for j in range(blocks)]) for c in range(3)]
            for j in range(blocks):
                field = [ld(c, j) for c in range(3)]
                dx = [ld(c, j, dx=1) - ld(c, j, dx=-1) for c in range(3)]
                dz = [ld(c, j, dz=1) - ld(c, j, dz=-1) for c in range(3)]
                current = (dy[2][j] - dz[1], dz[0] - dx[2], dx[1] - dy[0][j])
                spread = dx[0] + dy[1][j] + dz[2]
                square = dot(field, field)
                inverse = 1.0 / jnp.maximum(square, 1.0)
                capped = jnp.minimum(square, 1.0)
                along = dot(current, field)
                ratio = along * inverse
                bulk = dot(current, current)
                spread_square = spread * spread
                pull = (bulk + spread_square) * inverse * (1.0 - capped) + ratio * ratio
                density = bulk * capped - ratio * along + spread_square
                functional = functional + masked(density, own, None if counted is None else counted(x))
                twist = [ratio * field[c] - capped * current[c] for c in range(3)]
                local = [ratio * current[c] - pull * field[c] for c in range(3)]
                for k, value in enumerate([*twist, capped * spread, *local]):
                    parts_ref[k, x, j, r : r + ROWS, :] = value
        return functional

    return lax.fori_loop(0, planes, plane, functional, unroll=4)


def forces(parts_ref, at, r, blocks):
    def ld(k, j, dx=0, dz=0):
        return parts_ref[k, at + dx, j, r + dz : r + dz + ROWS, :]

    dy = {k: y_diff([ld(k, j) for j in range(blocks)]) for k in (0, 2, 3)}
    for j in range(blocks):

        def dx(k):
            return ld(k, j, dx=1) - ld(k, j, dx=-1)

        def dz(k):
            return ld(k, j, dz=1) - ld(k, j, dz=-1)

        yield j, [
            (dy[2][j] - dz(1)) + (dx(3) + ld(4, j)),
            (dz(0) - dx(2)) + (dy[3][j] + ld(5, j)),
            (dx(1) - dy[0][j]) + (dz(3) + ld(6, j)),
        ]


def store_sums(sums_ref, functional, slope, rows):
    functional = jnp.sum(functional, axis=0, keepdims=True)
    slope = jnp.sum(slope, axis=0, keepdims=True)
    tile = jnp.where(rows == 0, functional, jnp.where(rows == 1, slope, 0.0))
    for k in range(sums_ref.shape[0]):
        sums_ref[k] = tile


def rate_of(sums_ref, cells):
    total = sums_ref[0]
    for k in range(1, sums_ref.shape[0]):
        total = total + sums_ref[k]
    functional = jnp.sum(total[0:1], axis=1, keepdims=True) * 0.25 / cells
    slope = jnp.sum(total[1:2], axis=1, keepdims=True) * 0.0625 / cells
    return (0.25 * step_scale) * functional / (slope + 1e-6)


def entry_kernel(magnetic, core, face_xa, face_xb):
    _, cx, cz, ny = magnetic.shape
    even_x = is_even("gx")
    matrix = dealing(ny, False)
    for c in range(3):
        value = dealt(magnetic[c].reshape(cx * cz, ny), matrix).reshape(cx, cz, ny)
        core[c] = value
        low, high = value[:NEAR], value[cx - NEAR :]
        face_xa[c] = jnp.where(even_x, high, low)
        face_xb[c] = jnp.where(even_x, low, high)


def first_forces(parts_ref, parts_of, fp, planes, cz, blocks, rows, slope):
    halo = HALO - 2
    z_first, z_all = lax.axis_index("gz") * cz, lax.axis_size("gz") * cz

    def plane(x, slope):
        for r in windows(BASE - halo, BASE + cz + halo):
            own = row_mask(rows, r, cz)
            height = rows + (r - BASE) + z_first
            inside = None if own is None else (height >= 0) & (height < z_all)
            for j, force in forces(parts_ref, parts_of(x), r, blocks):
                slope = slope + masked(dot(force, force), own)
                for c in range(3):
                    fp[c, x, j, r : r + ROWS, :] = masked(force[c], inside)
        return slope

    return lax.fori_loop(0, planes, plane, slope, unroll=4)


def z_halos(bp, c, plane, j, top, a, b):
    low, high = sorted_out("gz", a, b)
    bp[c, plane, j, BASE - HALO : BASE, :] = low
    bp[c, plane, j, top : top + HALO, :] = high


def corner_row(d):
    return sum(HALO - k for k in range(1, d))


def corner_rows(corner, first, d, reach):
    none = jnp.zeros((d, LANES), jnp.float32)
    if d == HALO:
        return none, none
    high, low = [corner[at : at + HALO - d] for at in (first + corner_row(d), first + corner_row(reach + 1) + corner_row(d))]
    return jnp.concatenate([high, none], 0), jnp.concatenate([none, low], 0)


def corners_kernel(face_za, face_zb, corner_a, corner_b):
    _, cx, _, ny = face_za.shape
    even_x = is_even("gx")
    for j in range(ny // LANES):
        cut = slice(j * LANES, (j + 1) * LANES)
        packed = []
        for edge in (lambda d: d - 1, lambda d: cx - d):
            pieces = []
            for c in range(3):
                rims = [sorted_out("gz", face_za[c, edge(d), :, cut], face_zb[c, edge(d), :, cut]) for d in range(1, NEAR + 1)]
                pieces += [high[: HALO - d] for d, (_, high) in enumerate(rims, 1)]
                pieces += [low[d:] for d, (low, _) in enumerate(rims, 1)]
            pieces.append(jnp.zeros((corner_a.shape[0] - 6 * corner_row(NEAR + 1), LANES), jnp.float32))
            packed.append(jnp.concatenate(pieces, axis=0))
        corner_a[:, cut] = jnp.where(even_x, packed[1], packed[0])
        corner_b[:, cut] = jnp.where(even_x, packed[0], packed[1])


def z_halos(bp, c, plane, j, top, a, b):
    low, high = sorted_out("gz", a, b)
    bp[c, plane, j, BASE - HALO : BASE, :] = low
    bp[c, plane, j, top : top + HALO, :] = high


def inner_kernel(core, face_za, face_zb, bp, fp, sums_ref, parts_ref, faces):
    _, cx, cz, ny = core.shape
    blocks = ny // LANES
    halo = HALO - 2

    both = jnp.concatenate([face_za[...], face_zb[...]], axis=2)
    faces[...] = dealt(both.reshape(-1, ny), dealing(ny, False)).reshape(faces.shape)

    def own(x, _):
        for c in range(3):
            for j in range(blocks):
                cut = slice(j * LANES, (j + 1) * LANES)
                for z in range(0, cz, ROWS):
                    bp[c, x, j, BASE + z : BASE + z + ROWS, :] = core[c, x, z : z + ROWS, cut]
                z_halos(bp, c, x, j, BASE + cz, faces[c, x, :HALO, cut], faces[c, x, HALO:, cut])
        return 0

    lax.fori_loop(0, cx, own, 0)
    rows = row_index()
    zero = jnp.zeros((ROWS, LANES), jnp.float32)
    sums_ref[0] = descent_stages(bp, lambda x: x + 1, cx - 2, halo, cz, blocks, parts_ref, None, zero, rows)
    sums_ref[1] = first_forces(parts_ref, lambda x: x + 1, fp, cx - 4, cz, blocks, rows, zero)


def outer_kernel(own, part, face_xa, face_xb, corner_a, corner_b, bp, fp, sums_ref, rim_a, rim_b, parts_ref, corner):
    _, cx, blocks, _, _ = own.shape
    cz = face_xa.shape[2]
    halo = HALO - 2
    rows = row_index()
    top = BASE + cz
    end = NEAR + HALO

    def copied(x, _):
        for c in range(3):
            for j in range(blocks):
                for r in range(0, top + BASE, ROWS):
                    bp[c, x + NEAR, j, r : r + ROWS, :] = own[c, x, j, r : r + ROWS, :]
                    bp[c, x + end, j, r : r + ROWS, :] = own[c, x + cx - HALO, j, r : r + ROWS, :]
        return 0

    lax.fori_loop(0, HALO, copied, 0)
    ny = corner_a.shape[1]
    corner[...] = dealt(jnp.concatenate([corner_a[...], corner_b[...]], axis=0), dealing(ny, False))
    count = corner_a.shape[0]
    for d in range(1, NEAR + 1):
        for c in range(3):
            for j in range(blocks):
                cut = slice(j * LANES, (j + 1) * LANES)
                corners = sorted_out("gx", corner[:count, cut], corner[count:, cut])
                for side, (plane, k) in enumerate(((NEAR - d, NEAR - d), (end + HALO + d - 1, d - 1))):
                    for z in range(0, cz, ROWS):
                        span = slice(z, z + ROWS)
                        value = sorted_out("gx", face_xa[c, k, span, cut], face_xb[c, k, span, cut])[side]
                        bp[c, plane, j, BASE + z : BASE + z + ROWS, :] = value
                    high, low = corner_rows(corners[side], 2 * c * corner_row(NEAR + 1), d, NEAR)
                    bp[c, plane, j, BASE - HALO : BASE, :] = low
                    bp[c, plane, j, top : top + HALO, :] = high
    functional = descent_stages(
        bp,
        lambda x: x + 1 + jnp.where(x >= 4, 2, 0),
        8,
        halo,
        cz,
        blocks,
        parts_ref,
        lambda x: (x == 1) | (x == 6),
        part[0],
        rows,
    )
    slope = first_forces(parts_ref, lambda x: x + 1 + jnp.where(x >= 2, 2, 0), fp, 4, cz, blocks, rows, part[1])
    store_sums(sums_ref, functional, slope, rows)
    even = is_even("gx")
    for c in range(3):
        for j in range(blocks):
            cut = slice(j * LANES, (j + 1) * LANES)

            def send(at, count, low, high):
                rim_a[at : at + count, cut] = jnp.where(even, high, low)
                rim_b[at : at + count, cut] = jnp.where(even, low, high)

            for d in range(1, NEAR + 1):
                for z in range(0, cz, ROWS):
                    span = slice(BASE + z, BASE + z + ROWS)
                    send((c * NEAR + d - 1) * cz + z, ROWS, fp[c, d - 1, j, span, :], fp[c, 2 * NEAR - d, j, span, :])
            for k, r in enumerate((BASE - 1, top)):
                row = slice(r, r + 1)
                send(3 * NEAR * cz + 2 * c + k, 1, fp[c, 0, j, row, :], fp[c, 2 * NEAR - 1, j, row, :])


def second_kernel(
    cells, own_b, inner_f, outer_b, outer_f, rim_a, rim_b, sums0, core_b, core_f, bp, sums_ref, parts_ref
):
    _, cx, cz, ny = core_b.shape
    blocks = ny // LANES
    rows = row_index()
    even_x, even_z = is_even("gx"), is_even("gz")
    rate = rate_of(sums0, cells)
    halo = HALO - 2

    def step(x, field, at, force, there):
        for c in range(3):
            for j in range(blocks):
                for r in range(0, cz + 2 * BASE, ROWS):
                    bp[c, x, j, r : r + ROWS, :] = (
                        field[c, at, j, r : r + ROWS, :] + rate * force[c, there, j, r : r + ROWS, :]
                    )

    def inner_step(x, _):
        step(x + 4, own_b, x + 2, inner_f, x)
        return 0

    lax.fori_loop(0, cx - 4, inner_step, 0, unroll=6)
    for k in range(NEAR):
        step(k + halo, own_b, k, outer_f, k)
        step(k + cx, own_b, k + cx - NEAR, outer_f, k + NEAR)
    top = BASE + cz
    for d in range(1, NEAR + 1):
        for c in range(3):
            for j in range(blocks):
                cut = slice(j * LANES, (j + 1) * LANES)
                for side, (x, at) in enumerate(((halo - d, NEAR - d), (halo + cx + d - 1, 2 * HALO + NEAR + d - 1))):
                    for r in (0, top):
                        bp[c, x, j, r : r + ROWS, :] = outer_b[c, at, j, r : r + ROWS, :]
                    for z in range(0, cz, ROWS):
                        r, k = BASE + z, (c * NEAR + d - 1) * cz + z
                        force = sorted_out("gx", rim_a[k : k + ROWS, cut], rim_b[k : k + ROWS, cut])[side]
                        bp[c, x, j, r : r + ROWS, :] = outer_b[c, at, j, r : r + ROWS, :] + rate * force
                    if d > 1:
                        continue
                    for n, r in enumerate((BASE - 1, top)):
                        k = 3 * NEAR * cz + 2 * c + n
                        force = sorted_out("gx", rim_a[k : k + 1, cut], rim_b[k : k + 1, cut])[side]
                        bp[c, x, j, r : r + 1, :] = outer_b[c, at, j, r : r + 1, :] + rate * force
    zero = jnp.zeros((ROWS, LANES), jnp.float32)
    functional = descent_stages(
        bp,
        lambda x: x + 1,
        cx + 2,
        0,
        cz,
        blocks,
        parts_ref,
        lambda x: (x >= 1) & (x <= cx),
        zero,
        rows,
    )

    def plane(x, slope):
        for z in range(0, cz, ROWS):
            r = BASE + z
            for j, force in forces(parts_ref, x + 1, r, blocks):
                cut = slice(j * LANES, (j + 1) * LANES)
                slope = slope + dot(force, force)
                for c in range(3):
                    core_b[c, x, z : z + ROWS, cut] = bp[c, x + halo, j, r : r + ROWS, :]
                    core_f[c, x, z : z + ROWS, cut] = force[c]
        return slope

    slope = lax.fori_loop(0, cx, plane, zero, unroll=4)
    store_sums(sums_ref, functional, slope, rows)


LAYERS = [(0, 0, d) for d in (1, 2, 3, 4)] + [(0, 1, d) for d in (1, 2, 3)] + [(1, 0, 3), (1, 0, 4), (1, 1, 3)]


def faces_kernel(core_b, core_f, friction, face_xa, face_xb, face_za, face_zb):
    _, cx, cz, ny = core_b.shape
    blocks = ny // LANES
    even_x, even_z = is_even("gx"), is_even("gz")

    def plane(x, _):
        for j in range(blocks):
            cut = slice(j * LANES, (j + 1) * LANES)
            for c in range(2):
                low, high = core_f[c, x, 0:HALO, cut], core_f[c, x, cz - HALO : cz, cut]
                face_za[c * cx + x, :, cut] = jnp.where(even_z, high, low)
                face_zb[c * cx + x, :, cut] = jnp.where(even_z, low, high)
                low, high = core_b[c, x, 2:4, cut], core_b[c, x, cz - 4 : cz - 2, cut]
                face_za[2 * cx + x, 2 * c : 2 * c + 2, cut] = jnp.where(even_z, high, low)
                face_zb[2 * cx + x, 2 * c : 2 * c + 2, cut] = jnp.where(even_z, low, high)
            for k, (source, c) in enumerate(((core_f, 0), (core_f, 1), (core_b, 0), (core_b, 1))):
                value = source[c, x, 0:ROWS, cut]
                for z in range(ROWS, cz, ROWS):
                    value = value + source[c, x, z : z + ROWS, cut]
                face_za[3 * cx + 1 + x, k : k + 1, cut] = jnp.sum(value, axis=0, keepdims=True)
        return 0

    lax.fori_loop(0, cx, plane, 0, unroll=4)
    for j in range(blocks):
        cut = slice(j * LANES, (j + 1) * LANES)
        for k, (which, c, d) in enumerate(LAYERS):
            source = (core_f, core_b)[which]
            for z in range(0, cz, ROWS):
                low, high = source[c, d - 1, z : z + ROWS, cut], source[c, cx - d, z : z + ROWS, cut]
                face_xa[k, z : z + ROWS, cut] = jnp.where(even_x, high, low)
                face_xb[k, z : z + ROWS, cut] = jnp.where(even_x, low, high)
        low, high = friction[0:HALO], friction[cz - HALO : cz]
        face_za[3 * cx, :, cut] = jnp.where(even_z, high, low)
        face_zb[3 * cx, :, cut] = jnp.where(even_z, low, high)


def z_rims(face_za, face_zb, bp, rate, cx, cz, c, x, j):
    cut = slice(j * LANES, (j + 1) * LANES)
    top = BASE + cz
    force = sorted_out("gz", face_za[c * cx + x, :, cut], face_zb[c * cx + x, :, cut])
    span = slice(2 * c, 2 * c + 2)
    far = sorted_out("gz", face_za[2 * cx + x, span, cut], face_zb[2 * cx + x, span, cut])
    low = jnp.concatenate([far[0], bp[c, x + 2, j, BASE - 2 : BASE, :]], axis=0)
    high = jnp.concatenate([bp[c, x + 2, j, top : top + 2, :], far[1]], axis=0)
    return low + rate * force[0], high + rate * force[1]


def suffix(value, rows):
    for reach in (1, 2, 4):
        value = value + jnp.where(rows < ROWS - reach, pltpu.roll(value, ROWS - reach, 0), 0.0)
    return value


def prefix(value, rows):
    for reach in (1, 2, 4):
        value = value + jnp.where(rows >= reach, pltpu.roll(value, reach, 0), 0.0)
    return value


def column(ap, c, plane, j, low, own, high, beyond, rows):
    sign = 1.0 if c == 0 else -1.0
    out = 1 - c
    top = BASE + ROWS * len(own)
    ap[out, plane, j, top : top + HALO, :] = high
    value = ap[out, plane, j, top : top + ROWS, :]
    ap[out, plane, j, top : top + ROWS, :] = sign * (beyond - (prefix(value, rows) - value))
    carry = beyond
    for k in reversed(range(len(own))):
        value = suffix(own[k], rows) + carry
        ap[out, plane, j, BASE + k * ROWS : BASE + (k + 1) * ROWS, :] = sign * value
        carry = value[0:1]
    ap[out, plane, j, BASE - HALO : BASE, :] = low
    value = suffix(ap[out, plane, j, 0:BASE, :], rows) + carry
    ap[out, plane, j, 0:BASE, :] = jnp.where(lax.axis_index("gz") > 0, sign * value, 0.0)


def induced(a_ref, bm, planes, halo, at_of, out_of, own_of, flat, cx, cz, blocks, rows):
    x_first, x_all, z_first, z_all = own_place(cx, cz)

    def plane(x, _):
        at, out = at_of(x), out_of(x)
        inside_x = None
        if own_of is not None:
            there = x_first + own_of(x)
            inside_x = (there >= 0) & (there < x_all)
        for r in windows(BASE - halo, BASE + cz + halo):
            height = rows + (r - BASE) + z_first
            inside_z = None if row_mask(rows, r, cz) is None else (height >= 0) & (height < z_all)

            def ld(c, j, dx=0, dz=0):
                return a_ref[c, at + dx, j, r + dz : r + dz + ROWS, :]

            dy = {c: y_diff([ld(c, j) for j in range(blocks)]) for c in ((0,) if flat else (0, 2))}
            for j in range(blocks):
                curl_x = ld(1, j, dz=-1) - ld(1, j, dz=1)
                curl_y = ld(0, j, dz=1) - ld(0, j, dz=-1)
                curl_z = ld(1, j, dx=1) - ld(1, j, dx=-1) - dy[0][j]
                if not flat:
                    curl_x = curl_x + dy[2][j]
                    curl_y = curl_y - (ld(2, j, dx=1) - ld(2, j, dx=-1))
                for c, value in enumerate((curl_x, curl_y, curl_z)):
                    bm[c, out, j, r : r + ROWS, :] = masked(value, inside_z, inside_x)
        return 0

    lax.fori_loop(0, planes, plane, 0, unroll=4)


def pushed(bm, x, r, rub, blocks):
    def ld(c, j, dx=0, dz=0):
        return bm[c, x + dx, j, r + dz : r + dz + ROWS, :]

    dy = [y_diff([ld(c, j) for j in range(blocks)]) if c != 1 else None for c in range(3)]
    weight = rub[r : r + ROWS]
    for j in range(blocks):
        field = [ld(c, j) for c in range(3)]
        current = (
            dy[2][j] - (ld(1, j, dz=1) - ld(1, j, dz=-1)),
            (ld(0, j, dz=1) - ld(0, j, dz=-1)) - (ld(2, j, dx=1) - ld(2, j, dx=-1)),
            (ld(1, j, dx=1) - ld(1, j, dx=-1)) - dy[0][j],
        )
        square = dot(field, field)
        scale = weight * (0.0625 / jnp.maximum(0.25 * square, 1.0))
        both = dot(current, field)
        yield j, [scale * (field[c] * both - current[c] * square) for c in range(3)]


def first_push(ap, bm, an, rub, planes, at_of, out_of, cz, blocks):
    def plane(x, _):
        halo = HALO - 2
        for r in windows(BASE - halo, BASE + cz + halo):
            for j, change in pushed(bm, at_of(x), r, rub, blocks):
                for c in range(2):
                    an[c, out_of(x), j, r : r + ROWS, :] = ap[c, x + 2, j, r : r + ROWS, :] + change[c]
                an[2, out_of(x), j, r : r + ROWS, :] = change[2]
        return 0

    lax.fori_loop(0, planes, plane, 0, unroll=4)


def last_push(an, bm, out, rub, planes, at_of, cz, blocks):
    def plane(x, _):
        for z in range(0, cz, ROWS):
            for j, change in pushed(bm, at_of(x), BASE + z, rub, blocks):
                cut = slice(j * LANES, (j + 1) * LANES)
                for c in range(3):
                    out[c, x, z : z + ROWS, cut] = an[c, x + 2, j, BASE + z : BASE + z + ROWS, :] + change[c]
        return 0

    lax.fori_loop(0, planes, plane, 0, unroll=2)


def middle_kernel(
    cells, core_b, core_f, bp, sums0, friction, face_za, face_zb, above, out, ap, bm, an, bn, inner, rub, relaxed, sent
):
    _, cx, cz, ny = core_b.shape
    blocks = ny // LANES
    rows = row_index()
    _, _, z_first, z_all = own_place(cx, cz)
    rate = rate_of(sums0, cells)
    top = BASE + cz

    rub[BASE:top] = friction[...]
    low, high = sorted_out("gz", face_za[3 * cx, :, :LANES], face_zb[3 * cx, :, :LANES])
    rub[BASE - HALO : BASE] = low
    rub[top : top + HALO] = high
    for r in range(0, cz + 2 * BASE, ROWS):
        height = rows + (r - BASE) + z_first
        inside = (height >= 0) & (height < z_all)
        rub[r : r + ROWS] = jnp.where(inside, time_step / rub[r : r + ROWS], 0.0)

    def own_plane(x, _):
        for j in range(blocks):
            cut = slice(j * LANES, (j + 1) * LANES)
            for c in range(3):
                own = [
                    core_b[c, x, z : z + ROWS, cut] + rate * core_f[c, x, z : z + ROWS, cut]
                    for z in range(0, cz, ROWS)
                ]
                for z in range(0, cz, ROWS):
                    relaxed[c, x, z : z + ROWS, cut] = own[z // ROWS]
                if c == 2:
                    continue
                low, high = z_rims(face_za, face_zb, bp, rate, cx, cz, c, x, j)
                column(ap, c, x, j, low, own, high, above[x, c : c + 1, cut], rows)
        return 0

    lax.fori_loop(0, cx, own_plane, 0, unroll=4)
    matrix = dealing(ny, True)
    relaxed[...] = dealt(relaxed[...].reshape(3 * cx * cz, ny), matrix).reshape(relaxed.shape)
    copy = pltpu.make_async_copy(relaxed, out, sent)
    copy.start()
    induced(ap, bm, cx - 2, HALO - 1, lambda x: x + 1, lambda x: x, None, True, cx, cz, blocks, rows)
    first_push(ap, bm, an, rub, cx - 4, lambda x: x + 1, lambda x: x, cz, blocks)
    induced(an, bn, cx - 6, 1, lambda x: x + 1, lambda x: x, None, False, cx, cz, blocks, rows)
    last_push(an, bn, inner, rub, cx - 8, lambda x: x + 1, cz, blocks)
    inner[...] = dealt(inner[...].reshape(-1, ny), matrix).reshape(inner.shape)
    copy.wait()


def ends_kernel(
    cells, bp, sums0, face_xa, face_xb, corner_a, corner_b, own_ap, own_bm, own_an, own_bn, inner, rub, potential, ap, bm, an, rim, sent
):
    _, cx, cz, ny = potential.shape
    blocks = ny // LANES
    rows = row_index()
    copies = [pltpu.make_async_copy(inner, potential.at[:, HALO : cx - HALO], sent.at[0])]
    copies[0].start()
    rate = rate_of(sums0, cells)

    for d in range(1, HALO + 1):
        for c in range(2):
            if (0, c, d) not in LAYERS:
                continue
            for j in range(blocks):
                cut = slice(j * LANES, (j + 1) * LANES)

                def layer(which, span):
                    k = LAYERS.index((which, c, d))
                    return sorted_out("gx", face_xa[k, span, cut], face_xb[k, span, cut])

                own = ([], [])
                for z in range(0, cz, ROWS):
                    force = layer(0, slice(z, z + ROWS))
                    if d <= 2:
                        field = [bp[c, at, j, BASE + z : BASE + z + ROWS, :] for at in (2 - d, cx + 1 + d)]
                    else:
                        field = layer(1, slice(z, z + ROWS))
                    for side in range(2):
                        own[side].append(field[side] + rate * force[side])
                corners = sorted_out("gx", corner_a[c, :, cut], corner_b[c, :, cut])
                for side, plane in enumerate((HALO - d, 2 * HALO + d - 1)):
                    corner = corners[side]
                    high, low = corner_rows(corner, HALO, d, HALO - 1)
                    column(ap, c, plane, j, low, own[side], high, corner[d - 1 : d], rows)

    def borrow(into, source, low, high):
        for k in range(2):
            for c in range(source.shape[0]):
                into[c, 4 + k] = source[c, low + k]
                into[c, 6 + k] = source[c, high + k]

    def at_of(x):
        return x + 1 + jnp.where(x >= 4, 2, 0)

    def out_of(x):
        return x + jnp.where(x >= 4, 4, 0)

    borrow(ap, own_ap, 0, cx - 2)
    induced(ap, bm, 8, HALO - 1, at_of, out_of, lambda x: x - 3 + jnp.where(x >= 4, cx - 2, 0), True, cx, cz, blocks, rows)
    borrow(bm, own_bm, 0, cx - 4)
    first_push(ap, bm, an, rub, 8, at_of, out_of, cz, blocks)
    borrow(an, own_an, 0, cx - 6)
    induced(an, bm, 8, 1, at_of, out_of, lambda x: x - 1 + jnp.where(x >= 4, cx - 6, 0), False, cx, cz, blocks, rows)
    borrow(bm, own_bn, 0, cx - 8)
    last_push(an, bm, rim, rub, 8, at_of, cz, blocks)
    rim[...] = dealt(rim[...].reshape(-1, ny), dealing(ny, True)).reshape(rim.shape)
    copies.append(pltpu.make_async_copy(rim.at[:, :HALO], potential.at[:, :HALO], sent.at[1]))
    copies.append(pltpu.make_async_copy(rim.at[:, HALO:], potential.at[:, cx - HALO :], sent.at[2]))
    for copy in copies[1:]:
        copy.start()
    for copy in copies:
        copy.wait()


def pack_kernel(cells, count, *refs):
    columns, (face_za, face_zb, bp, sums0, above, corner_a, corner_b) = refs[:count], refs[count:]
    cx, _, ny = above.shape
    cz = bp.shape[3] - 2 * BASE
    even_x = is_even("gx")
    place = lax.axis_index("gz")
    rate = rate_of(sums0, cells)

    def total(x, _):
        column = jnp.zeros(columns[0].shape[1:], jnp.float32)
        for level, part in enumerate(columns):
            column = column + jnp.where((place >> level) % 2 == 0, part[x], 0.0)
        above[x] = column[2:4] + rate * column[0:2]
        return 0

    lax.fori_loop(0, cx, total, 0, unroll=4)
    for c in range(2):
        for j in range(ny // LANES):
            cut = slice(j * LANES, (j + 1) * LANES)
            packed = []
            for edge in (lambda d: d - 1, lambda d: cx - d):
                rims = [z_rims(face_za, face_zb, bp, rate, cx, cz, c, edge(d), j) for d in range(1, HALO)]
                pieces = [above[edge(d), c : c + 1, cut] for d in range(1, HALO + 1)]
                pieces += [high[: HALO - d] for d, (_, high) in enumerate(rims, 1)]
                pieces += [low[d:] for d, (low, _) in enumerate(rims, 1)]
                packed.append(jnp.concatenate(pieces, axis=0))
            corner_a[c, :, cut] = jnp.where(even_x, packed[1], packed[0])
            corner_b[c, :, cut] = jnp.where(even_x, packed[0], packed[1])


def call(kernel, outs, *args, scratch=(), cost=0, limit=8, outside_out=0):
    shapes = [jax.ShapeDtypeStruct(shape, jnp.float32) for shape in outs]
    return pl.pallas_call(
        kernel,
        out_shape=shapes,
        in_specs=[pl.BlockSpec(memory_space=pltpu.VMEM)] * len(args),
        out_specs=[pl.BlockSpec(memory_space=pl.ANY if k < outside_out else pltpu.VMEM) for k in range(len(outs))],
        scratch_shapes=[pltpu.VMEM(item, jnp.float32) if isinstance(item, tuple) else item for item in scratch],
        compiler_params=pltpu.CompilerParams(vmem_limit_bytes=limit * 1024 * 1024),
        cost_estimate=pl.CostEstimate(flops=cost, bytes_accessed=cost // 10, transcendentals=0),
    )(*args)


def body(magnetic, friction):
    _, cx, cz, ny = magnetic.shape
    blocks = ny // LANES
    height = cz + 2 * BASE
    count_z, count_x = lax.axis_size("gz"), lax.axis_size("gx")
    devices = count_z * count_x
    cells = cx * cz * ny * devices
    work = cx * cz * ny * 200

    def planes_of(components, planes):
        return (components, planes, blocks, height, LANES)

    def padded(components, layers):
        return planes_of(components, cx + 2 * layers)

    tiles = (devices, ROWS, LANES)
    core = (3, cx, cz, ny)
    rubbed = jnp.broadcast_to(friction[:, None], (cz, LANES))

    even, far = is_even("gz"), cz - HALO
    faces_z = [
        lax.dynamic_slice_in_dim(magnetic, jnp.where(even == first, far, 0), HALO, 2) for first in (True, False)
    ]
    faces_z = swapped(faces_z, "gz")
    magnetic, *faces_x = call(
        entry_kernel,
        [core, *[(3, NEAR, cz, ny)] * 2],
        magnetic,
        cost=work,
        limit=8,
    )
    faces_x = swapped(faces_x, "gx")
    corner = (-(-6 * corner_row(NEAR + 1) // ROWS) * ROWS, ny)
    corners = call(corners_kernel, [corner] * 2, *faces_z, cost=work // 50)
    corners = swapped(corners, "gx")
    own_b, inner_f, part = call(
        inner_kernel,
        [padded(3, 0), padded(3, -2), (2, ROWS, LANES)],
        magnetic,
        *faces_z,
        scratch=[padded(7, -1), (3, cx, 2 * HALO, ny)],
        cost=work,
        limit=13,
    )
    outer_b, outer_f, sums, *rims = call(
        outer_kernel,
        [planes_of(3, 2 * (NEAR + HALO)), planes_of(3, 2 * NEAR), tiles, *[(3 * NEAR * cz + ROWS, ny)] * 2],
        own_b,
        part,
        *faces_x,
        *corners,
        scratch=[planes_of(7, 8), (2 * corner[0], ny)],
        cost=work,
        limit=9,
    )
    rims = swapped(rims, "gx")
    core_b, core_f, bp, sums = call(
        functools.partial(second_kernel, cells),
        [core, core, padded(3, HALO - 2), tiles],
        own_b,
        inner_f,
        outer_b,
        outer_f,
        *rims,
        shared(sums),
        scratch=[padded(7, 1)],
        cost=work,
        limit=11,
    )
    faces = call(
        faces_kernel,
        [*[(len(LAYERS), cz, ny)] * 2, (4 * cx + 1, HALO, ny), (3 * cx + 1, HALO, ny)],
        core_b,
        core_f,
        rubbed,
        cost=work,
    )
    faces_z = swapped(faces[2:], "gz")
    faces_x = swapped(faces[:2], "gx")
    sums = shared(sums)
    columns = [faces_z[0][3 * cx + 1 :]]
    group = faces[2][3 * cx + 1 :] + columns[0]
    stride = 2
    while stride < count_z:
        columns.append(lax.ppermute(group, "gz", [(i, i ^ stride) for i in range(count_z)]))
        stride *= 2
        if stride < count_z:
            group = group + columns[-1]
    above, *corners = call(
        functools.partial(pack_kernel, cells, len(columns)),
        [(cx, 2, ny), *[(2, HALO + 2 * corner_row(HALO), ny)] * 2],
        *columns,
        *faces_z,
        bp,
        sums,
        cost=work // 50,
    )
    corners = swapped(corners, "gx")
    relaxed, *shares = call(
        functools.partial(middle_kernel, cells),
        [core, padded(2, 0), padded(3, -1), padded(3, -2), padded(3, -3), (3, cx - 2 * HALO, cz, ny), (height, LANES)],
        core_b,
        core_f,
        bp,
        sums,
        rubbed,
        *faces_z,
        above,
        scratch=[core, pltpu.SemaphoreType.DMA],
        outside_out=1,
        cost=work,
        limit=8,
    )
    (potential,) = call(
        functools.partial(ends_kernel, cells),
        [core],
        bp,
        sums,
        *faces_x,
        *corners,
        *shares,
        scratch=[planes_of(2, 12), planes_of(3, 12), planes_of(3, 12), (3, 2 * HALO, cz, ny), pltpu.SemaphoreType.DMA((3,))],
        outside_out=1,
        cost=work,
        limit=14,
    )
    return relaxed, potential


def solution(mesh):
    return jax.shard_map(
        body,
        mesh=mesh,
        in_specs=(P(None, "gx", "gz", "runs"), P("gz")),
        out_specs=(P(None, "gx", "gz", "runs"), P(None, "gx", "gz", "runs")),
        check_vma=False,
    )
```
